512 devices in a mesh: src: 32 (over z, x), rcv: 16 (over y, core).
Axes of the slice: x: 4, y: 8, z: 8, core: 2. Of those that a mesh axis runs over, the one named last changes fastest.
Arguments:
- stiffness: bfloat16 [2, 131072, 2048], P(None, 'src', 'rcv'), may hold values from -0.046875 to 0.046875
- newton_rhs: float32 [48, 2, 131072], P(None, None, ('src', 'rcv')), may hold values from -6 to 6
- traction: float32 [48, 2, 2048], P(None, None, 'rcv'), may hold values from -8 to 8
- opening: float32 [48, 2048], P(None, 'rcv'), may hold values from -6 to 6
- state: int32 [48, 2048], P(None, 'rcv'), may hold values from 0 to 2
- elements: int32 [2048], P('rcv'), may hold values from 0 to 131071, as said below
Outputs:
- increment: float32 [48, 2, 131072], P(None, None, ('src', 'rcv'))
- residual: float32 [48, 2, 131072], P(None, None, ('src', 'rcv'))
The draws below stay inside these ranges and needn't reach their ends.
Inputs may be any that keep to these rules, and one draw needn't show every extreme that they name: 2048 distinct source elements, including 0 and 131071. `state`: 0 sticking, 1 slipping, 2 open.
All inputs are finite; a program needn't handle non-finite values.
Results may differ from the reference program's by a relative error of at most 0.012.
The reference program's roundings to bfloat16 on the way (of `vb` and `weighted`) count: a program that leaves them out, or rounds other values in their place, can miss the bound.
Values may be sent and summed in bfloat16 or wider, within the bound.
A program may use at most 64 MiB of HBM per device.

```python
import jax
import jax.numpy as jnp
from jax import lax

R_DEV = 128
CASES = 48
ITERS = 2
SOURCES = 131072
RECEIVERS = 2048
N_RCV = 16


def draw_elements(key, part):
    key = jax.random.fold_in(key, 11)
    first_key, second_key = jax.random.split(key)
    middle = jax.random.permutation(first_key, SOURCES - 2)[:RECEIVERS - 2] + 1
    chosen = jnp.concatenate([jnp.array([0, SOURCES - 1], dtype=jnp.int32), middle.astype(jnp.int32)])
    order = jax.random.permutation(second_key, RECEIVERS)
    return chosen[order].astype(jnp.int32)


def with_ends(values, stream_key, low, top_value):
    place = [jax.random.randint(jax.random.fold_in(stream_key, axis), (), 0, length) for axis, length in enumerate(values.shape)]
    main_axis = values.shape.index(max(values.shape))
    neighbour = place[:main_axis] + [(place[main_axis] + 1) % values.shape[main_axis]] + place[main_axis + 1:]
    return values.at[tuple(place)].set(low).at[tuple(neighbour)].set(top_value)


def steps_of(stream_key, dims, pieces, low, top_value):
    factor_of = 1.0
    for axis_at, shards_of in pieces:
        heights = jax.random.uniform(jax.random.fold_in(jax.random.fold_in(stream_key, 6), axis_at), (shards_of,), jnp.float32, low / len(pieces), top_value / len(pieces))
        factor_of = factor_of * jnp.repeat(jnp.exp(heights), dims[axis_at] // shards_of).reshape((-1,) + (1,) * (len(dims) - 1 - axis_at))
    return factor_of


def scatter_about(stream_key, dims, scale, bound, shards=(), kind=jnp.bfloat16):
    gain = steps_of(stream_key, dims, shards, -0.22, 0.18) if shards else 1.0
    drawn = jax.random.normal(stream_key, dims, jnp.float32) * scale * gain
    return jnp.minimum(jnp.maximum(drawn, -bound), bound).astype(kind)


def setup_inputs(seed: int = 0) -> dict:
    seeds = jax.random.split(jax.random.key(seed), 7)
    stiffness = scatter_about(seeds[0], (2, SOURCES, RECEIVERS), (1.0 / (SOURCES * RECEIVERS) ** 0.25), 0.046875, ((1, 32), (2, 16)))
    newton_rhs = scatter_about(seeds[1], (CASES, 2, SOURCES), 1.0, 6.0, ((2, 512),), jnp.float32)
    traction = scatter_about(seeds[2], (CASES, 2, RECEIVERS), 1.5, 8.0, ((2, 16),), jnp.float32)
    opening = scatter_about(seeds[3], (CASES, RECEIVERS), 1.0, 6.0, ((1, 16),), jnp.float32)
    state = with_ends(jax.random.randint(seeds[4], (CASES, RECEIVERS), 0, 3), jax.random.fold_in(seeds[4], 1), 0, 2).astype(jnp.int32)
    elements = draw_elements(jax.random.fold_in(seeds[6], 71), 0)
    return dict(stiffness=stiffness, newton_rhs=newton_rhs, traction=traction, opening=opening, state=state, elements=elements)


def coefficients(traction, opening, state):
    tau = traction[:, 0, :]
    press = traction[:, 1, :]
    radius = jnp.sqrt(opening * opening + press * press + 0.5)
    a_normal = 1.0 - opening / radius
    b_normal = 1.0 - press / radius
    ratio = jnp.abs(tau) / (1.0 + 0.6 * jnp.abs(press))
    a_shear = jnp.where(state == 0, 1.0, jnp.where(state == 1, ratio, 0.0))
    b_shear = jnp.where(state == 0, ratio, 1.0)
    coef_a = jnp.stack([a_shear, a_normal], axis=1).astype(jnp.float32)
    coef_b = jnp.stack([b_shear, b_normal], axis=1).astype(jnp.float32)
    return (coef_a, coef_b)

def apply_operator(vector, stiffness, coef_a, coef_b, elements):
    vb = vector.astype(jnp.bfloat16)
    shear = jnp.dot(vb[:, 0, :], stiffness[0], preferred_element_type=jnp.float32)
    normal = jnp.dot(vb[:, 1, :], stiffness[1], preferred_element_type=jnp.float32)
    kd = jnp.stack([shear, normal], axis=1)
    ed = vb[:, :, elements].astype(jnp.float32)
    jv = coef_a * ed + coef_b * kd
    weighted = (coef_b * jv).astype(jnp.bfloat16)
    lifted = coef_a * jv

    def add_block(total, index):
        first = (index * R_DEV).astype(jnp.int32)
        w_block = lax.dynamic_slice_in_dim(weighted, first, R_DEV, 2)
        l_block = lax.dynamic_slice_in_dim(lifted, first, R_DEV, 2)
        e_block = lax.dynamic_slice_in_dim(elements, first, R_DEV, 0)
        k_block = lax.dynamic_slice_in_dim(stiffness, first, R_DEV, 2)
        back_shear = jnp.dot(w_block[:, 0, :], k_block[0].T, preferred_element_type=jnp.float32)
        back_normal = jnp.dot(w_block[:, 1, :], k_block[1].T, preferred_element_type=jnp.float32)
        term = jnp.stack([back_shear, back_normal], axis=1)
        term = term.at[:, :, e_block].add(l_block)
        return (total + term, None)
    start = jnp.zeros(vector.shape, jnp.float32)
    total, unused = lax.scan(add_block, start, jnp.arange(N_RCV, dtype=jnp.int32))
    return total + 0.5 * vector

def reference(stiffness, newton_rhs, traction, opening, state, elements):
    coef_a, coef_b = coefficients(traction, opening, state)
    increment = jnp.zeros_like(newton_rhs)
    residual = newton_rhs
    direction = newton_rhs
    norm_now = lax.optimization_barrier(jnp.sum(residual * residual, axis=(1, 2)))
    for step in range(ITERS):
        image = apply_operator(direction, stiffness, coef_a, coef_b, elements)
        alpha = norm_now / lax.optimization_barrier(jnp.sum(direction * image, axis=(1, 2)))
        increment = increment + alpha[:, None, None] * direction
        residual = residual - alpha[:, None, None] * image
        norm_next = lax.optimization_barrier(jnp.sum(residual * residual, axis=(1, 2)))
        direction = residual + (norm_next / norm_now)[:, None, None] * direction
        norm_now = norm_next
    return (increment, residual)
```

```python
import jax
import jax.numpy as jnp
from jax import lax
from jax.experimental import pallas as pl
from jax.experimental.pallas import tpu as pltpu
from jax.sharding import PartitionSpec as P

MESH = pl.DeviceIdType.MESH
F32 = jnp.float32
BF16 = jnp.bfloat16
B = 48
L = 256
NY = 8
N_RCV = 16
N_SRC = 32
TILES = 13


def dot_nt(a, b):
    return lax.dot_general(a, b, (((1,), (1,)), ((), ())), preferred_element_type=F32)


def kernel(k_hbm, g_hbm, tr_hbm, op_hbm, st_hbm, el_hbm, x_hbm, r_hbm,
           g_ref, tr_ref, op_ref, st_ref, el_ref, x_ref, r_ref,
           kw, low, elb, co, co_send, sb, gat, acc, j0, ar_s, ar_in, ar_out,
           rs_send, rs_in, rs_fin, own, sib, p_ref, tb,
           k_sem, in_sem, out_sem, sib_send, sib_recv, kp_send, kp_recv, ag_send, ag_recv, rs_ssem, rs_recv, rf_recv,
           sp_send, sp_recv, a1_send, a1_recv, a2_send, a2_recv, t_send, t_recv):
    src = lax.axis_index("src")
    rcv = lax.axis_index("rcv")
    y = rcv // 2
    c = lax.rem(rcv, 2)
    other = 1 - c

    def chip(d):
        return lax.rem(y + d + NY, NY)

    def at_chip(d, core):
        return (src, chip(d) * 2 + core)

    def remote(s, d, ss, rs, dev):
        return pltpu.make_async_remote_copy(
            src_ref=s, dst_ref=d, send_sem=ss, recv_sem=rs, device_id=dev, device_id_type=MESH)

    here = (src, y * 2 + other)

    def wait_recv(ref, sem):
        remote(ref, ref, sem, sem, here).wait_recv()

    def wait_send(ref, sem):
        remote(ref, ref, sem, sem, here).wait_send()

    barrier = pltpu.get_barrier_semaphore()

    def greet(dev):
        pl.semaphore_signal(barrier, inc=1, device_id=dev, device_id_type=MESH)

    def greet_rcv(d, carry):
        greet((src, lax.rem(rcv + d, N_RCV)))
        return carry

    def greet_src(d, carry):
        greet((lax.rem(src + d, N_SRC), rcv))
        return carry

    lax.fori_loop(1, N_RCV, greet_rcv, 0)
    lax.fori_loop(1, N_SRC, greet_src, 0)

    loads = [
        pltpu.make_async_copy(a, b, in_sem.at[i])
        for i, (a, b) in enumerate((
            (g_hbm, g_ref), (tr_hbm, tr_ref), (op_hbm, op_ref), (st_hbm, st_ref), (el_hbm, el_ref)))
    ]
    for load in loads:
        load.start()
    k_copy = pltpu.make_async_copy(k_hbm.at[c], kw.at[c], k_sem)
    k_copy.start()

    lane = lax.broadcasted_iota(jnp.int32, (B, 128), 1)
    case = lax.broadcasted_iota(jnp.int32, (B, 128), 0)
    diag = lane == case

    def row_of(v):
        col = jnp.sum(v, axis=1, keepdims=True)
        return jnp.sum(jnp.where(diag, col, 0.0), axis=0, keepdims=True)

    def col_of(row):
        return jnp.sum(jnp.where(diag, row, 0.0), axis=1, keepdims=True)

    def stage(it, v0, v1):
        b0, b1 = v0.astype(BF16), v1.astype(BF16)
        sb[it, 0] = b0
        sb[it, 1] = b1
        gat[it, rcv] = jnp.where(c == 0, b0, b1)

    loads[0].wait()
    g0, g1 = g_ref[:, 0, :], g_ref[:, 1, :]
    stage(0, g0, g1)
    gg_row = row_of(g0 * g0 + g1 * g1)

    for load in loads[1:]:
        load.wait()
    tau, press = tr_ref[:, 0, :], tr_ref[:, 1, :]
    opening, state = op_ref[...], st_ref[...]
    radius = jnp.sqrt(opening * opening + press * press + 0.5)
    a_n = 1.0 - opening / radius
    b_n = 1.0 - press / radius
    ratio = jnp.abs(tau) / (1.0 + 0.6 * jnp.abs(press))
    a_s = jnp.where(state == 0, 1.0, jnp.where(state == 1, ratio, 0.0))
    b_s = jnp.where(state == 0, ratio, 1.0)
    co[c, 0] = jnp.where(c == 0, a_s, a_n)
    co[c, 1] = jnp.where(c == 0, b_s, b_n)
    co_send[0] = jnp.where(c == 0, a_n, a_s)
    co_send[1] = jnp.where(c == 0, b_n, b_s)
    elb[c, :8, :] = jnp.broadcast_to(el_ref[...], (8, 128))
    pl.semaphore_wait(barrier, N_RCV + N_SRC - 2)

    def gather_start(it):
        for comp in range(2):
            for d in (2, -2, 1, -1):
                remote(sb.at[it, comp], gat.at[it, rcv], ag_send.at[it], ag_recv.at[it, rcv], at_chip(d, comp)).start()
        remote(sb.at[it, other], gat.at[it, rcv], ag_send.at[it], ag_recv.at[it, rcv], here).start()

    def share_k(d):
        q = chip(d)
        rows = pl.ds(pl.multiple_of(q * (2 * L), 2 * L), 2 * L)
        remote(k_hbm.at[other, rows], kw.at[c, rows], kp_send, kp_recv.at[q], here).start()

    def arrived(it, d, h):
        slot = chip(d) * 2 + h
        wait_recv(gat.at[it, slot], ag_recv.at[it, slot])

    def relay(it):
        for d in (1, -1):
            for h in range(2):
                arrived(it, -2 * d, h)
                slot = chip(-2 * d) * 2 + h
                part = gat.at[it, slot]
                if (d == 1) == (h == 0):
                    remote(part, part, ag_send.at[it], ag_recv.at[it, slot], at_chip(2 * d, c)).start()
                remote(part, part, ag_send.at[it], ag_recv.at[it, slot], at_chip(d, c)).start()

    def block(q):
        rows = pl.ds(pl.multiple_of(q * (2 * L), 2 * L), 2 * L)
        return jnp.concatenate([kw[0, rows, :], kw[1, rows, :]], axis=1)

    def add_chip(it, d):
        q = chip(d)
        if it == 0:
            rows = pl.ds(pl.multiple_of(q * (2 * L), 2 * L), 2 * L)
            wait_recv(kw.at[other, rows], kp_recv.at[q])
        v0, v1 = gat[it, q * 2], gat[it, q * 2 + 1]
        acc[0] += jnp.dot(jnp.concatenate([v0, v1], axis=1), block(q), preferred_element_type=F32)
        ed = jnp.dot(jnp.concatenate([v0, v1], axis=0), low[...], preferred_element_type=F32)
        high = elb[:, 8:9, :]
        high = jnp.concatenate([high[0], high[1]], axis=1)
        acc[1] += jnp.where(high == q * 2, ed[:B], 0.0) + jnp.where(high == q * 2 + 1, ed[B:], 0.0)

    def coef(i):
        return jnp.concatenate([co[0, i], co[1, i]], axis=1)

    def reduce_src(it, tiles):
        lane_tile = coef(0) * acc[1] + coef(1) * acc[0]
        for half in range(2):
            ar_s[it, 6 * half:6 * half + 6] = lane_tile[:, 128 * half:128 * half + 128].reshape(6, 8, 128)

        def send(t, carry):
            owner = 2 * t + c

            @pl.when(owner != src)
            def _():
                remote(ar_s.at[it, t], ar_in.at[it, src], a1_send.at[it], a1_recv.at[it], (owner, rcv)).start()
            return carry

        lax.fori_loop(0, tiles, send, 0)
        mine = src - c
        is_owner = (lax.rem(mine + 2, 2) == 0) & (mine >= 0) & (mine < 2 * tiles)

        @pl.when(is_owner)
        def _():
            t = mine // 2
            ar_in[it, src] = ar_s[it, t]
            wait_recv(ar_in.at[it, pl.ds(0, N_SRC - 1)], a1_recv.at[it])
            ar_out[it, t] = jnp.sum(ar_in[it], axis=0)

            def spread(d, carry):
                remote(ar_out.at[it, t], ar_out.at[it, t], a2_send.at[it], a2_recv.at[it],
                       (lax.rem(src + d, N_SRC), rcv)).start()
                return carry

            lax.fori_loop(1, N_SRC, spread, 0)
            wait_recv(ar_out.at[it, pl.ds(0, tiles - 1)], a2_recv.at[it])
            wait_send(ar_s.at[it, pl.ds(0, tiles - 1)], a1_send.at[it])

        @pl.when(jnp.logical_not(is_owner))
        def _():
            wait_recv(ar_out.at[it, pl.ds(0, tiles)], a2_recv.at[it])
            wait_send(ar_s.at[it, pl.ds(0, tiles)], a1_send.at[it])

        return jnp.concatenate(
            [ar_out[it, 6 * half:6 * half + 6].reshape(B, 128) for half in range(2)], axis=1)

    def finish_src(it, tiles):
        mine = src - c
        is_owner = (lax.rem(mine + 2, 2) == 0) & (mine >= 0) & (mine < 2 * tiles)

        @pl.when(is_owner)
        def _():
            wait_send(ar_in.at[it, pl.ds(0, N_SRC - 1)], a2_send.at[it])

    def share_scalars(it, tile):
        tb[it, rcv] = tile

        def send(d, carry):
            remote(tb.at[it, rcv], tb.at[it, rcv], t_send.at[it], t_recv.at[it],
                   (src, lax.rem(rcv + d, N_RCV))).start()
            return carry

        lax.fori_loop(1, N_RCV, send, 0)

    def sum_scalars(it):
        wait_recv(tb.at[it, pl.ds(0, N_RCV - 1)], t_recv.at[it])
        return jnp.sum(tb[it], axis=0)

    def scatter_sources(it, jv, scalars=None):
        w = (coef(1) * jv).astype(BF16)
        lift = coef(0) * jv
        high = jnp.concatenate([elb[0, 8:9, :], elb[1, 8:9, :]], axis=1)

        def part(d):
            q = chip(d)
            both = dot_nt(w, block(q))
            sparse = jnp.concatenate(
                [jnp.where(high == q * 2, lift, 0.0), jnp.where(high == q * 2 + 1, lift, 0.0)], axis=0)
            spread = dot_nt(sparse.astype(BF16), low[...])
            return both[:, :L] + spread[:B], both[:, L:] + spread[B:]

        def send(slot, value, to, landing):
            rs_send[it, slot] = value.astype(BF16)
            remote(rs_send.at[it, slot], rs_in.at[it, landing], rs_ssem.at[it], rs_recv.at[it, landing],
                   at_chip(to, c)).start()

        def home(slot, value, d, h):
            rs_send[it, slot] = value.astype(BF16)
            landing = {1: 0, -1: 2, 2: 4, -2: 6}[d] + c
            remote(rs_send.at[it, slot], rs_fin.at[it, landing], rs_ssem.at[it], rf_recv.at[it, landing],
                   at_chip(d, h)).start()

        def came(landing):
            wait_recv(rs_in.at[it, landing], rs_recv.at[it, landing])
            return rs_in[it, landing].astype(F32)

        far = part(4)
        send(0, far[0], 2, 0)
        send(1, far[1], -2, 1)
        for k, d in enumerate((1, -1)):
            far = part(3 * d)
            send(2 + 2 * k, far[0], d, 2 + 2 * k)
            send(3 + 2 * k, far[1], d, 3 + 2 * k)
        for k, d in enumerate((1, -1)):
            near = part(d)
            home(6 + 2 * k, near[0], d, 0)
            home(7 + 2 * k, near[1], d, 1)
        if scalars is not None:
            share_scalars(it, scalars)
        up, down, mine = part(2), part(-2), part(0)
        own[it, 0] = mine[0]
        own[it, 1] = mine[1]
        remote(own.at[it, other], sib.at[it], sp_send.at[it], sp_recv.at[it], here).start()
        home(10, up[1] + came(3), 2, 1)
        home(11, down[0] + came(4), -2, 0)
        home(12, up[0] + came(2) + came(0), 2, 0)
        home(13, down[1] + came(5) + came(1), -2, 1)

    def sources_sum(it):
        wait_recv(sib.at[it], sp_recv.at[it])
        out = []
        for comp in range(2):
            total = jnp.where(c == comp, own[it, c], sib[it])
            for way in range(4):
                slot = way * 2 + comp
                wait_recv(rs_fin.at[it, slot], rf_recv.at[it, slot])
                total += rs_fin[it, slot].astype(F32)
            out.append(total)
        return out

    gather_start(0)
    co_share = remote(co_send, co.at[c], sib_send.at[0], sib_recv.at[0], here)
    co_share.start()
    el_share = remote(elb.at[c, pl.ds(0, 8)], elb.at[c, pl.ds(0, 8)], sib_send.at[1], sib_recv.at[1], here)
    el_share.start()
    for d in (0, 1, -1, 2, -2):
        share_k(d)
    acc[...] = jnp.zeros((2, B, 256), F32)
    wait_recv(elb.at[other, pl.ds(0, 8)], sib_recv.at[1])
    place = jnp.concatenate([elb[0, 0:1, :], elb[1, 0:1, :]], axis=1) - src * (NY * 2 * L)
    low[...] = jnp.where(
        lax.broadcasted_iota(jnp.int32, (L, 256), 0) == (place & (L - 1)), 1.0, 0.0).astype(BF16)
    high = place >> 8
    elb[0, 8:, :] = jnp.broadcast_to(high[:, :128], (8, 128))
    elb[1, 8:, :] = jnp.broadcast_to(high[:, 128:], (8, 128))
    k_copy.wait()

    relay(0)
    for d in (3, -3, 4):
        share_k(d)

    def add_all(it):
        arrived(it, 0, other)
        add_chip(it, 0)
        for d in (1, -1):
            arrived(it, d, 0)
            arrived(it, d, 1)
            add_chip(it, d)
        for d in (2, -2):
            add_chip(it, d)
        for d in (3, -3, 4):
            arrived(it, d, 0)
            arrived(it, d, 1)
            add_chip(it, d)

    add_all(0)
    wait_recv(co.at[other], sib_recv.at[0])
    jv = reduce_src(0, TILES - 1)
    j0[...] = jv
    gp_row = row_of(jv * jv)
    scatter_sources(0, jv)
    p0, p1 = sources_sum(0)

    stage(1, p0, p1)
    gather_start(1)
    p_ref[0] = p0
    p_ref[1] = p1
    pp_row = row_of(p0 * p0 + p1 * p1)
    share_scalars(0, jnp.concatenate(
        [gg_row, pp_row, gp_row * (1.0 / N_SRC), jnp.zeros((5, 128), F32)], axis=0))
    acc[...] = jnp.zeros((2, B, 256), F32)
    relay(1)
    add_all(1)
    ar_s[1, TILES - 1] = sum_scalars(0)
    jp = reduce_src(1, TILES)
    sums = ar_out[1, TILES - 1]
    gg, pp, gp = sums[0:1], sums[1:2], sums[2:3]
    alpha0 = gg / (0.5 * gg + gp)
    left = gp / (0.5 * gg + gp)
    rr = alpha0 * (alpha0 * pp - left * gp)
    beta = rr / gg
    scale = left + beta
    alpha0_c, left_c, scale_c = col_of(alpha0), col_of(left), col_of(scale)
    jv = scale_c * j0[...] - alpha0_c * jp
    scatter_sources(1, jv, jnp.broadcast_to(row_of(jv * jv), (8, 128)))
    jj = sum_scalars(1)[0:1]
    alpha1 = rr / (0.5 * rr * (1.0 + beta) + jj)
    alpha1_c = col_of(alpha1)
    base = []
    for comp in range(2):
        gv = g_ref[:, comp, :]
        pv = p_ref[comp]
        direction = scale_c * gv - alpha0_c * pv
        x_ref[:, comp, :] = alpha0_c * gv + alpha1_c * direction
        base.append(left_c * gv - alpha0_c * pv - alpha1_c * (0.5 * direction))
    x_out = pltpu.make_async_copy(x_ref, x_hbm, out_sem.at[0])
    x_out.start()
    q = sources_sum(1)
    for comp in range(2):
        r_ref[:, comp, :] = base[comp] - alpha1_c * q[comp]
    r_out = pltpu.make_async_copy(r_ref, r_hbm, out_sem.at[1])
    r_out.start()

    co_share.wait_send()
    el_share.wait_send()
    wait_send(kw.at[c], kp_send)
    for it in range(2):
        wait_send(gat.at[it, pl.ds(0, 15)], ag_send.at[it])
        wait_send(rs_send.at[it, pl.ds(0, 14)], rs_ssem.at[it])
        wait_send(own.at[it, 0], sp_send.at[it])
        wait_send(tb.at[it, pl.ds(0, N_RCV - 1)], t_send.at[it])
        finish_src(it, TILES - 1 + it)
    x_out.wait()
    r_out.wait()


def shards(stiffness, newton_rhs, traction, opening, state, elements):
    dma, vmem = pltpu.SemaphoreType.DMA, pltpu.VMEM
    out = jax.ShapeDtypeStruct((B, 2, L), F32)
    return pl.pallas_call(
        kernel,
        out_shape=(out, out),
        in_specs=[pl.BlockSpec(memory_space=pl.ANY)] * 6,
        out_specs=[pl.BlockSpec(memory_space=pl.ANY)] * 2,
        scratch_shapes=[
            vmem((B, 2, L), F32),
            vmem((B, 2, 128), F32),
            vmem((B, 128), F32),
            vmem((B, 128), jnp.int32),
            vmem((1, 128), jnp.int32),
            vmem((B, 2, L), F32),
            vmem((B, 2, L), F32),
            vmem((2, NY * 2 * L, 128), BF16),
            vmem((L, 256), BF16),
            vmem((2, 16, 128), jnp.int32),
            vmem((2, 2, B, 128), F32),
            vmem((2, B, 128), F32),
            vmem((2, 2, B, L), BF16),
            vmem((2, 16, B, L), BF16),
            vmem((2, B, 256), F32),
            vmem((B, 256), F32),
            vmem((2, TILES, 8, 128), F32),
            vmem((2, N_SRC, 8, 128), F32),
            vmem((2, TILES, 8, 128), F32),
            vmem((2, 16, B, L), BF16),
            vmem((2, 6, B, L), BF16),
            vmem((2, 8, B, L), BF16),
            vmem((2, 2, B, L), F32),
            vmem((2, B, L), F32),
            vmem((2, B, L), F32),
            vmem((2, N_RCV, 8, 128), F32),
            dma, dma((5,)), dma((2,)), dma((2,)), dma((2,)), dma, dma((NY,)),
            dma((2,)), dma((2, 16)), dma((2,)), dma((2, 6)), dma((2, 8)),
            dma((2,)), dma((2,)), dma((2,)), dma((2,)), dma((2,)), dma((2,)), dma((2,)), dma((2,)),
        ],
        compiler_params=pltpu.CompilerParams(
            collective_id=0, has_side_effects=True, vmem_limit_bytes=60 * 1024 * 1024),
        cost_estimate=pl.CostEstimate(flops=8 * B * 4096 * 512, bytes_accessed=4 << 20, transcendentals=0),
    )(stiffness, newton_rhs, traction, opening, state, elements.reshape(1, 128))


def solution(mesh):
    placed = (
        P(None, "src", "rcv"),
        P(None, None, ("src", "rcv")),
        P(None, None, "rcv"),
        P(None, "rcv"),
        P(None, "rcv"),
        P("rcv"),
    )
    return jax.shard_map(
        shards,
        mesh=mesh,
        in_specs=placed,
        out_specs=(P(None, None, ("src", "rcv")), P(None, None, ("src", "rcv"))),
        check_vma=False,
    )
```

```python
import jax
import jax.numpy as jnp
from jax import lax
from jax.experimental import pallas as pl
from jax.experimental.pallas import tpu as pltpu
from jax.sharding import PartitionSpec as P

MESH = pl.DeviceIdType.MESH
F32 = jnp.float32
BF16 = jnp.bfloat16
B = 48
L = 256
NY = 8
N_RCV = 16
N_SRC = 32
TILES = 6


def dot_nt(a, b):
    return lax.dot_general(a, b, (((1,), (1,)), ((), ())), preferred_element_type=F32)


def kernel(k_hbm, g_hbm, tr_hbm, op_hbm, st_hbm, el_hbm, x_hbm, r_hbm,
           g_ref, tr_ref, op_ref, st_ref, el_ref, x_ref, r_ref,
           kw, low, elb, co, co_send, sb, gat, acc, j0, ar_s, ar_in, ar_out, sc_s, sc_in, sc_out,
           rs_send, rs_in, rs_fin, own, pown, sib, tb,
           k_sem, in_sem, out_sem, sib_send, sib_recv, kp_send, kp_recv, ag_send, ag_recv, rs_ssem, rs_recv, rf_recv,
           sp_send, sp_recv, a1_send, a1_recv, a2_send, a2_recv,
           s1_send, s1_recv, s2_send, s2_recv, t_send, t_recv):
    src = lax.axis_index("src")
    rcv = lax.axis_index("rcv")
    y = rcv // 2
    c = lax.rem(rcv, 2)
    other = 1 - c

    def chip(d):
        return lax.rem(y + d + NY, NY)

    def at_chip(d, core):
        return (src, chip(d) * 2 + core)

    def remote(s, d, ss, rs, dev):
        return pltpu.make_async_remote_copy(
            src_ref=s, dst_ref=d, send_sem=ss, recv_sem=rs, device_id=dev, device_id_type=MESH)

    here = (src, y * 2 + other)

    def wait_recv(ref, sem):
        remote(ref, ref, sem, sem, here).wait_recv()

    def wait_send(ref, sem):
        remote(ref, ref, sem, sem, here).wait_send()

    loads = [
        pltpu.make_async_copy(a, b, in_sem.at[i])
        for i, (a, b) in enumerate((
            (g_hbm, g_ref), (tr_hbm, tr_ref), (op_hbm, op_ref), (st_hbm, st_ref), (el_hbm, el_ref)))
    ]
    for load in loads:
        load.start()

    barrier = pltpu.get_barrier_semaphore()

    def greet(dev):
        pl.semaphore_signal(barrier, inc=1, device_id=dev, device_id_type=MESH)

    def greet_rcv(d, carry):
        greet((src, lax.rem(rcv + d, N_RCV)))
        return carry

    def greet_src(d, carry):
        greet((lax.rem(src + d, N_SRC), rcv))
        return carry

    lax.fori_loop(1, N_RCV, greet_rcv, 0)
    lax.fori_loop(1, N_SRC, greet_src, 0)

    k_copy = pltpu.make_async_copy(k_hbm.at[c], kw.at[c], k_sem)
    k_copy.start()

    lane = lax.broadcasted_iota(jnp.int32, (B, 128), 1)
    case = lax.broadcasted_iota(jnp.int32, (B, 128), 0)
    diag = lane == case

    def row_of(v):
        col = jnp.sum(v, axis=1, keepdims=True)
        return jnp.sum(jnp.where(diag, col, 0.0), axis=0, keepdims=True)

    def col_of(row):
        return jnp.sum(jnp.where(diag, row, 0.0), axis=1, keepdims=True)

    loads[0].wait()
    g0, g1 = g_ref[:, 0, :], g_ref[:, 1, :]
    b0, b1 = g0.astype(BF16), g1.astype(BF16)
    sb[0] = b0
    sb[1] = b1
    gat[0, rcv] = jnp.where(c == 0, b0, b1)
    gg_row = row_of(g0 * g0 + g1 * g1)

    pl.semaphore_wait(barrier, N_RCV + N_SRC - 2)

    for ways in ((2, -2), (1, -1)):
        for comp in range(2):
            for d in ways:
                remote(sb.at[comp], gat.at[0, rcv], ag_send.at[0], ag_recv.at[0, rcv], at_chip(d, comp)).start()
    remote(sb.at[other], gat.at[0, rcv], ag_send.at[0], ag_recv.at[0, rcv], here).start()

    def share_k(d):
        q = chip(d)
        rows = pl.ds(pl.multiple_of(q * (2 * L), 2 * L), 2 * L)
        remote(k_hbm.at[other, rows], kw.at[c, rows], kp_send, kp_recv.at[q], here).start()

    def arrived(it, d, h):
        slot = chip(d) * 2 + h
        wait_recv(gat.at[it, slot], ag_recv.at[it, slot])

    def relay(it):
        for h in range(2):
            for d in (1, -1):
                arrived(it, -2 * d, h)
                slot = chip(-2 * d) * 2 + h
                part = gat.at[it, slot]
                if (d == 1) == (h == 0):
                    remote(part, part, ag_send.at[it], ag_recv.at[it, slot], at_chip(2 * d, c)).start()
                remote(part, part, ag_send.at[it], ag_recv.at[it, slot], at_chip(d, c)).start()

    def block(q):
        rows = pl.ds(pl.multiple_of(q * (2 * L), 2 * L), 2 * L)
        return jnp.concatenate([kw[0, rows, :], kw[1, rows, :]], axis=1)

    def add_chip(it, d):
        q = chip(d)
        if it == 0:
            rows = pl.ds(pl.multiple_of(q * (2 * L), 2 * L), 2 * L)
            wait_recv(kw.at[other, rows], kp_recv.at[q])
        v0, v1 = gat[it, q * 2], gat[it, q * 2 + 1]
        acc[0] += jnp.dot(jnp.concatenate([v0, v1], axis=1), block(q), preferred_element_type=F32)
        ed = jnp.dot(jnp.concatenate([v0, v1], axis=0), low[...], preferred_element_type=F32)
        high = elb[:, 8:9, :]
        high = jnp.concatenate([high[0], high[1]], axis=1)
        acc[1] += jnp.where(high == q * 2, ed[:B], 0.0) + jnp.where(high == q * 2 + 1, ed[B:], 0.0)

    def coef(i):
        return jnp.concatenate([co[0, i], co[1, i]], axis=1)

    def others(send):
        def one(d, carry):
            send((lax.rem(src + d, N_SRC), rcv))
            return carry

        lax.fori_loop(1, N_SRC, one, 0)

    tile = (src - 2 * c + 5) // 5 - 1
    sums_tile = (lax.rem(src - 2 * c + 5, 5) == 0) & (tile >= 0) & (tile < TILES)
    sums_scalars = src == 30 + c

    def reduce_src(it):
        part = (coef(0) * acc[1] + coef(1) * acc[0]).astype(BF16)
        for half in range(2):
            ar_s[it, 3 * half:3 * half + 3] = part[:, 128 * half:128 * half + 128].reshape(3, 16, 128)

        def send(t, carry):
            owner = 5 * t + 2 * c

            @pl.when(owner != src)
            def _():
                remote(ar_s.at[it, t], ar_in.at[it, src], a1_send.at[it], a1_recv.at[it], (owner, rcv)).start()
            return carry

        lax.fori_loop(0, TILES, send, 0)
        if it == 1:
            sc_s[...] = sum_scalars(0)

            @pl.when(jnp.logical_not(sums_scalars))
            def _():
                remote(sc_s, sc_in.at[src], s1_send, s1_recv, (30 + c, rcv)).start()

            @pl.when(sums_scalars)
            def _():
                sc_in[src] = sc_s[...]
                wait_recv(sc_in.at[pl.ds(0, N_SRC - 1)], s1_recv)
                sc_out[...] = jnp.sum(sc_in[...], axis=0)
                others(lambda dev: remote(sc_out, sc_out, s2_send, s2_recv, dev).start())

        @pl.when(sums_tile)
        def _():
            ar_in[it, src] = ar_s[it, tile]
            wait_recv(ar_in.at[it, pl.ds(0, N_SRC - 1)], a1_recv.at[it])
            ar_out[it, tile] = jnp.sum(ar_in[it].astype(F32), axis=0).astype(BF16)
            part = ar_out.at[it, tile]
            others(lambda dev: remote(part, part, a2_send.at[it], a2_recv.at[it], dev).start())
            wait_recv(ar_out.at[it, pl.ds(0, TILES - 1)], a2_recv.at[it])

        @pl.when(jnp.logical_not(sums_tile))
        def _():
            wait_recv(ar_out.at[it, pl.ds(0, TILES)], a2_recv.at[it])

        if it == 1:
            pl.when(jnp.logical_not(sums_scalars))(lambda: wait_recv(sc_out, s2_recv))
        return jnp.concatenate(
            [ar_out[it, 3 * half:3 * half + 3].reshape(B, 128) for half in range(2)], axis=1).astype(F32)

    def finish_src(it):
        @pl.when(sums_tile)
        def _():
            wait_send(ar_in.at[it, pl.ds(0, N_SRC - 1)], a2_send.at[it])
            wait_send(ar_s.at[it, pl.ds(0, TILES - 1)], a1_send.at[it])

        @pl.when(jnp.logical_not(sums_tile))
        def _():
            wait_send(ar_s.at[it, pl.ds(0, TILES)], a1_send.at[it])

        if it == 1:
            pl.when(sums_scalars)(lambda: wait_send(sc_in.at[pl.ds(0, N_SRC - 1)], s2_send))
            pl.when(jnp.logical_not(sums_scalars))(lambda: wait_send(sc_s, s1_send))

    def share_scalars(it, tile):
        tb[it, rcv] = tile

        def send(d, carry):
            remote(tb.at[it, rcv], tb.at[it, rcv], t_send.at[it], t_recv.at[it],
                   (src, lax.rem(rcv + d, N_RCV))).start()
            return carry

        lax.fori_loop(1, N_RCV, send, 0)

    def sum_scalars(it):
        wait_recv(tb.at[it, pl.ds(0, N_RCV - 1)], t_recv.at[it])
        return jnp.sum(tb[it], axis=0)

    def scatter_sources(it, jv, scalars=None):
        w = (coef(1) * jv).astype(BF16)
        lift = coef(0) * jv
        high = jnp.concatenate([elb[0, 8:9, :], elb[1, 8:9, :]], axis=1)

        def part(d):
            q = chip(d)
            both = dot_nt(w, block(q))
            sparse = jnp.concatenate(
                [jnp.where(high == q * 2, lift, 0.0), jnp.where(high == q * 2 + 1, lift, 0.0)], axis=0)
            spread = dot_nt(sparse.astype(BF16), low[...])
            return both[:, :L] + spread[:B], both[:, L:] + spread[B:]

        def send(slot, value, to, landing):
            rs_send[it, slot] = value.astype(BF16)
            remote(rs_send.at[it, slot], rs_in.at[it, landing], rs_ssem.at[it], rs_recv.at[it, landing],
                   at_chip(to, c)).start()

        def home(slot, value, d, h):
            rs_send[it, slot] = value.astype(BF16)
            landing = {1: 0, -1: 2, 2: 4, -2: 6}[d] + (h if it == 0 else c)
            remote(rs_send.at[it, slot], rs_fin.at[it, landing], rs_ssem.at[it], rf_recv.at[it, landing],
                   at_chip(d, c if it == 0 else h)).start()

        def came(landing):
            wait_recv(rs_in.at[it, landing], rs_recv.at[it, landing])
            return rs_in[it, landing].astype(F32)

        for k, d in enumerate((1, -1)):
            far = part(3 * d)
            send(2 + 2 * k, far[0], d, 2 + 2 * k)
            send(3 + 2 * k, far[1], d, 3 + 2 * k)
        far = part(4)
        send(0, far[0], 2, 0)
        send(1, far[1], -2, 1)
        for k, d in enumerate((1, -1)):
            near = part(d)
            home(6 + 2 * k, near[0], d, 0)
            home(7 + 2 * k, near[1], d, 1)
        if scalars is not None:
            share_scalars(it, scalars())
        up, down, mine = part(2), part(-2), part(0)
        own[it, 0] = mine[0]
        own[it, 1] = mine[1]
        if it == 1:
            remote(own.at[it, other], sib.at[it], sp_send.at[it], sp_recv.at[it], here).start()
        home(10, up[1] + came(3), 2, 1)
        home(11, down[0] + came(4), -2, 0)
        home(12, up[0] + came(2) + came(0), 2, 0)
        home(13, down[1] + came(5) + came(1), -2, 1)

    def arrivals(it, i):
        total = 0.0
        for way in range(4):
            slot = way * 2 + i
            wait_recv(rs_fin.at[it, slot], rf_recv.at[it, slot])
            total += rs_fin[it, slot].astype(F32)
        return total

    for load in loads[1:]:
        load.wait()
    tau, press = tr_ref[:, 0, :], tr_ref[:, 1, :]
    opening, state = op_ref[...], st_ref[...]
    radius = jnp.sqrt(opening * opening + press * press + 0.5)
    a_n = 1.0 - opening / radius
    b_n = 1.0 - press / radius
    ratio = jnp.abs(tau) / (1.0 + 0.6 * jnp.abs(press))
    a_s = jnp.where(state == 0, 1.0, jnp.where(state == 1, ratio, 0.0))
    b_s = jnp.where(state == 0, ratio, 1.0)
    co[c, 0] = jnp.where(c == 0, a_s, a_n)
    co[c, 1] = jnp.where(c == 0, b_s, b_n)
    co_send[0] = jnp.where(c == 0, a_n, a_s)
    co_send[1] = jnp.where(c == 0, b_n, b_s)
    elb[c, :8, :] = jnp.broadcast_to(el_ref[...], (8, 128))
    co_share = remote(co_send, co.at[c], sib_send.at[0], sib_recv.at[0], here)
    co_share.start()
    el_share = remote(elb.at[c, pl.ds(0, 8)], elb.at[c, pl.ds(0, 8)], sib_send.at[1], sib_recv.at[1], here)
    el_share.start()
    for d in (0, 1, -1, 2, -2):
        share_k(d)
    acc[...] = jnp.zeros((2, B, 256), F32)
    wait_recv(elb.at[other, pl.ds(0, 8)], sib_recv.at[1])
    for d in (3, -3, 4):
        share_k(d)
    place = jnp.concatenate([elb[0, 0:1, :], elb[1, 0:1, :]], axis=1) - src * (NY * 2 * L)
    low[...] = jnp.where(
        lax.broadcasted_iota(jnp.int32, (L, 256), 0) == (place & (L - 1)), 1.0, 0.0).astype(BF16)
    high = place >> 8
    elb[0, 8:, :] = jnp.broadcast_to(high[:, :128], (8, 128))
    elb[1, 8:, :] = jnp.broadcast_to(high[:, 128:], (8, 128))
    k_copy.wait()

    relay(0)

    def add_all(it):
        if it == 0:
            arrived(it, 0, other)
        add_chip(it, 0)
        for d in (1, -1):
            arrived(it, d, 0)
            arrived(it, d, 1)
            add_chip(it, d)
        for d in (2, -2):
            add_chip(it, d)
        for d in (3, -3, 4):
            arrived(it, d, 0)
            arrived(it, d, 1)
            add_chip(it, d)

    add_all(0)
    wait_recv(co.at[other], sib_recv.at[0])
    jv = reduce_src(0)
    j0[...] = jv
    scatter_sources(0, jv)
    gp_row = row_of(jv * jv)

    pp = 0.0
    for h in range(2):
        p = own[0, h] + arrivals(0, h)
        pown[h] = p
        pp += p * p
        part = gat.at[1, y * 2 + h]
        part[...] = p.astype(BF16)
        for d in (2, -2):
            remote(part, part, ag_send.at[1], ag_recv.at[1, y * 2 + h], at_chip(d, c)).start()
    for h in range(2):
        part = gat.at[1, y * 2 + h]
        for d in (1, -1):
            remote(part, part, ag_send.at[1], ag_recv.at[1, y * 2 + h], at_chip(d, c)).start()
    remote(pown.at[other], sib.at[0], sp_send.at[0], sp_recv.at[0], here).start()
    pp_row = row_of(pp)
    share_scalars(0, jnp.concatenate(
        [gg_row, pp_row, gp_row * (1.0 / N_SRC), jnp.zeros((5, 128), F32)], axis=0))
    acc[...] = jnp.zeros((2, B, 256), F32)
    relay(1)
    add_all(1)
    jp = reduce_src(1)
    sums = sc_out[...]
    gg, pp, gp = sums[0:1], sums[1:2], sums[2:3]
    alpha0 = gg / (0.5 * gg + gp)
    left = gp / (0.5 * gg + gp)
    rr = alpha0 * (alpha0 * pp - left * gp)
    beta = rr / gg
    scale = left + beta
    alpha0_c, left_c, scale_c = col_of(alpha0), col_of(left), col_of(scale)
    jv = scale_c * j0[...] - alpha0_c * jp
    scatter_sources(1, jv, lambda: jnp.broadcast_to(row_of(jv * jv), (8, 128)))
    jj = sum_scalars(1)[0:1]
    alpha1 = rr / (0.5 * rr * (1.0 + beta) + jj)
    alpha1_c = col_of(alpha1)
    wait_recv(sib.at[0], sp_recv.at[0])
    base = []
    for comp in range(2):
        gv = g_ref[:, comp, :]
        pv = jnp.where(c == comp, pown[c], sib[0])
        direction = scale_c * gv - alpha0_c * pv
        x_ref[:, comp, :] = alpha0_c * gv + alpha1_c * direction
        base.append(left_c * gv - alpha0_c * pv - alpha1_c * (0.5 * direction))
    x_out = pltpu.make_async_copy(x_ref, x_hbm, out_sem.at[0])
    x_out.start()
    wait_recv(sib.at[1], sp_recv.at[1])
    for comp in range(2):
        q = jnp.where(c == comp, own[1, c], sib[1]) + arrivals(1, comp)
        r_ref[:, comp, :] = base[comp] - alpha1_c * q
    r_out = pltpu.make_async_copy(r_ref, r_hbm, out_sem.at[1])
    r_out.start()

    co_share.wait_send()
    el_share.wait_send()
    wait_send(kw.at[c], kp_send)
    for it in range(2):
        wait_send(gat.at[it, pl.ds(0, 15 - it)], ag_send.at[it])
        wait_send(rs_send.at[it, pl.ds(0, 14)], rs_ssem.at[it])
        wait_send(own.at[it, 0], sp_send.at[it])
        wait_send(tb.at[it, pl.ds(0, N_RCV - 1)], t_send.at[it])
        finish_src(it)
    x_out.wait()
    r_out.wait()


def hand_on(x_in, r_in, x_out, r_out, sem):
    copies = [pltpu.make_async_copy(x_in, x_out, sem.at[0]), pltpu.make_async_copy(r_in, r_out, sem.at[1])]
    for copy in copies:
        copy.start()
    for copy in copies:
        copy.wait()


def shards(stiffness, newton_rhs, traction, opening, state, elements):
    dma, vmem = pltpu.SemaphoreType.DMA, pltpu.VMEM
    out = jax.ShapeDtypeStruct((B, 2, L), F32)
    x, r = pl.pallas_call(
        kernel,
        out_shape=(out, out),
        in_specs=[pl.BlockSpec(memory_space=pl.ANY)] * 6,
        out_specs=[pl.BlockSpec(memory_space=pl.ANY)] * 2,
        scratch_shapes=[
            vmem((B, 2, L), F32),
            vmem((B, 2, 128), F32),
            vmem((B, 128), F32),
            vmem((B, 128), jnp.int32),
            vmem((1, 128), jnp.int32),
            vmem((B, 2, L), F32),
            vmem((B, 2, L), F32),
            vmem((2, NY * 2 * L, 128), BF16),
            vmem((L, 256), BF16),
            vmem((2, 16, 128), jnp.int32),
            vmem((2, 2, B, 128), F32),
            vmem((2, B, 128), F32),
            vmem((2, B, L), BF16),
            vmem((2, 16, B, L), BF16),
            vmem((2, B, 256), F32),
            vmem((B, 256), F32),
            vmem((2, TILES, 16, 128), BF16),
            vmem((2, N_SRC, 16, 128), BF16),
            vmem((2, TILES, 16, 128), BF16),
            vmem((8, 128), F32),
            vmem((N_SRC, 8, 128), F32),
            vmem((8, 128), F32),
            vmem((2, 16, B, L), BF16),
            vmem((2, 6, B, L), BF16),
            vmem((2, 8, B, L), BF16),
            vmem((2, 2, B, L), F32),
            vmem((2, B, L), F32),
            vmem((2, B, L), F32),
            vmem((2, N_RCV, 8, 128), F32),
            dma, dma((5,)), dma((2,)), dma((2,)), dma((2,)), dma, dma((NY,)),
            dma((2,)), dma((2, 16)), dma((2,)), dma((2, 6)), dma((2, 8)),
            dma((2,)), dma((2,)), dma((2,)), dma((2,)), dma((2,)), dma((2,)), dma, dma, dma, dma, dma((2,)), dma((2,)),
        ],
        compiler_params=pltpu.CompilerParams(
            collective_id=0, has_side_effects=True, vmem_limit_bytes=60 * 1024 * 1024),
        cost_estimate=pl.CostEstimate(flops=8 * B * 4096 * 512, bytes_accessed=4 << 20, transcendentals=0),
    )(stiffness, newton_rhs, traction, opening, state, elements.reshape(1, 128))
    anywhere = [pl.BlockSpec(memory_space=pl.ANY)] * 2
    return pl.pallas_call(
        hand_on, out_shape=(out, out), in_specs=anywhere, out_specs=anywhere, scratch_shapes=[dma((2,))],
        compiler_params=pltpu.CompilerParams(vmem_limit_bytes=60 * 1024 * 1024))(x, r)


def solution(mesh):
    placed = (
        P(None, "src", "rcv"),
        P(None, None, ("src", "rcv")),
        P(None, None, "rcv"),
        P(None, "rcv"),
        P(None, "rcv"),
        P("rcv"),
    )
    return jax.shard_map(
        shards,
        mesh=mesh,
        in_specs=placed,
        out_specs=(P(None, None, ("src", "rcv")), P(None, None, ("src", "rcv"))),
        check_vma=False,
    )
```

```python
import jax
import jax.numpy as jnp
from jax import lax
from jax.experimental import pallas as pl
from jax.experimental.pallas import tpu as pltpu
from jax.sharding import PartitionSpec as P

MESH = pl.DeviceIdType.MESH
F32 = jnp.float32
BF16 = jnp.bfloat16
B = 48
L = 256
NY = 8
N_RCV = 16
N_SRC = 32
TILES = 6


def dot_nt(a, b):
    return lax.dot_general(a, b, (((1,), (1,)), ((), ())), preferred_element_type=F32)


def kernel(k_hbm, g_hbm, tr_hbm, op_hbm, st_hbm, el_hbm, x_hbm, r_hbm,
           g_ref, tr_ref, op_ref, st_ref, el_ref, x_ref, r_ref,
           kw, k_own, low, elb, co, co_send, sb, gat, acc, j0, ar_s, ar_in, ar_out, sc_s, sc_in, sc_out,
           rs_send, rs_in, rs_fin, own, pown, sib, tb,
           k_sem, in_sem, out_sem, sib_send, sib_recv, kp_send, kp_recv, ag_send, ag_recv, rs_ssem, rs_recv, rf_recv,
           sp_send, sp_recv, a1_send, a1_recv, a2_send, a2_recv,
           s1_send, s1_recv, s2_send, s2_recv, t_send, t_recv):
    src = lax.axis_index("src")
    rcv = lax.axis_index("rcv")
    y = rcv // 2
    c = lax.rem(rcv, 2)
    other = 1 - c

    def chip(d):
        return lax.rem(y + d + NY, NY)

    def at_chip(d, core):
        return (src, chip(d) * 2 + core)

    def remote(s, d, ss, rs, dev):
        return pltpu.make_async_remote_copy(
            src_ref=s, dst_ref=d, send_sem=ss, recv_sem=rs, device_id=dev, device_id_type=MESH)

    here = (src, y * 2 + other)

    def wait_recv(ref, sem):
        remote(ref, ref, sem, sem, here).wait_recv()

    def wait_send(ref, sem):
        remote(ref, ref, sem, sem, here).wait_send()

    loads = [
        pltpu.make_async_copy(a, b, in_sem.at[i])
        for i, (a, b) in enumerate((
            (g_hbm, g_ref), (tr_hbm, tr_ref), (op_hbm, op_ref), (st_hbm, st_ref), (el_hbm, el_ref)))
    ]
    for load in loads:
        load.start()

    barrier = pltpu.get_barrier_semaphore()

    def greet(dev):
        pl.semaphore_signal(barrier, inc=1, device_id=dev, device_id_type=MESH)

    def greet_rcv(d, carry):
        greet((src, lax.rem(rcv + d, N_RCV)))
        return carry

    def greet_src(d, carry):
        greet((lax.rem(src + d, N_SRC), rcv))
        return carry

    lax.fori_loop(1, N_RCV, greet_rcv, 0)
    lax.fori_loop(1, N_SRC, greet_src, 0)

    k_away = pltpu.make_async_copy(k_hbm.at[other], k_own, k_sem.at[1])
    k_away.start()
    k_copy = pltpu.make_async_copy(k_hbm.at[c], kw.at[c], k_sem.at[0])
    k_copy.start()

    lane = lax.broadcasted_iota(jnp.int32, (B, 128), 1)
    case = lax.broadcasted_iota(jnp.int32, (B, 128), 0)
    diag = lane == case

    def row_of(v):
        col = jnp.sum(v, axis=1, keepdims=True)
        return jnp.sum(jnp.where(diag, col, 0.0), axis=0, keepdims=True)

    def col_of(row):
        return jnp.sum(jnp.where(diag, row, 0.0), axis=1, keepdims=True)

    loads[0].wait()
    g0, g1 = g_ref[:, 0, :], g_ref[:, 1, :]
    b0, b1 = g0.astype(BF16), g1.astype(BF16)
    sb[0] = b0
    sb[1] = b1
    gat[0, rcv] = jnp.where(c == 0, b0, b1)
    gg_row = row_of(g0 * g0 + g1 * g1)

    pl.semaphore_wait(barrier, N_RCV + N_SRC - 2)

    for ways in ((2, -2), (1, -1)):
        for comp in range(2):
            for d in ways:
                remote(sb.at[comp], gat.at[0, rcv], ag_send.at[0], ag_recv.at[0, rcv], at_chip(d, comp)).start()
    remote(sb.at[other], gat.at[0, rcv], ag_send.at[0], ag_recv.at[0, rcv], here).start()

    def share_k(d):
        q = chip(d)
        rows = pl.ds(pl.multiple_of(q * (2 * L), 2 * L), 2 * L)
        remote(k_own.at[rows], kw.at[c, rows], kp_send, kp_recv.at[q], here).start()

    def arrived(it, d, h):
        slot = chip(d) * 2 + h
        wait_recv(gat.at[it, slot], ag_recv.at[it, slot])

    def relay(it):
        for h in range(2):
            for d in (1, -1):
                arrived(it, -2 * d, h)
                slot = chip(-2 * d) * 2 + h
                part = gat.at[it, slot]
                if (d == 1) == (h == 0):
                    remote(part, part, ag_send.at[it], ag_recv.at[it, slot], at_chip(2 * d, c)).start()
                remote(part, part, ag_send.at[it], ag_recv.at[it, slot], at_chip(d, c)).start()

    def block(q):
        rows = pl.ds(pl.multiple_of(q * (2 * L), 2 * L), 2 * L)
        return jnp.concatenate([kw[0, rows, :], kw[1, rows, :]], axis=1)

    def add_chip(it, d):
        q = chip(d)
        if it == 0:
            rows = pl.ds(pl.multiple_of(q * (2 * L), 2 * L), 2 * L)
            wait_recv(kw.at[other, rows], kp_recv.at[q])
        v0, v1 = gat[it, q * 2], gat[it, q * 2 + 1]
        acc[0] += jnp.dot(jnp.concatenate([v0, v1], axis=1), block(q), preferred_element_type=F32)
        ed = jnp.dot(jnp.concatenate([v0, v1], axis=0), low[...], preferred_element_type=F32)
        high = elb[:, 8:9, :]
        high = jnp.concatenate([high[0], high[1]], axis=1)
        acc[1] += jnp.where(high == q * 2, ed[:B], 0.0) + jnp.where(high == q * 2 + 1, ed[B:], 0.0)

    def coef(i):
        return jnp.concatenate([co[0, i], co[1, i]], axis=1)

    def others(send):
        def one(d, carry):
            send((lax.rem(src + d, N_SRC), rcv))
            return carry

        lax.fori_loop(1, N_SRC, one, 0)

    tile = (src - 2 * c + 5) // 5 - 1
    sums_tile = (lax.rem(src - 2 * c + 5, 5) == 0) & (tile >= 0) & (tile < TILES)
    sums_scalars = src == 30 + c

    def reduce_src(it):
        part = (coef(0) * acc[1] + coef(1) * acc[0]).astype(BF16)
        for half in range(2):
            ar_s[it, 3 * half:3 * half + 3] = part[:, 128 * half:128 * half + 128].reshape(3, 16, 128)

        def send(t, carry):
            owner = 5 * t + 2 * c

            @pl.when(owner != src)
            def _():
                remote(ar_s.at[it, t], ar_in.at[it, src], a1_send.at[it], a1_recv.at[it], (owner, rcv)).start()
            return carry

        lax.fori_loop(0, TILES, send, 0)
        if it == 1:
            sc_s[...] = sum_scalars(0)

            @pl.when(jnp.logical_not(sums_scalars))
            def _():
                remote(sc_s, sc_in.at[src], s1_send, s1_recv, (30 + c, rcv)).start()

            @pl.when(sums_scalars)
            def _():
                sc_in[src] = sc_s[...]
                wait_recv(sc_in.at[pl.ds(0, N_SRC - 1)], s1_recv)
                sc_out[...] = jnp.sum(sc_in[...], axis=0)
                others(lambda dev: remote(sc_out, sc_out, s2_send, s2_recv, dev).start())

        @pl.when(sums_tile)
        def _():
            ar_in[it, src] = ar_s[it, tile]
            wait_recv(ar_in.at[it, pl.ds(0, N_SRC - 1)], a1_recv.at[it])
            ar_out[it, tile] = jnp.sum(ar_in[it].astype(F32), axis=0).astype(BF16)
            part = ar_out.at[it, tile]
            others(lambda dev: remote(part, part, a2_send.at[it], a2_recv.at[it], dev).start())
            wait_recv(ar_out.at[it, pl.ds(0, TILES - 1)], a2_recv.at[it])

        @pl.when(jnp.logical_not(sums_tile))
        def _():
            wait_recv(ar_out.at[it, pl.ds(0, TILES)], a2_recv.at[it])

        if it == 1:
            pl.when(jnp.logical_not(sums_scalars))(lambda: wait_recv(sc_out, s2_recv))
        return jnp.concatenate(
            [ar_out[it, 3 * half:3 * half + 3].reshape(B, 128) for half in range(2)], axis=1).astype(F32)

    def finish_src(it):
        @pl.when(sums_tile)
        def _():
            wait_send(ar_in.at[it, pl.ds(0, N_SRC - 1)], a2_send.at[it])
            wait_send(ar_s.at[it, pl.ds(0, TILES - 1)], a1_send.at[it])

        @pl.when(jnp.logical_not(sums_tile))
        def _():
            wait_send(ar_s.at[it, pl.ds(0, TILES)], a1_send.at[it])

        if it == 1:
            pl.when(sums_scalars)(lambda: wait_send(sc_in.at[pl.ds(0, N_SRC - 1)], s2_send))
            pl.when(jnp.logical_not(sums_scalars))(lambda: wait_send(sc_s, s1_send))

    def share_scalars(it, tile):
        tb[it, rcv] = tile

        def send(d, carry):
            remote(tb.at[it, rcv], tb.at[it, rcv], t_send.at[it], t_recv.at[it],
                   (src, lax.rem(rcv + d, N_RCV))).start()
            return carry

        lax.fori_loop(1, N_RCV, send, 0)

    def sum_scalars(it):
        wait_recv(tb.at[it, pl.ds(0, N_RCV - 1)], t_recv.at[it])
        return jnp.sum(tb[it], axis=0)

    def scatter_sources(it, jv, scalars=None):
        w = (coef(1) * jv).astype(BF16)
        lift = coef(0) * jv
        high = jnp.concatenate([elb[0, 8:9, :], elb[1, 8:9, :]], axis=1)

        def part(d):
            q = chip(d)
            both = dot_nt(w, block(q))
            sparse = jnp.concatenate(
                [jnp.where(high == q * 2, lift, 0.0), jnp.where(high == q * 2 + 1, lift, 0.0)], axis=0)
            spread = dot_nt(sparse.astype(BF16), low[...])
            return both[:, :L] + spread[:B], both[:, L:] + spread[B:]

        def send(slot, value, to, landing):
            rs_send[it, slot] = value.astype(BF16)
            remote(rs_send.at[it, slot], rs_in.at[it, landing], rs_ssem.at[it], rs_recv.at[it, landing],
                   at_chip(to, c)).start()

        def home(slot, value, d, h):
            rs_send[it, slot] = value.astype(BF16)
            landing = {1: 0, -1: 2, 2: 4, -2: 6}[d] + (h if it == 0 else c)
            remote(rs_send.at[it, slot], rs_fin.at[it, landing], rs_ssem.at[it], rf_recv.at[it, landing],
                   at_chip(d, c if it == 0 else h)).start()

        def came(landing):
            wait_recv(rs_in.at[it, landing], rs_recv.at[it, landing])
            return rs_in[it, landing].astype(F32)

        for k, d in enumerate((1, -1)):
            far = part(3 * d)
            send(2 + 2 * k, far[0], d, 2 + 2 * k)
            send(3 + 2 * k, far[1], d, 3 + 2 * k)
        far = part(4)
        send(0, far[0], 2, 0)
        send(1, far[1], -2, 1)
        for k, d in enumerate((1, -1)):
            near = part(d)
            home(6 + 2 * k, near[0], d, 0)
            home(7 + 2 * k, near[1], d, 1)
        if scalars is not None:
            share_scalars(it, scalars())
        up, down, mine = part(2), part(-2), part(0)
        own[it, 0] = mine[0]
        own[it, 1] = mine[1]
        if it == 1:
            remote(own.at[it, other], sib.at[it], sp_send.at[it], sp_recv.at[it], here).start()
        home(10, up[1] + came(3), 2, 1)
        home(11, down[0] + came(4), -2, 0)
        home(12, up[0] + came(2) + came(0), 2, 0)
        home(13, down[1] + came(5) + came(1), -2, 1)

    def arrivals(it, i):
        total = 0.0
        for way in range(4):
            slot = way * 2 + i
            wait_recv(rs_fin.at[it, slot], rf_recv.at[it, slot])
            total += rs_fin[it, slot].astype(F32)
        return total

    for load in loads[1:]:
        load.wait()
    tau, press = tr_ref[:, 0, :], tr_ref[:, 1, :]
    opening, state = op_ref[...], st_ref[...]
    radius = jnp.sqrt(opening * opening + press * press + 0.5)
    a_n = 1.0 - opening / radius
    b_n = 1.0 - press / radius
    ratio = jnp.abs(tau) / (1.0 + 0.6 * jnp.abs(press))
    a_s = jnp.where(state == 0, 1.0, jnp.where(state == 1, ratio, 0.0))
    b_s = jnp.where(state == 0, ratio, 1.0)
    co[c, 0] = jnp.where(c == 0, a_s, a_n)
    co[c, 1] = jnp.where(c == 0, b_s, b_n)
    co_send[0] = jnp.where(c == 0, a_n, a_s)
    co_send[1] = jnp.where(c == 0, b_n, b_s)
    elb[c, :8, :] = jnp.broadcast_to(el_ref[...], (8, 128))
    co_share = remote(co_send, co.at[c], sib_send.at[0], sib_recv.at[0], here)
    co_share.start()
    el_share = remote(elb.at[c, pl.ds(0, 8)], elb.at[c, pl.ds(0, 8)], sib_send.at[1], sib_recv.at[1], here)
    el_share.start()
    k_away.wait()
    for d in (0, 1, -1, 2, -2):
        share_k(d)
    acc[...] = jnp.zeros((2, B, 256), F32)
    wait_recv(elb.at[other, pl.ds(0, 8)], sib_recv.at[1])
    for d in (3, -3, 4):
        share_k(d)
    place = jnp.concatenate([elb[0, 0:1, :], elb[1, 0:1, :]], axis=1) - src * (NY * 2 * L)
    low[...] = jnp.where(
        lax.broadcasted_iota(jnp.int32, (L, 256), 0) == (place & (L - 1)), 1.0, 0.0).astype(BF16)
    high = place >> 8
    elb[0, 8:, :] = jnp.broadcast_to(high[:, :128], (8, 128))
    elb[1, 8:, :] = jnp.broadcast_to(high[:, 128:], (8, 128))
    k_copy.wait()

    relay(0)

    def add_all(it):
        if it == 0:
            arrived(it, 0, other)
        add_chip(it, 0)
        for d in (1, -1):
            arrived(it, d, 0)
            arrived(it, d, 1)
            add_chip(it, d)
        for d in (2, -2):
            add_chip(it, d)
        for d in (3, -3, 4):
            arrived(it, d, 0)
            arrived(it, d, 1)
            add_chip(it, d)

    add_all(0)
    wait_recv(co.at[other], sib_recv.at[0])
    jv = reduce_src(0)
    j0[...] = jv
    scatter_sources(0, jv)
    gp_row = row_of(jv * jv)

    pp = 0.0
    for h in range(2):
        p = own[0, h] + arrivals(0, h)
        pown[h] = p
        pp += p * p
        part = gat.at[1, y * 2 + h]
        part[...] = p.astype(BF16)
        for d in (2, -2):
            remote(part, part, ag_send.at[1], ag_recv.at[1, y * 2 + h], at_chip(d, c)).start()
    for h in range(2):
        part = gat.at[1, y * 2 + h]
        for d in (1, -1):
            remote(part, part, ag_send.at[1], ag_recv.at[1, y * 2 + h], at_chip(d, c)).start()
    remote(pown.at[other], sib.at[0], sp_send.at[0], sp_recv.at[0], here).start()
    pp_row = row_of(pp)
    share_scalars(0, jnp.concatenate(
        [gg_row, pp_row, gp_row * (1.0 / N_SRC), jnp.zeros((5, 128), F32)], axis=0))
    acc[...] = jnp.zeros((2, B, 256), F32)
    relay(1)
    add_all(1)
    jp = reduce_src(1)
    sums = sc_out[...]
    gg, pp, gp = sums[0:1], sums[1:2], sums[2:3]
    alpha0 = gg / (0.5 * gg + gp)
    left = gp / (0.5 * gg + gp)
    rr = alpha0 * (alpha0 * pp - left * gp)
    beta = rr / gg
    scale = left + beta
    alpha0_c, left_c, scale_c = col_of(alpha0), col_of(left), col_of(scale)
    jv = scale_c * j0[...] - alpha0_c * jp
    scatter_sources(1, jv, lambda: jnp.broadcast_to(row_of(jv * jv), (8, 128)))
    jj = sum_scalars(1)[0:1]
    alpha1 = rr / (0.5 * rr * (1.0 + beta) + jj)
    alpha1_c = col_of(alpha1)
    wait_recv(sib.at[0], sp_recv.at[0])
    base = []
    for comp in range(2):
        gv = g_ref[:, comp, :]
        pv = jnp.where(c == comp, pown[c], sib[0])
        direction = scale_c * gv - alpha0_c * pv
        x_ref[:, comp, :] = alpha0_c * gv + alpha1_c * direction
        base.append(left_c * gv - alpha0_c * pv - alpha1_c * (0.5 * direction))
    x_out = pltpu.make_async_copy(x_ref, x_hbm, out_sem.at[0])
    x_out.start()
    wait_recv(sib.at[1], sp_recv.at[1])
    for comp in range(2):
        q = jnp.where(c == comp, own[1, c], sib[1]) + arrivals(1, comp)
        r_ref[:, comp, :] = base[comp] - alpha1_c * q
    r_out = pltpu.make_async_copy(r_ref, r_hbm, out_sem.at[1])
    r_out.start()

    co_share.wait_send()
    el_share.wait_send()
    wait_send(kw.at[c], kp_send)
    for it in range(2):
        wait_send(gat.at[it, pl.ds(0, 15 - it)], ag_send.at[it])
        wait_send(rs_send.at[it, pl.ds(0, 14)], rs_ssem.at[it])
        wait_send(own.at[it, 0], sp_send.at[it])
        wait_send(tb.at[it, pl.ds(0, N_RCV - 1)], t_send.at[it])
        finish_src(it)
    x_out.wait()
    r_out.wait()


def shards(stiffness, newton_rhs, traction, opening, state, elements):
    dma, vmem = pltpu.SemaphoreType.DMA, pltpu.VMEM
    out = jax.ShapeDtypeStruct((B, 2, L), F32)
    return pl.pallas_call(
        kernel,
        out_shape=(out, out),
        in_specs=[pl.BlockSpec(memory_space=pl.ANY)] * 6,
        out_specs=[pl.BlockSpec(memory_space=pl.ANY)] * 2,
        scratch_shapes=[
            vmem((B, 2, L), F32),
            vmem((B, 2, 128), F32),
            vmem((B, 128), F32),
            vmem((B, 128), jnp.int32),
            vmem((1, 128), jnp.int32),
            vmem((B, 2, L), F32),
            vmem((B, 2, L), F32),
            vmem((2, NY * 2 * L, 128), BF16),
            vmem((NY * 2 * L, 128), BF16),
            vmem((L, 256), BF16),
            vmem((2, 16, 128), jnp.int32),
            vmem((2, 2, B, 128), F32),
            vmem((2, B, 128), F32),
            vmem((2, B, L), BF16),
            vmem((2, 16, B, L), BF16),
            vmem((2, B, 256), F32),
            vmem((B, 256), F32),
            vmem((2, TILES, 16, 128), BF16),
            vmem((2, N_SRC, 16, 128), BF16),
            vmem((2, TILES, 16, 128), BF16),
            vmem((8, 128), F32),
            vmem((N_SRC, 8, 128), F32),
            vmem((8, 128), F32),
            vmem((2, 16, B, L), BF16),
            vmem((2, 6, B, L), BF16),
            vmem((2, 8, B, L), BF16),
            vmem((2, 2, B, L), F32),
            vmem((2, B, L), F32),
            vmem((2, B, L), F32),
            vmem((2, N_RCV, 8, 128), F32),
            dma((2,)), dma((5,)), dma((2,)), dma((2,)), dma((2,)), dma, dma((NY,)),
            dma((2,)), dma((2, 16)), dma((2,)), dma((2, 6)), dma((2, 8)),
            dma((2,)), dma((2,)), dma((2,)), dma((2,)), dma((2,)), dma((2,)), dma, dma, dma, dma, dma((2,)), dma((2,)),
        ],
        compiler_params=pltpu.CompilerParams(
            collective_id=0, has_side_effects=True, vmem_limit_bytes=60 * 1024 * 1024),
        cost_estimate=pl.CostEstimate(flops=8 * B * 4096 * 512, bytes_accessed=4 << 20, transcendentals=0),
    )(stiffness, newton_rhs, traction, opening, state, elements.reshape(1, 128))


def solution(mesh):
    placed = (
        P(None, "src", "rcv"),
        P(None, None, ("src", "rcv")),
        P(None, None, "rcv"),
        P(None, "rcv"),
        P(None, "rcv"),
        P("rcv"),
    )
    return jax.shard_map(
        shards,
        mesh=mesh,
        in_specs=placed,
        out_specs=(P(None, None, ("src", "rcv")), P(None, None, ("src", "rcv"))),
        check_vma=False,
    )
```

```python
import jax
import jax.numpy as jnp
from jax import lax
from jax.experimental import pallas as pl
from jax.experimental.pallas import tpu as pltpu
from jax.sharding import PartitionSpec as P

MESH = pl.DeviceIdType.MESH
F32 = jnp.float32
BF16 = jnp.bfloat16
B = 48
L = 256
NY = 8
N_RCV = 16
N_SRC = 32
TILES = 6
ORDER = (0, 1, -1, 2, -2, 3, -3, 4)


def dot_nt(a, b):
    return lax.dot_general(a, b, (((1,), (1,)), ((), ())), preferred_element_type=F32)


def kernel(k_hbm, g_hbm, tr_hbm, op_hbm, st_hbm, el_hbm, x_ref, r_ref,
           g_ref, tr_ref, op_ref, st_ref, el_ref,
           kw, k_own, low, elb, co, co_send, sb, gat, acc, j0, ar_s, ar_in, ar_out, sc_s, sc_in, sc_out,
           rs_send, rs_in, rs_fin, own, pown, sib, tb,
           k_sem, ka_sem, g_sem, in_sem, sib_send, sib_recv, kp_send, kp_recv, ag_send, ag_recv, rs_ssem, rs_recv, rf_recv,
           sp_send, sp_recv, a1_send, a1_recv, a2_send, a2_recv,
           s1_send, s1_recv, s2_send, s2_recv, t_send, t_recv):
    src = lax.axis_index("src")
    rcv = lax.axis_index("rcv")
    y = rcv // 2
    c = lax.rem(rcv, 2)
    other = 1 - c

    def chip(d):
        return lax.rem(y + d + NY, NY)

    def at_chip(d, core):
        return (src, chip(d) * 2 + core)

    def remote(s, d, ss, rs, dev):
        return pltpu.make_async_remote_copy(
            src_ref=s, dst_ref=d, send_sem=ss, recv_sem=rs, device_id=dev, device_id_type=MESH)

    here = (src, y * 2 + other)

    def wait_recv(ref, sem):
        remote(ref, ref, sem, sem, here).wait_recv()

    def wait_send(ref, sem):
        remote(ref, ref, sem, sem, here).wait_send()

    g_loads = [
        pltpu.make_async_copy(g_hbm.at[pl.ds(8 * i, 8)], g_ref.at[pl.ds(8 * i, 8)], g_sem.at[i]) for i in range(B // 8)]
    for load in g_loads:
        load.start()
    loads = [
        pltpu.make_async_copy(a, b, in_sem.at[i])
        for i, (a, b) in enumerate((
            (tr_hbm, tr_ref), (op_hbm, op_ref), (st_hbm, st_ref), (el_hbm, el_ref)))
    ]
    for load in loads:
        load.start()

    barrier = pltpu.get_barrier_semaphore()

    def greet(dev):
        pl.semaphore_signal(barrier, inc=1, device_id=dev, device_id_type=MESH)

    def greet_rcv(d, carry):
        greet((src, lax.rem(rcv + d, N_RCV)))
        return carry

    def greet_src(d, carry):
        greet((lax.rem(src + d, N_SRC), rcv))
        return carry

    lax.fori_loop(1, N_RCV, greet_rcv, 0)
    lax.fori_loop(1, N_SRC, greet_src, 0)

    def k_rows(d):
        return pl.ds(pl.multiple_of(chip(d) * (2 * L), 2 * L), 2 * L)

    def k_away(d):
        return pltpu.make_async_copy(k_hbm.at[other, k_rows(d)], k_own.at[k_rows(d)], ka_sem.at[chip(d)])

    def k_copy(d):
        return pltpu.make_async_copy(k_hbm.at[c, k_rows(d)], kw.at[c, k_rows(d)], k_sem.at[chip(d)])

    for d in ORDER:
        k_away(d).start()
        k_copy(d).start()

    lane = lax.broadcasted_iota(jnp.int32, (B, 128), 1)
    case = lax.broadcasted_iota(jnp.int32, (B, 128), 0)
    diag = lane == case

    def row_of(v):
        col = jnp.sum(v, axis=1, keepdims=True)
        return jnp.sum(jnp.where(diag, col, 0.0), axis=0, keepdims=True)

    def col_of(row):
        return jnp.sum(jnp.where(diag, row, 0.0), axis=1, keepdims=True)

    for load in g_loads:
        load.wait()
    g0, g1 = g_ref[:, 0, :], g_ref[:, 1, :]
    b0, b1 = g0.astype(BF16), g1.astype(BF16)
    sb[0] = b0
    sb[1] = b1
    gat[0, rcv] = jnp.where(c == 0, b0, b1)
    gg_row = row_of(g0 * g0 + g1 * g1)

    pl.semaphore_wait(barrier, N_RCV + N_SRC - 2)

    def first_sends(comp):
        for d in (2, -2, 1, -1):
            remote(sb.at[comp], gat.at[0, rcv], ag_send.at[0], ag_recv.at[0, rcv], at_chip(d, comp)).start()

    first_sends(0)
    remote(sb.at[other], gat.at[0, rcv], ag_send.at[0], ag_recv.at[0, rcv], here).start()

    def share_k(d):
        k_away(d).wait()
        remote(k_own.at[k_rows(d)], kw.at[c, k_rows(d)], kp_send, kp_recv.at[chip(d)], here).start()

    def arrived(it, d, h):
        slot = chip(d) * 2 + h
        wait_recv(gat.at[it, slot], ag_recv.at[it, slot])

    def relay(it):
        for h in range(2):
            for d in (1, -1):
                arrived(it, -2 * d, h)
                slot = chip(-2 * d) * 2 + h
                part = gat.at[it, slot]
                if (d == 1) == (h == 0):
                    remote(part, part, ag_send.at[it], ag_recv.at[it, slot], at_chip(2 * d, c)).start()
                remote(part, part, ag_send.at[it], ag_recv.at[it, slot], at_chip(d, c)).start()

    def block(q):
        rows = pl.ds(pl.multiple_of(q * (2 * L), 2 * L), 2 * L)
        return jnp.concatenate([kw[0, rows, :], kw[1, rows, :]], axis=1)

    def add_chip(it, d):
        q = chip(d)
        if it == 0:
            k_copy(d).wait()
            wait_recv(kw.at[other, k_rows(d)], kp_recv.at[q])
        v0, v1 = gat[it, q * 2], gat[it, q * 2 + 1]
        acc[0] += jnp.dot(jnp.concatenate([v0, v1], axis=1), block(q), preferred_element_type=F32)
        ed = jnp.dot(jnp.concatenate([v0, v1], axis=0), low[...], preferred_element_type=F32)
        high = elb[:, 8:9, :]
        high = jnp.concatenate([high[0], high[1]], axis=1)
        acc[1] += jnp.where(high == q * 2, ed[:B], 0.0) + jnp.where(high == q * 2 + 1, ed[B:], 0.0)

    def coef(i):
        return jnp.concatenate([co[0, i], co[1, i]], axis=1)

    def others(send):
        def one(d, carry):
            send((lax.rem(src + d, N_SRC), rcv))
            return carry

        lax.fori_loop(1, N_SRC, one, 0)

    tile = (src - 2 * c + 5) // 5 - 1
    sums_tile = (lax.rem(src - 2 * c + 5, 5) == 0) & (tile >= 0) & (tile < TILES)
    sums_scalars = src == 30 + c

    def reduce_src(it):
        part = (coef(0) * acc[1] + coef(1) * acc[0]).astype(BF16)
        for half in range(2):
            ar_s[it, 3 * half:3 * half + 3] = part[:, 128 * half:128 * half + 128].reshape(3, 16, 128)

        def send(t, carry):
            owner = 5 * t + 2 * c

            @pl.when(owner != src)
            def _():
                remote(ar_s.at[it, t], ar_in.at[it, src], a1_send.at[it], a1_recv.at[it], (owner, rcv)).start()
            return carry

        lax.fori_loop(0, TILES, send, 0)
        if it == 1:
            sc_s[...] = sum_scalars(0)

            @pl.when(jnp.logical_not(sums_scalars))
            def _():
                remote(sc_s, sc_in.at[src], s1_send, s1_recv, (30 + c, rcv)).start()

            @pl.when(sums_scalars)
            def _():
                sc_in[src] = sc_s[...]
                wait_recv(sc_in.at[pl.ds(0, N_SRC - 1)], s1_recv)
                sc_out[...] = jnp.sum(sc_in[...], axis=0)
                others(lambda dev: remote(sc_out, sc_out, s2_send, s2_recv, dev).start())

        @pl.when(sums_tile)
        def _():
            ar_in[it, src] = ar_s[it, tile]
            wait_recv(ar_in.at[it, pl.ds(0, N_SRC - 1)], a1_recv.at[it])
            ar_out[it, tile] = jnp.sum(ar_in[it].astype(F32), axis=0).astype(BF16)
            part = ar_out.at[it, tile]
            others(lambda dev: remote(part, part, a2_send.at[it], a2_recv.at[it], dev).start())
            wait_recv(ar_out.at[it, pl.ds(0, TILES - 1)], a2_recv.at[it])

        @pl.when(jnp.logical_not(sums_tile))
        def _():
            wait_recv(ar_out.at[it, pl.ds(0, TILES)], a2_recv.at[it])

        if it == 1:
            pl.when(jnp.logical_not(sums_scalars))(lambda: wait_recv(sc_out, s2_recv))
        return jnp.concatenate(
            [ar_out[it, 3 * half:3 * half + 3].reshape(B, 128) for half in range(2)], axis=1).astype(F32)

    def finish_src(it):
        @pl.when(sums_tile)
        def _():
            wait_send(ar_in.at[it, pl.ds(0, N_SRC - 1)], a2_send.at[it])
            wait_send(ar_s.at[it, pl.ds(0, TILES - 1)], a1_send.at[it])

        @pl.when(jnp.logical_not(sums_tile))
        def _():
            wait_send(ar_s.at[it, pl.ds(0, TILES)], a1_send.at[it])

        if it == 1:
            pl.when(sums_scalars)(lambda: wait_send(sc_in.at[pl.ds(0, N_SRC - 1)], s2_send))
            pl.when(jnp.logical_not(sums_scalars))(lambda: wait_send(sc_s, s1_send))

    def share_scalars(it, tile):
        tb[it, rcv] = tile

        def send(d, carry):
            remote(tb.at[it, rcv], tb.at[it, rcv], t_send.at[it], t_recv.at[it],
                   (src, lax.rem(rcv + d, N_RCV))).start()
            return carry

        lax.fori_loop(1, N_RCV, send, 0)

    def sum_scalars(it):
        wait_recv(tb.at[it, pl.ds(0, N_RCV - 1)], t_recv.at[it])
        return jnp.sum(tb[it], axis=0)

    def scatter_sources(it, jv, scalars=None):
        w = (coef(1) * jv).astype(BF16)
        lift = coef(0) * jv
        high = jnp.concatenate([elb[0, 8:9, :], elb[1, 8:9, :]], axis=1)

        def part(d):
            q = chip(d)
            both = dot_nt(w, block(q))
            sparse = jnp.concatenate(
                [jnp.where(high == q * 2, lift, 0.0), jnp.where(high == q * 2 + 1, lift, 0.0)], axis=0)
            spread = dot_nt(sparse.astype(BF16), low[...])
            return both[:, :L] + spread[:B], both[:, L:] + spread[B:]

        def send(slot, value, to, landing):
            rs_send[it, slot] = value.astype(BF16)
            remote(rs_send.at[it, slot], rs_in.at[it, landing], rs_ssem.at[it], rs_recv.at[it, landing],
                   at_chip(to, c)).start()

        def home(slot, value, d, h):
            rs_send[it, slot] = value.astype(BF16)
            landing = {1: 0, -1: 2, 2: 4, -2: 6}[d] + (h if it == 0 else c)
            remote(rs_send.at[it, slot], rs_fin.at[it, landing], rs_ssem.at[it], rf_recv.at[it, landing],
                   at_chip(d, c if it == 0 else h)).start()

        def came(landing):
            wait_recv(rs_in.at[it, landing], rs_recv.at[it, landing])
            return rs_in[it, landing].astype(F32)

        for k, d in enumerate((1, -1)):
            far = part(3 * d)
            send(2 + 2 * k, far[0], d, 2 + 2 * k)
            send(3 + 2 * k, far[1], d, 3 + 2 * k)
        far = part(4)
        send(0, far[0], 2, 0)
        send(1, far[1], -2, 1)
        for k, d in enumerate((1, -1)):
            near = part(d)
            home(6 + 2 * k, near[0], d, 0)
            home(7 + 2 * k, near[1], d, 1)
        if scalars is not None:
            share_scalars(it, scalars())
        up, down, mine = part(2), part(-2), part(0)
        own[it, 0] = mine[0]
        own[it, 1] = mine[1]
        if it == 1:
            remote(own.at[it, other], sib.at[it], sp_send.at[it], sp_recv.at[it], here).start()
        home(10, up[1] + came(3), 2, 1)
        home(11, down[0] + came(4), -2, 0)
        home(12, up[0] + came(2) + came(0), 2, 0)
        home(13, down[1] + came(5) + came(1), -2, 1)

    def arrivals(it, i):
        total = 0.0
        for way in range(4):
            slot = way * 2 + i
            wait_recv(rs_fin.at[it, slot], rf_recv.at[it, slot])
            total += rs_fin[it, slot].astype(F32)
        return total

    for load in loads:
        load.wait()
    tau, press = tr_ref[:, 0, :], tr_ref[:, 1, :]
    opening, state = op_ref[...], st_ref[...]
    radius = jnp.sqrt(opening * opening + press * press + 0.5)
    a_n = 1.0 - opening / radius
    b_n = 1.0 - press / radius
    ratio = jnp.abs(tau) / (1.0 + 0.6 * jnp.abs(press))
    a_s = jnp.where(state == 0, 1.0, jnp.where(state == 1, ratio, 0.0))
    b_s = jnp.where(state == 0, ratio, 1.0)
    co[c, 0] = jnp.where(c == 0, a_s, a_n)
    co[c, 1] = jnp.where(c == 0, b_s, b_n)
    co_send[0] = jnp.where(c == 0, a_n, a_s)
    co_send[1] = jnp.where(c == 0, b_n, b_s)
    elb[c, :8, :] = jnp.broadcast_to(el_ref[...], (8, 128))
    co_share = remote(co_send, co.at[c], sib_send.at[0], sib_recv.at[0], here)
    co_share.start()
    el_share = remote(elb.at[c, pl.ds(0, 8)], elb.at[c, pl.ds(0, 8)], sib_send.at[1], sib_recv.at[1], here)
    el_share.start()
    for d in ORDER[:5]:
        share_k(d)
    first_sends(1)
    acc[...] = jnp.zeros((2, B, 256), F32)
    wait_recv(elb.at[other, pl.ds(0, 8)], sib_recv.at[1])
    for d in ORDER[5:]:
        share_k(d)
    place = jnp.concatenate([elb[0, 0:1, :], elb[1, 0:1, :]], axis=1) - src * (NY * 2 * L)
    low[...] = jnp.where(
        lax.broadcasted_iota(jnp.int32, (L, 256), 0) == (place & (L - 1)), 1.0, 0.0).astype(BF16)
    high = place >> 8
    elb[0, 8:, :] = jnp.broadcast_to(high[:, :128], (8, 128))
    elb[1, 8:, :] = jnp.broadcast_to(high[:, 128:], (8, 128))

    relay(0)

    def add_all(it):
        if it == 0:
            arrived(it, 0, other)
        add_chip(it, 0)
        for d in (1, -1):
            arrived(it, d, 0)
            arrived(it, d, 1)
            add_chip(it, d)
        for d in (2, -2):
            add_chip(it, d)
        for d in (3, -3, 4):
            arrived(it, d, 0)
            arrived(it, d, 1)
            add_chip(it, d)

    add_all(0)
    wait_recv(co.at[other], sib_recv.at[0])
    jv = reduce_src(0)
    j0[...] = jv
    scatter_sources(0, jv)
    gp_row = row_of(jv * jv)

    pp = 0.0
    for h in range(2):
        p = own[0, h] + arrivals(0, h)
        pown[h] = p
        pp += p * p
        part = gat.at[1, y * 2 + h]
        part[...] = p.astype(BF16)
        for d in (2, -2):
            remote(part, part, ag_send.at[1], ag_recv.at[1, y * 2 + h], at_chip(d, c)).start()
    for h in range(2):
        part = gat.at[1, y * 2 + h]
        for d in (1, -1):
            remote(part, part, ag_send.at[1], ag_recv.at[1, y * 2 + h], at_chip(d, c)).start()
    remote(pown.at[other], sib.at[0], sp_send.at[0], sp_recv.at[0], here).start()
    pp_row = row_of(pp)
    share_scalars(0, jnp.concatenate(
        [gg_row, pp_row, gp_row * (1.0 / N_SRC), jnp.zeros((5, 128), F32)], axis=0))
    acc[...] = jnp.zeros((2, B, 256), F32)
    relay(1)
    add_all(1)
    jp = reduce_src(1)
    sums = sc_out[...]
    gg, pp, gp = sums[0:1], sums[1:2], sums[2:3]
    alpha0 = gg / (0.5 * gg + gp)
    left = gp / (0.5 * gg + gp)
    rr = alpha0 * (alpha0 * pp - left * gp)
    beta = rr / gg
    scale = left + beta
    alpha0_c, left_c, scale_c = col_of(alpha0), col_of(left), col_of(scale)
    jv = scale_c * j0[...] - alpha0_c * jp
    scatter_sources(1, jv, lambda: jnp.broadcast_to(row_of(jv * jv), (8, 128)))
    jj = sum_scalars(1)[0:1]
    alpha1 = rr / (0.5 * rr * (1.0 + beta) + jj)
    alpha1_c = col_of(alpha1)
    wait_recv(sib.at[0], sp_recv.at[0])
    base = []
    for comp in range(2):
        gv = g_ref[:, comp, :]
        pv = jnp.where(c == comp, pown[c], sib[0])
        direction = scale_c * gv - alpha0_c * pv
        x_ref[:, comp, :] = alpha0_c * gv + alpha1_c * direction
        base.append(left_c * gv - alpha0_c * pv - alpha1_c * (0.5 * direction))
    wait_recv(sib.at[1], sp_recv.at[1])
    for comp in range(2):
        q = jnp.where(c == comp, own[1, c], sib[1]) + arrivals(1, comp)
        r_ref[:, comp, :] = base[comp] - alpha1_c * q

    co_share.wait_send()
    el_share.wait_send()
    wait_send(kw.at[c], kp_send)
    for it in range(2):
        wait_send(gat.at[it, pl.ds(0, 15 - it)], ag_send.at[it])
        wait_send(rs_send.at[it, pl.ds(0, 14)], rs_ssem.at[it])
        wait_send(own.at[it, 0], sp_send.at[it])
        wait_send(tb.at[it, pl.ds(0, N_RCV - 1)], t_send.at[it])
        finish_src(it)


def shards(stiffness, newton_rhs, traction, opening, state, elements):
    dma, vmem = pltpu.SemaphoreType.DMA, pltpu.VMEM
    out = jax.ShapeDtypeStruct((B, 2, L), F32)
    return pl.pallas_call(
        kernel,
        out_shape=(out, out),
        in_specs=[pl.BlockSpec(memory_space=pl.ANY)] * 6,
        out_specs=[pl.BlockSpec(memory_space=pltpu.VMEM)] * 2,
        scratch_shapes=[
            vmem((B, 2, L), F32),
            vmem((B, 2, 128), F32),
            vmem((B, 128), F32),
            vmem((B, 128), jnp.int32),
            vmem((1, 128), jnp.int32),
            vmem((2, NY * 2 * L, 128), BF16),
            vmem((NY * 2 * L, 128), BF16),
            vmem((L, 256), BF16),
            vmem((2, 16, 128), jnp.int32),
            vmem((2, 2, B, 128), F32),
            vmem((2, B, 128), F32),
            vmem((2, B, L), BF16),
            vmem((2, 16, B, L), BF16),
            vmem((2, B, 256), F32),
            vmem((B, 256), F32),
            vmem((2, TILES, 16, 128), BF16),
            vmem((2, N_SRC, 16, 128), BF16),
            vmem((2, TILES, 16, 128), BF16),
            vmem((8, 128), F32),
            vmem((N_SRC, 8, 128), F32),
            vmem((8, 128), F32),
            vmem((2, 16, B, L), BF16),
            vmem((2, 6, B, L), BF16),
            vmem((2, 8, B, L), BF16),
            vmem((2, 2, B, L), F32),
            vmem((2, B, L), F32),
            vmem((2, B, L), F32),
            vmem((2, N_RCV, 8, 128), F32),
            dma((NY,)), dma((NY,)), dma((B // 8,)), dma((4,)), dma((2,)), dma((2,)), dma, dma((NY,)),
            dma((2,)), dma((2, 16)), dma((2,)), dma((2, 6)), dma((2, 8)),
            dma((2,)), dma((2,)), dma((2,)), dma((2,)), dma((2,)), dma((2,)), dma, dma, dma, dma, dma((2,)), dma((2,)),
        ],
        compiler_params=pltpu.CompilerParams(
            collective_id=0, has_side_effects=True, vmem_limit_bytes=24 * 1024 * 1024),
        cost_estimate=pl.CostEstimate(flops=8 * B * 4096 * 512, bytes_accessed=4 << 20, transcendentals=0),
    )(*(pltpu.with_memory_space_constraint(a, pltpu.HBM) for a in (
        stiffness, newton_rhs, traction, opening, state, elements.reshape(1, 128))))


def solution(mesh):
    placed = (
        P(None, "src", "rcv"),
        P(None, None, ("src", "rcv")),
        P(None, None, "rcv"),
        P(None, "rcv"),
        P(None, "rcv"),
        P("rcv"),
    )
    return jax.shard_map(
        shards,
        mesh=mesh,
        in_specs=placed,
        out_specs=(P(None, None, ("src", "rcv")), P(None, None, ("src", "rcv"))),
        check_vma=False,
    )
```

```python
import jax
import jax.numpy as jnp
from jax import lax
from jax.experimental import pallas as pl
from jax.experimental.pallas import tpu as pltpu
from jax.sharding import PartitionSpec as P

MESH = pl.DeviceIdType.MESH
F32 = jnp.float32
BF16 = jnp.bfloat16
B = 48
L = 256
NY = 8
N_RCV = 16
N_SRC = 32
TILES = 6


def away(i):
    return (i + 1) // 2 * (2 * (i % 2) - 1)


def dot_nt(a, b):
    return lax.dot_general(a, b, (((1,), (1,)), ((), ())), preferred_element_type=F32)


def kernel(k_hbm, g_hbm, tr_hbm, op_hbm, st_hbm, el_hbm, x_ref, r_ref,
           g_ref, tr_ref, op_ref, st_ref, el_ref,
           kw, k_own, low, elb, co, co_send, sb, gat, acc, j0, ar_s, ar_in, ar_out, sc_s, sc_in, sc_out,
           rs_send, rs_in, rs_fin, fresh, pown, sib, tb, rows,
           k_sem, ka_sem, g_sem, in_sem, sib_send, sib_recv, kp_send, kp_recv, ag_send, ag_recv, rs_ssem, rs_recv, rf_recv,
           sp_send, sp_recv, a1_send, a1_recv, a2_send, a2_recv,
           s1_send, s1_recv, s2_send, s2_recv, t_send, t_recv):
    src = lax.axis_index("src")
    rcv = lax.axis_index("rcv")
    y = rcv // 2
    c = lax.rem(rcv, 2)
    other = 1 - c

    def chip(d):
        return lax.rem(y + d + NY, NY)

    def at_chip(d, core):
        return (src, chip(d) * 2 + core)

    def remote(s, d, ss, rs, dev):
        return pltpu.make_async_remote_copy(
            src_ref=s, dst_ref=d, send_sem=ss, recv_sem=rs, device_id=dev, device_id_type=MESH)

    here = (src, y * 2 + other)

    def wait_recv(ref, sem):
        remote(ref, ref, sem, sem, here).wait_recv()

    def wait_send(ref, sem):
        remote(ref, ref, sem, sem, here).wait_send()

    g_loads = [
        pltpu.make_async_copy(g_hbm.at[pl.ds(8 * i, 8)], g_ref.at[pl.ds(8 * i, 8)], g_sem.at[i]) for i in range(B // 8)]
    for load in g_loads:
        load.start()
    loads = [
        pltpu.make_async_copy(a, b, in_sem.at[i])
        for i, (a, b) in enumerate((
            (tr_hbm, tr_ref), (op_hbm, op_ref), (st_hbm, st_ref), (el_hbm, el_ref)))
    ]
    for load in loads:
        load.start()

    barrier = pltpu.get_barrier_semaphore()

    def greet(dev):
        pl.semaphore_signal(barrier, inc=1, device_id=dev, device_id_type=MESH)

    def greet_rcv(d, carry):
        greet((src, lax.rem(rcv + d, N_RCV)))
        return carry

    def greet_src(d, carry):
        greet((lax.rem(src + d, N_SRC), rcv))
        return carry

    lax.fori_loop(1, N_RCV, greet_rcv, 0)
    lax.fori_loop(1, N_SRC, greet_src, 0)

    def k_rows(d):
        return pl.ds(pl.multiple_of(chip(d) * (2 * L), 2 * L), 2 * L)

    def k_away(d):
        return pltpu.make_async_copy(k_hbm.at[other, k_rows(d)], k_own.at[k_rows(d)], ka_sem.at[chip(d)])

    def k_copy(d):
        return pltpu.make_async_copy(k_hbm.at[c, k_rows(d)], kw.at[c, k_rows(d)], k_sem.at[chip(d)])

    def k_start(i, carry):
        k_away(away(i)).start()
        k_copy(away(i)).start()
        return carry

    lax.fori_loop(0, NY, k_start, 0)

    lane = lax.broadcasted_iota(jnp.int32, (B, 128), 1)
    case = lax.broadcasted_iota(jnp.int32, (B, 128), 0)
    diag = lane == case

    def row_of(v):
        col = jnp.sum(v, axis=1, keepdims=True)
        return jnp.sum(jnp.where(diag, col, 0.0), axis=0, keepdims=True)

    def col_of(row):
        return jnp.sum(jnp.where(diag, row, 0.0), axis=1, keepdims=True)

    for load in g_loads:
        load.wait()
    g0, g1 = g_ref[:, 0, :], g_ref[:, 1, :]
    b0, b1 = g0.astype(BF16), g1.astype(BF16)
    sb[0] = b0
    sb[1] = b1
    gat[0, rcv] = jnp.where(c == 0, b0, b1)
    rows[0:1, :] = row_of(g0 * g0 + g1 * g1)

    pl.semaphore_wait(barrier, N_RCV + N_SRC - 2)

    def first_sends(comp):
        for d in (2, -2, 1, -1):
            remote(sb.at[comp], gat.at[0, rcv], ag_send.at[0], ag_recv.at[0, rcv], at_chip(d, comp)).start()

    first_sends(0)
    remote(sb.at[other], gat.at[0, rcv], ag_send.at[0], ag_recv.at[0, rcv], here).start()

    def share_k(i, carry):
        d = away(i)
        k_away(d).wait()
        remote(k_own.at[k_rows(d)], kw.at[c, k_rows(d)], kp_send, kp_recv.at[chip(d)], here).start()
        return carry

    def arrived(it, d, h):
        slot = chip(d) * 2 + h
        wait_recv(gat.at[it, slot], ag_recv.at[it, slot])

    def relay(it):
        for h in range(2):
            for d in (1, -1):
                arrived(it, -2 * d, h)
                slot = chip(-2 * d) * 2 + h
                part = gat.at[it, slot]
                if (d == 1) == (h == 0):
                    remote(part, part, ag_send.at[it], ag_recv.at[it, slot], at_chip(2 * d, c)).start()
                remote(part, part, ag_send.at[it], ag_recv.at[it, slot], at_chip(d, c)).start()

    def block(q):
        rows = pl.ds(pl.multiple_of(q * (2 * L), 2 * L), 2 * L)
        return jnp.concatenate([kw[0, rows, :], kw[1, rows, :]], axis=1)

    def high_bits():
        return jnp.concatenate([elb[0, 8:9, :], elb[1, 8:9, :]], axis=1)

    def add_chips(it):
        acc[...] = jnp.zeros((2, B, 256), F32)

        def add_chip(i, carry):
            d = away(i)
            q = chip(d)

            @pl.when(it == 0)
            def _():
                k_copy(d).wait()
                wait_recv(kw.at[other, k_rows(d)], kp_recv.at[q])
                pl.when(i == 0)(lambda: arrived(0, 0, other))

            @pl.when((i >= 1) & ((i < 3) | (i > 4)))
            def _():
                arrived(it, d, 0)
                arrived(it, d, 1)

            v0, v1 = gat[it, q * 2], gat[it, q * 2 + 1]
            acc[0] += jnp.dot(jnp.concatenate([v0, v1], axis=1), block(q), preferred_element_type=F32)
            ed = jnp.dot(jnp.concatenate([v0, v1], axis=0), low[...], preferred_element_type=F32)
            high = high_bits()
            acc[1] += jnp.where(high == q * 2, ed[:B], 0.0) + jnp.where(high == q * 2 + 1, ed[B:], 0.0)
            return carry

        lax.fori_loop(0, NY, add_chip, 0)

    def coef(i):
        return jnp.concatenate([co[0, i], co[1, i]], axis=1)

    def others(send):
        def one(d, carry):
            send((lax.rem(src + d, N_SRC), rcv))
            return carry

        lax.fori_loop(1, N_SRC, one, 0)

    tile = (src - 2 * c + 5) // 5 - 1
    sums_tile = (lax.rem(src - 2 * c + 5, 5) == 0) & (tile >= 0) & (tile < TILES)
    sums_scalars = src == 30 + c

    def reduce_src(it):
        part = (coef(0) * acc[1] + coef(1) * acc[0]).astype(BF16)
        for half in range(2):
            ar_s[it, 3 * half:3 * half + 3] = part[:, 128 * half:128 * half + 128].reshape(3, 16, 128)

        def send(t, carry):
            owner = 5 * t + 2 * c

            @pl.when(owner != src)
            def _():
                remote(ar_s.at[it, t], ar_in.at[it, src], a1_send.at[it], a1_recv.at[it], (owner, rcv)).start()
            return carry

        lax.fori_loop(0, TILES, send, 0)

        @pl.when(it == 1)
        def _():
            sc_s[...] = sum_scalars(0)

            @pl.when(jnp.logical_not(sums_scalars))
            def _():
                remote(sc_s, sc_in.at[src], s1_send, s1_recv, (30 + c, rcv)).start()

            @pl.when(sums_scalars)
            def _():
                sc_in[src] = sc_s[...]
                wait_recv(sc_in.at[pl.ds(0, N_SRC - 1)], s1_recv)
                sc_out[...] = jnp.sum(sc_in[...], axis=0)
                others(lambda dev: remote(sc_out, sc_out, s2_send, s2_recv, dev).start())

        @pl.when(sums_tile)
        def _():
            ar_in[it, src] = ar_s[it, tile]
            wait_recv(ar_in.at[it, pl.ds(0, N_SRC - 1)], a1_recv.at[it])
            ar_out[it, tile] = jnp.sum(ar_in[it].astype(F32), axis=0).astype(BF16)
            part = ar_out.at[it, tile]
            others(lambda dev: remote(part, part, a2_send.at[it], a2_recv.at[it], dev).start())
            wait_recv(ar_out.at[it, pl.ds(0, TILES - 1)], a2_recv.at[it])

        @pl.when(jnp.logical_not(sums_tile))
        def _():
            wait_recv(ar_out.at[it, pl.ds(0, TILES)], a2_recv.at[it])

        pl.when((it == 1) & jnp.logical_not(sums_scalars))(lambda: wait_recv(sc_out, s2_recv))
        return jnp.concatenate(
            [ar_out[it, 3 * half:3 * half + 3].reshape(B, 128) for half in range(2)], axis=1).astype(F32)

    def finish_src(it):
        @pl.when(sums_tile)
        def _():
            wait_send(ar_in.at[it, pl.ds(0, N_SRC - 1)], a2_send.at[it])
            wait_send(ar_s.at[it, pl.ds(0, TILES - 1)], a1_send.at[it])

        @pl.when(jnp.logical_not(sums_tile))
        def _():
            wait_send(ar_s.at[it, pl.ds(0, TILES)], a1_send.at[it])

        if it == 1:
            pl.when(sums_scalars)(lambda: wait_send(sc_in.at[pl.ds(0, N_SRC - 1)], s2_send))
            pl.when(jnp.logical_not(sums_scalars))(lambda: wait_send(sc_s, s1_send))

    def share_scalars(it, tile):
        tb[it, rcv] = tile

        def send(d, carry):
            remote(tb.at[it, rcv], tb.at[it, rcv], t_send.at[it], t_recv.at[it],
                   (src, lax.rem(rcv + d, N_RCV))).start()
            return carry

        lax.fori_loop(1, N_RCV, send, 0)

    def sum_scalars(it):
        wait_recv(tb.at[it, pl.ds(0, N_RCV - 1)], t_recv.at[it])
        return jnp.sum(tb[it], axis=0)

    def scatter_sources(it, jv):
        w = (coef(1) * jv).astype(BF16)
        lift = coef(0) * jv

        def home(slot, d, h):
            landing = {1: 0, -1: 2, 2: 4, -2: 6}[d] + h + it * (c - h)
            remote(rs_send.at[it, slot], rs_fin.at[it, landing], rs_ssem.at[it], rf_recv.at[it, landing],
                   at_chip(d, c + it * (h - c))).start()

        def came(landing):
            wait_recv(rs_in.at[it, landing], rs_recv.at[it, landing])
            return rs_in[it, landing].astype(F32)

        def part(i, carry):
            q = chip(away(lax.rem(i + 5, NY)))
            high = high_bits()
            both = dot_nt(w, block(q))
            sparse = jnp.concatenate(
                [jnp.where(high == q * 2, lift, 0.0), jnp.where(high == q * 2 + 1, lift, 0.0)], axis=0)
            spread = dot_nt(sparse.astype(BF16), low[...])
            for h in range(2):
                value = both[:, h * L:h * L + L] + spread[h * B:h * B + B]
                fresh[i, h] = value
                rs_send[it, 2 * i + h] = value.astype(BF16)

            def onward(h, to, landing):
                remote(rs_send.at[it, 2 * i + h], rs_in.at[it, landing], rs_ssem.at[it], rs_recv.at[it, landing],
                       at_chip(to, c)).start()

            for at, d in ((0, 1), (1, -1)):
                @pl.when(i == at)
                def _():
                    onward(0, d, 2 + 2 * at)
                    onward(1, d, 3 + 2 * at)

                @pl.when(i == 4 + at)
                def _():
                    home(8 + 2 * at, d, 0)
                    home(9 + 2 * at, d, 1)

            @pl.when(i == 2)
            def _():
                onward(0, 2, 0)
                onward(1, -2, 1)

            @pl.when((i == 3) & (it == 1))
            def _():
                remote(fresh.at[3, other], sib.at[1], sp_send.at[1], sp_recv.at[1], here).start()
            return carry

        lax.fori_loop(0, NY, part, 0)

        @pl.when(it == 1)
        def _():
            share_scalars(1, jnp.broadcast_to(row_of(jv * jv), (8, 128)))

        for d, h, relays in ((2, 1, (3,)), (-2, 0, (4,)), (2, 0, (2, 0)), (-2, 1, (5, 1))):
            at = 6 if d == 2 else 7
            value = fresh[at, h]
            for landing in relays:
                value += came(landing)
            rs_send[it, 2 * at + h] = value.astype(BF16)
            home(2 * at + h, d, h)

    def arrivals(it, i):
        total = 0.0
        for way in range(4):
            slot = way * 2 + i
            wait_recv(rs_fin.at[it, slot], rf_recv.at[it, slot])
            total += rs_fin[it, slot].astype(F32)
        return total

    for load in loads:
        load.wait()
    tau, press = tr_ref[:, 0, :], tr_ref[:, 1, :]
    opening, state = op_ref[...], st_ref[...]
    radius = jnp.sqrt(opening * opening + press * press + 0.5)
    a_n = 1.0 - opening / radius
    b_n = 1.0 - press / radius
    ratio = jnp.abs(tau) / (1.0 + 0.6 * jnp.abs(press))
    a_s = jnp.where(state == 0, 1.0, jnp.where(state == 1, ratio, 0.0))
    b_s = jnp.where(state == 0, ratio, 1.0)
    co[c, 0] = jnp.where(c == 0, a_s, a_n)
    co[c, 1] = jnp.where(c == 0, b_s, b_n)
    co_send[0] = jnp.where(c == 0, a_n, a_s)
    co_send[1] = jnp.where(c == 0, b_n, b_s)
    elb[c, :8, :] = jnp.broadcast_to(el_ref[...], (8, 128))
    co_share = remote(co_send, co.at[c], sib_send.at[0], sib_recv.at[0], here)
    co_share.start()
    el_share = remote(elb.at[c, pl.ds(0, 8)], elb.at[c, pl.ds(0, 8)], sib_send.at[1], sib_recv.at[1], here)
    el_share.start()
    lax.fori_loop(0, 5, share_k, 0)
    first_sends(1)
    wait_recv(elb.at[other, pl.ds(0, 8)], sib_recv.at[1])
    lax.fori_loop(5, NY, share_k, 0)
    place = jnp.concatenate([elb[0, 0:1, :], elb[1, 0:1, :]], axis=1) - src * (NY * 2 * L)
    low[...] = jnp.where(
        lax.broadcasted_iota(jnp.int32, (L, 256), 0) == (place & (L - 1)), 1.0, 0.0).astype(BF16)
    high = place >> 8
    elb[0, 8:, :] = jnp.broadcast_to(high[:, :128], (8, 128))
    elb[1, 8:, :] = jnp.broadcast_to(high[:, 128:], (8, 128))

    j0[...] = jnp.zeros((B, 256), F32)
    sc_out[...] = jnp.zeros((8, 128), F32)

    def scalars():
        gg, pp, gp = sc_out[0:1, :], sc_out[1:2, :], sc_out[2:3, :]
        alpha0 = gg / (0.5 * gg + gp)
        left = gp / (0.5 * gg + gp)
        rr = alpha0 * (alpha0 * pp - left * gp)
        return alpha0, left, rr, rr / gg

    def apply(it, carry):
        relay(it)
        add_chips(it)
        pl.when(it == 0)(lambda: wait_recv(co.at[other], sib_recv.at[0]))
        image = reduce_src(it)
        alpha0, left, rr, beta = scalars()
        jv = jnp.where(it == 0, image, col_of(left + beta) * j0[...] - col_of(alpha0) * image)
        j0[...] = jv
        scatter_sources(it, jv)

        @pl.when(it == 0)
        def _():
            pp = 0.0
            for h in range(2):
                p = fresh[3, h] + arrivals(0, h)
                pown[h] = p
                pp += p * p
                part = gat.at[1, y * 2 + h]
                part[...] = p.astype(BF16)
                for d in (2, -2):
                    remote(part, part, ag_send.at[1], ag_recv.at[1, y * 2 + h], at_chip(d, c)).start()
            for h in range(2):
                part = gat.at[1, y * 2 + h]
                for d in (1, -1):
                    remote(part, part, ag_send.at[1], ag_recv.at[1, y * 2 + h], at_chip(d, c)).start()
            remote(pown.at[other], sib.at[0], sp_send.at[0], sp_recv.at[0], here).start()
            share_scalars(0, jnp.concatenate(
                [rows[0:1, :], row_of(pp), row_of(jv * jv) * (1.0 / N_SRC), jnp.zeros((5, 128), F32)], axis=0))
        return carry

    lax.fori_loop(0, 2, apply, 0)
    alpha0, left, rr, beta = scalars()
    alpha0_c, left_c, scale_c = col_of(alpha0), col_of(left), col_of(left + beta)
    jj = sum_scalars(1)[0:1]
    alpha1_c = col_of(rr / (0.5 * rr * (1.0 + beta) + jj))
    wait_recv(sib.at[0], sp_recv.at[0])
    base = []
    for comp in range(2):
        gv = g_ref[:, comp, :]
        pv = jnp.where(c == comp, pown[c], sib[0])
        direction = scale_c * gv - alpha0_c * pv
        x_ref[:, comp, :] = alpha0_c * gv + alpha1_c * direction
        base.append(left_c * gv - alpha0_c * pv - alpha1_c * (0.5 * direction))
    wait_recv(sib.at[1], sp_recv.at[1])
    for comp in range(2):
        q = jnp.where(c == comp, fresh[3, c], sib[1]) + arrivals(1, comp)
        r_ref[:, comp, :] = base[comp] - alpha1_c * q

    co_share.wait_send()
    el_share.wait_send()
    wait_send(kw.at[c], kp_send)
    for it in range(2):
        wait_send(gat.at[it, pl.ds(0, 15 - it)], ag_send.at[it])
        wait_send(rs_send.at[it, pl.ds(0, 14)], rs_ssem.at[it])
        wait_send(sib.at[it], sp_send.at[it])
        wait_send(tb.at[it, pl.ds(0, N_RCV - 1)], t_send.at[it])
        finish_src(it)


def shards(stiffness, newton_rhs, traction, opening, state, elements):
    dma, vmem = pltpu.SemaphoreType.DMA, pltpu.VMEM
    out = jax.ShapeDtypeStruct((B, 2, L), F32)
    return pl.pallas_call(
        kernel,
        out_shape=(out, out),
        in_specs=[pl.BlockSpec(memory_space=pl.ANY)] * 6,
        out_specs=[pl.BlockSpec(memory_space=pltpu.VMEM)] * 2,
        scratch_shapes=[
            vmem((B, 2, L), F32),
            vmem((B, 2, 128), F32),
            vmem((B, 128), F32),
            vmem((B, 128), jnp.int32),
            vmem((1, 128), jnp.int32),
            vmem((2, NY * 2 * L, 128), BF16),
            vmem((NY * 2 * L, 128), BF16),
            vmem((L, 256), BF16),
            vmem((2, 16, 128), jnp.int32),
            vmem((2, 2, B, 128), F32),
            vmem((2, B, 128), F32),
            vmem((2, B, L), BF16),
            vmem((2, 16, B, L), BF16),
            vmem((2, B, 256), F32),
            vmem((B, 256), F32),
            vmem((2, TILES, 16, 128), BF16),
            vmem((2, N_SRC, 16, 128), BF16),
            vmem((2, TILES, 16, 128), BF16),
            vmem((8, 128), F32),
            vmem((N_SRC, 8, 128), F32),
            vmem((8, 128), F32),
            vmem((2, 16, B, L), BF16),
            vmem((2, 6, B, L), BF16),
            vmem((2, 8, B, L), BF16),
            vmem((NY, 2, B, L), F32),
            vmem((2, B, L), F32),
            vmem((2, B, L), F32),
            vmem((2, N_RCV, 8, 128), F32),
            vmem((8, 128), F32),
            dma((NY,)), dma((NY,)), dma((B // 8,)), dma((4,)), dma((2,)), dma((2,)), dma, dma((NY,)),
            dma((2,)), dma((2, 16)), dma((2,)), dma((2, 6)), dma((2, 8)),
            dma((2,)), dma((2,)), dma((2,)), dma((2,)), dma((2,)), dma((2,)), dma, dma, dma, dma, dma((2,)), dma((2,)),
        ],
        compiler_params=pltpu.CompilerParams(
            collective_id=0, has_side_effects=True, vmem_limit_bytes=24 * 1024 * 1024),
        cost_estimate=pl.CostEstimate(flops=8 * B * 4096 * 512, bytes_accessed=4 << 20, transcendentals=0),
    )(*(pltpu.with_memory_space_constraint(a, pltpu.HBM) for a in (
        stiffness, newton_rhs, traction, opening, state, elements.reshape(1, 128))))


def solution(mesh):
    placed = (
        P(None, "src", "rcv"),
        P(None, None, ("src", "rcv")),
        P(None, None, "rcv"),
        P(None, "rcv"),
        P(None, "rcv"),
        P("rcv"),
    )
    return jax.shard_map(
        shards,
        mesh=mesh,
        in_specs=placed,
        out_specs=(P(None, None, ("src", "rcv")), P(None, None, ("src", "rcv"))),
        check_vma=False,
    )
```

```python
import jax
import jax.numpy as jnp
from jax import lax
from jax.experimental import pallas as pl
from jax.experimental.pallas import tpu as pltpu
from jax.sharding import PartitionSpec as P

MESH = pl.DeviceIdType.MESH
F32 = jnp.float32
BF16 = jnp.bfloat16
B = 48
L = 256
NY = 8
N_RCV = 16
N_SRC = 32
TILES = 6
ORDER = (0, 1, -1, 2, -2, 3, -3, 4)


def dot_nt(a, b):
    return lax.dot_general(a, b, (((1,), (1,)), ((), ())), preferred_element_type=F32)


def kernel(k_hbm, g_hbm, tr_hbm, op_hbm, st_hbm, el_hbm, x_ref, r_ref,
           g_ref, tr_ref, op_ref, st_ref, el_ref,
           kw, k_own, low, elb, co, co_send, sb, gat, acc, j0, ar_s, ar_in, ar_out, sc_s, sc_in, sc_out,
           rs_send, rs_in, rs_fin, own, pown, sib, tb0, tb1,
           k_sem, ka_sem, g_sem, in_sem, sib_send, sib_recv, kp_send, kp_recv, ag_send, ag_recv, rs_ssem, rs_recv, rf_recv,
           sp_send, sp_recv, a1_send, a1_recv, a2_send, a2_recv,
           s1_send, s1_recv, s2_send, s2_recv, t_send, t_recv):
    src = lax.axis_index("src")
    rcv = lax.axis_index("rcv")
    y = rcv // 2
    c = lax.rem(rcv, 2)
    other = 1 - c

    def chip(d):
        return lax.rem(y + d + NY, NY)

    def at_chip(d, core):
        return (src, chip(d) * 2 + core)

    def remote(s, d, ss, rs, dev):
        return pltpu.make_async_remote_copy(
            src_ref=s, dst_ref=d, send_sem=ss, recv_sem=rs, device_id=dev, device_id_type=MESH)

    here = (src, y * 2 + other)

    def wait_recv(ref, sem):
        remote(ref, ref, sem, sem, here).wait_recv()

    def wait_send(ref, sem):
        remote(ref, ref, sem, sem, here).wait_send()

    g_loads = [
        pltpu.make_async_copy(g_hbm.at[pl.ds(8 * i, 8)], g_ref.at[pl.ds(8 * i, 8)], g_sem.at[i]) for i in range(B // 8)]
    for load in g_loads:
        load.start()
    loads = [
        pltpu.make_async_copy(a, b, in_sem.at[i])
        for i, (a, b) in enumerate((
            (tr_hbm, tr_ref), (op_hbm, op_ref), (st_hbm, st_ref), (el_hbm, el_ref)))
    ]
    for load in loads:
        load.start()

    barrier = pltpu.get_barrier_semaphore()

    def greet(dev):
        pl.semaphore_signal(barrier, inc=1, device_id=dev, device_id_type=MESH)

    def greet_rcv(d, carry):
        greet((src, lax.rem(rcv + d, N_RCV)))
        return carry

    def greet_src(d, carry):
        greet((lax.rem(src + d, N_SRC), rcv))
        return carry

    lax.fori_loop(1, N_RCV, greet_rcv, 0)
    lax.fori_loop(1, N_SRC, greet_src, 0)

    def k_rows(d):
        return pl.ds(pl.multiple_of(chip(d) * (2 * L), 2 * L), 2 * L)

    def k_away(d):
        return pltpu.make_async_copy(k_hbm.at[other, k_rows(d)], k_own.at[k_rows(d)], ka_sem.at[chip(d)])

    def k_copy(d):
        return pltpu.make_async_copy(k_hbm.at[c, k_rows(d)], kw.at[c, k_rows(d)], k_sem.at[chip(d)])

    for d in ORDER:
        k_away(d).start()
        k_copy(d).start()

    lane = lax.broadcasted_iota(jnp.int32, (B, 128), 1)
    case = lax.broadcasted_iota(jnp.int32, (B, 128), 0)
    diag = lane == case

    def row_of(v):
        col = jnp.sum(v, axis=1, keepdims=True)
        return jnp.sum(jnp.where(diag, col, 0.0), axis=0, keepdims=True)

    def col_of(row):
        return jnp.sum(jnp.where(diag, row, 0.0), axis=1, keepdims=True)

    for load in g_loads:
        load.wait()
    g0, g1 = g_ref[:, 0, :], g_ref[:, 1, :]
    b0, b1 = g0.astype(BF16), g1.astype(BF16)
    sb[0] = b0
    sb[1] = b1
    gat[0, rcv] = jnp.where(c == 0, b0, b1)
    gg_row = row_of(g0 * g0 + g1 * g1)

    pl.semaphore_wait(barrier, N_RCV + N_SRC - 2)

    def first_sends(comp):
        for d in (2, -2, 1, -1):
            remote(sb.at[comp], gat.at[0, rcv], ag_send.at[0], ag_recv.at[0, rcv], at_chip(d, comp)).start()

        @pl.when(c != comp)
        def _():
            remote(sb.at[comp], gat.at[0, rcv], ag_send.at[0], ag_recv.at[0, rcv], here).start()

    first_sends(0)

    def share_k(d):
        k_away(d).wait()
        remote(k_own.at[k_rows(d)], kw.at[c, k_rows(d)], kp_send, kp_recv.at[chip(d)], here).start()

    def arrived(it, d, h):
        slot = chip(d) * 2 + h
        wait_recv(gat.at[it, slot], ag_recv.at[it, slot])

    def relay(it):
        for h in range(2):
            for d in (1, -1):
                arrived(it, -2 * d, h)
                slot = chip(-2 * d) * 2 + h
                part = gat.at[it, slot]
                if (d == 1) == (h == 0):
                    remote(part, part, ag_send.at[it], ag_recv.at[it, slot], at_chip(2 * d, c)).start()
                remote(part, part, ag_send.at[it], ag_recv.at[it, slot], at_chip(d, c)).start()

    def block(q):
        rows = pl.ds(pl.multiple_of(q * (2 * L), 2 * L), 2 * L)
        return jnp.concatenate([kw[0, rows, :], kw[1, rows, :]], axis=1)

    def add_chip(it, d):
        q = chip(d)
        if it == 0:
            k_copy(d).wait()
            wait_recv(kw.at[other, k_rows(d)], kp_recv.at[q])
        v0, v1 = gat[it, q * 2], gat[it, q * 2 + 1]
        acc[0] += jnp.dot(jnp.concatenate([v0, v1], axis=1), block(q), preferred_element_type=F32)
        ed = jnp.dot(jnp.concatenate([v0, v1], axis=0), low[...], preferred_element_type=F32)
        high = elb[:, 8:9, :]
        high = jnp.concatenate([high[0], high[1]], axis=1)
        acc[1] += jnp.where(high == q * 2, ed[:B], 0.0) + jnp.where(high == q * 2 + 1, ed[B:], 0.0)

    def coef(i):
        return jnp.concatenate([co[0, i], co[1, i]], axis=1)

    def others(send):
        def one(d, carry):
            send((lax.rem(src + d, N_SRC), rcv))
            return carry

        lax.fori_loop(1, N_SRC, one, 0)

    tile = (src - 2 * c + 5) // 5 - 1
    sums_tile = (lax.rem(src - 2 * c + 5, 5) == 0) & (tile >= 0) & (tile < TILES)
    sums_scalars = src == 30 + c

    def reduce_src(it):
        part = (coef(0) * acc[1] + coef(1) * acc[0]).astype(BF16)
        for half in range(2):
            ar_s[it, 3 * half:3 * half + 3] = part[:, 128 * half:128 * half + 128].reshape(3, 16, 128)

        def send(t, carry):
            owner = 5 * t + 2 * c

            @pl.when(owner != src)
            def _():
                remote(ar_s.at[it, t], ar_in.at[it, src], a1_send.at[it], a1_recv.at[it], (owner, rcv)).start()
            return carry

        lax.fori_loop(0, TILES, send, 0)
        if it == 1:
            sc_s[...] = sum_scalars(0)

            @pl.when(jnp.logical_not(sums_scalars))
            def _():
                remote(sc_s, sc_in.at[src], s1_send, s1_recv, (30 + c, rcv)).start()

            @pl.when(sums_scalars)
            def _():
                sc_in[src] = sc_s[...]
                wait_recv(sc_in.at[pl.ds(0, N_SRC - 1)], s1_recv)
                sc_out[...] = jnp.sum(sc_in[...], axis=0)
                others(lambda dev: remote(sc_out, sc_out, s2_send, s2_recv, dev).start())

        @pl.when(sums_tile)
        def _():
            ar_in[it, src] = ar_s[it, tile]
            wait_recv(ar_in.at[it, pl.ds(0, N_SRC - 1)], a1_recv.at[it])
            ar_out[it, tile] = jnp.sum(ar_in[it].astype(F32), axis=0).astype(BF16)
            part = ar_out.at[it, tile]
            others(lambda dev: remote(part, part, a2_send.at[it], a2_recv.at[it], dev).start())
            wait_recv(ar_out.at[it, pl.ds(0, TILES - 1)], a2_recv.at[it])

        @pl.when(jnp.logical_not(sums_tile))
        def _():
            wait_recv(ar_out.at[it, pl.ds(0, TILES)], a2_recv.at[it])

        if it == 1:
            pl.when(jnp.logical_not(sums_scalars))(lambda: wait_recv(sc_out, s2_recv))
        return jnp.concatenate(
            [ar_out[it, 3 * half:3 * half + 3].reshape(B, 128) for half in range(2)], axis=1).astype(F32)

    def finish_src(it):
        @pl.when(sums_tile)
        def _():
            wait_send(ar_in.at[it, pl.ds(0, N_SRC - 1)], a2_send.at[it])
            wait_send(ar_s.at[it, pl.ds(0, TILES - 1)], a1_send.at[it])

        @pl.when(jnp.logical_not(sums_tile))
        def _():
            wait_send(ar_s.at[it, pl.ds(0, TILES)], a1_send.at[it])

        if it == 1:
            pl.when(sums_scalars)(lambda: wait_send(sc_in.at[pl.ds(0, N_SRC - 1)], s2_send))
            pl.when(jnp.logical_not(sums_scalars))(lambda: wait_send(sc_s, s1_send))

    def share_scalars(it, row):
        tb = (tb0, tb1)[it]
        tb[rcv] = row

        def send(d, carry):
            remote(tb.at[rcv], tb.at[rcv], t_send.at[it], t_recv.at[it], (src, lax.rem(rcv + d, N_RCV))).start()
            return carry

        lax.fori_loop(1, N_RCV, send, 0)

    def sum_scalars(it):
        tb = (tb0, tb1)[it]
        wait_recv(tb.at[pl.ds(0, N_RCV - 1)], t_recv.at[it])
        return jnp.sum(tb[...], axis=0)

    def scatter_sources(it, jv, scalars=None):
        w = (coef(1) * jv).astype(BF16)
        lift = coef(0) * jv
        high = jnp.concatenate([elb[0, 8:9, :], elb[1, 8:9, :]], axis=1)

        def part(d):
            q = chip(d)
            both = dot_nt(w, block(q))
            sparse = jnp.concatenate(
                [jnp.where(high == q * 2, lift, 0.0), jnp.where(high == q * 2 + 1, lift, 0.0)], axis=0)
            spread = dot_nt(sparse.astype(BF16), low[...])
            return both[:, :L] + spread[:B], both[:, L:] + spread[B:]

        def send(slot, value, to, landing):
            rs_send[it, slot] = value.astype(BF16)
            remote(rs_send.at[it, slot], rs_in.at[it, landing], rs_ssem.at[it], rs_recv.at[it, landing],
                   at_chip(to, c)).start()

        def home(slot, value, d, h):
            rs_send[it, slot] = value.astype(BF16)
            landing = {1: 0, -1: 2, 2: 4, -2: 6}[d] + (h if it == 0 else c)
            remote(rs_send.at[it, slot], rs_fin.at[it, landing], rs_ssem.at[it], rf_recv.at[it, landing],
                   at_chip(d, c if it == 0 else h)).start()

        def came(landing):
            wait_recv(rs_in.at[it, landing], rs_recv.at[it, landing])
            return rs_in[it, landing].astype(F32)

        for k, d in enumerate((1, -1)):
            far = part(3 * d)
            send(2 + 2 * k, far[0], d, 2 + 2 * k)
            send(3 + 2 * k, far[1], d, 3 + 2 * k)
        far = part(4)
        send(0, far[0], 2, 0)
        send(1, far[1], -2, 1)
        for k, d in enumerate((1, -1)):
            near = part(d)
            home(6 + 2 * k, near[0], d, 0)
            home(7 + 2 * k, near[1], d, 1)
        if scalars is not None:
            share_scalars(it, scalars())
        up, down, mine = part(2), part(-2), part(0)
        own[it, 0] = mine[0]
        own[it, 1] = mine[1]
        if it == 1:
            remote(own.at[it, other], sib.at[it], sp_send.at[it], sp_recv.at[it], here).start()
        home(10, up[1] + came(3), 2, 1)
        home(11, down[0] + came(4), -2, 0)
        home(12, up[0] + came(2) + came(0), 2, 0)
        home(13, down[1] + came(5) + came(1), -2, 1)

    def arrivals(it, i):
        total = 0.0
        for way in range(4):
            slot = way * 2 + i
            wait_recv(rs_fin.at[it, slot], rf_recv.at[it, slot])
            total += rs_fin[it, slot].astype(F32)
        return total

    for load in loads:
        load.wait()
    tau, press = tr_ref[:, 0, :], tr_ref[:, 1, :]
    opening, state = op_ref[...], st_ref[...]
    radius = jnp.sqrt(opening * opening + press * press + 0.5)
    a_n = 1.0 - opening / radius
    b_n = 1.0 - press / radius
    ratio = jnp.abs(tau) / (1.0 + 0.6 * jnp.abs(press))
    a_s = jnp.where(state == 0, 1.0, jnp.where(state == 1, ratio, 0.0))
    b_s = jnp.where(state == 0, ratio, 1.0)
    co[c, 0] = jnp.where(c == 0, a_s, a_n)
    co[c, 1] = jnp.where(c == 0, b_s, b_n)
    co_send[0] = jnp.where(c == 0, a_n, a_s)
    co_send[1] = jnp.where(c == 0, b_n, b_s)
    elb[c, :8, :] = jnp.broadcast_to(el_ref[...], (8, 128))
    co_share = remote(co_send, co.at[c], sib_send.at[0], sib_recv.at[0], here)
    co_share.start()
    el_share = remote(elb.at[c, pl.ds(0, 8)], elb.at[c, pl.ds(0, 8)], sib_send.at[1], sib_recv.at[1], here)
    el_share.start()
    for d in ORDER[:5]:
        share_k(d)
    acc[...] = jnp.zeros((2, B, 256), F32)
    wait_recv(elb.at[other, pl.ds(0, 8)], sib_recv.at[1])
    for d in ORDER[5:]:
        share_k(d)
    place = jnp.concatenate([elb[0, 0:1, :], elb[1, 0:1, :]], axis=1) - src * (NY * 2 * L)
    low[...] = jnp.where(
        lax.broadcasted_iota(jnp.int32, (L, 256), 0) == (place & (L - 1)), 1.0, 0.0).astype(BF16)
    high = place >> 8
    elb[0, 8:, :] = jnp.broadcast_to(high[:, :128], (8, 128))
    elb[1, 8:, :] = jnp.broadcast_to(high[:, 128:], (8, 128))

    @pl.when(c == 0)
    def _():
        relay(0)
        first_sends(1)

    @pl.when(c == 1)
    def _():
        arrived(0, 0, 0)
        first_sends(1)
        relay(0)

    def add_all(it):
        if it == 0:
            pl.when(c == 0)(lambda: arrived(0, 0, 1))
        add_chip(it, 0)
        for d in (1, -1):
            arrived(it, d, 0)
            arrived(it, d, 1)
            add_chip(it, d)
        for d in (2, -2):
            add_chip(it, d)
        for d in (3, -3, 4):
            arrived(it, d, 0)
            arrived(it, d, 1)
            add_chip(it, d)

    add_all(0)
    wait_recv(co.at[other], sib_recv.at[0])
    jv = reduce_src(0)
    j0[...] = jv
    scatter_sources(0, jv)
    gp_row = row_of(jv * jv)

    pp = 0.0
    for h in range(2):
        p = own[0, h] + arrivals(0, h)
        pown[h] = p
        pp += p * p
        part = gat.at[1, y * 2 + h]
        part[...] = p.astype(BF16)
        for d in (2, -2):
            remote(part, part, ag_send.at[1], ag_recv.at[1, y * 2 + h], at_chip(d, c)).start()
    for h in range(2):
        part = gat.at[1, y * 2 + h]
        for d in (1, -1):
            remote(part, part, ag_send.at[1], ag_recv.at[1, y * 2 + h], at_chip(d, c)).start()
    remote(pown.at[other], sib.at[0], sp_send.at[0], sp_recv.at[0], here).start()
    pp_row = row_of(pp)
    share_scalars(0, jnp.concatenate([gg_row, pp_row, gp_row * (1.0 / N_SRC)], axis=1))
    acc[...] = jnp.zeros((2, B, 256), F32)
    relay(1)
    add_all(1)
    jp = reduce_src(1)
    sums = sc_out[...]
    gg, pp, gp = sums[:, :128], sums[:, 128:256], sums[:, 256:]
    alpha0 = gg / (0.5 * gg + gp)
    left = gp / (0.5 * gg + gp)
    rr = alpha0 * (alpha0 * pp - left * gp)
    beta = rr / gg
    scale = left + beta
    alpha0_c, left_c, scale_c = col_of(alpha0), col_of(left), col_of(scale)
    jv = scale_c * j0[...] - alpha0_c * jp
    scatter_sources(1, jv, lambda: row_of(jv * jv))
    jj = sum_scalars(1)
    alpha1 = rr / (0.5 * rr * (1.0 + beta) + jj)
    alpha1_c = col_of(alpha1)
    wait_recv(sib.at[0], sp_recv.at[0])
    base = []
    for comp in range(2):
        gv = g_ref[:, comp, :]
        pv = jnp.where(c == comp, pown[c], sib[0])
        direction = scale_c * gv - alpha0_c * pv
        x_ref[:, comp, :] = alpha0_c * gv + alpha1_c * direction
        base.append(left_c * gv - alpha0_c * pv - alpha1_c * (0.5 * direction))
    wait_recv(sib.at[1], sp_recv.at[1])
    for comp in range(2):
        q = jnp.where(c == comp, own[1, c], sib[1]) + arrivals(1, comp)
        r_ref[:, comp, :] = base[comp] - alpha1_c * q

    co_share.wait_send()
    el_share.wait_send()
    wait_send(kw.at[c], kp_send)
    for it in range(2):
        wait_send(gat.at[it, pl.ds(0, 15 - it)], ag_send.at[it])
        wait_send(rs_send.at[it, pl.ds(0, 14)], rs_ssem.at[it])
        wait_send(own.at[it, 0], sp_send.at[it])
        wait_send((tb0, tb1)[it].at[pl.ds(0, N_RCV - 1)], t_send.at[it])
        finish_src(it)


def shards(stiffness, newton_rhs, traction, opening, state, elements):
    dma, vmem = pltpu.SemaphoreType.DMA, pltpu.VMEM
    out = jax.ShapeDtypeStruct((B, 2, L), F32)
    return pl.pallas_call(
        kernel,
        out_shape=(out, out),
        in_specs=[pl.BlockSpec(memory_space=pl.ANY)] * 6,
        out_specs=[pl.BlockSpec(memory_space=pltpu.VMEM)] * 2,
        scratch_shapes=[
            vmem((B, 2, L), F32),
            vmem((B, 2, 128), F32),
            vmem((B, 128), F32),
            vmem((B, 128), jnp.int32),
            vmem((1, 128), jnp.int32),
            vmem((2, NY * 2 * L, 128), BF16),
            vmem((NY * 2 * L, 128), BF16),
            vmem((L, 256), BF16),
            vmem((2, 16, 128), jnp.int32),
            vmem((2, 2, B, 128), F32),
            vmem((2, B, 128), F32),
            vmem((2, B, L), BF16),
            vmem((2, 16, B, L), BF16),
            vmem((2, B, 256), F32),
            vmem((B, 256), F32),
            vmem((2, TILES, 16, 128), BF16),
            vmem((2, N_SRC, 16, 128), BF16),
            vmem((2, TILES, 16, 128), BF16),
            vmem((1, 384), F32),
            vmem((N_SRC, 1, 384), F32),
            vmem((1, 384), F32),
            vmem((2, 16, B, L), BF16),
            vmem((2, 6, B, L), BF16),
            vmem((2, 8, B, L), BF16),
            vmem((2, 2, B, L), F32),
            vmem((2, B, L), F32),
            vmem((2, B, L), F32),
            vmem((N_RCV, 1, 384), F32),
            vmem((N_RCV, 1, 128), F32),
            dma((NY,)), dma((NY,)), dma((B // 8,)), dma((4,)), dma((2,)), dma((2,)), dma, dma((NY,)),
            dma((2,)), dma((2, 16)), dma((2,)), dma((2, 6)), dma((2, 8)),
            dma((2,)), dma((2,)), dma((2,)), dma((2,)), dma((2,)), dma((2,)), dma, dma, dma, dma, dma((2,)), dma((2,)),
        ],
        compiler_params=pltpu.CompilerParams(
            collective_id=0, has_side_effects=True, vmem_limit_bytes=24 * 1024 * 1024),
        cost_estimate=pl.CostEstimate(flops=8 * B * 4096 * 512, bytes_accessed=4 << 20, transcendentals=0),
    )(*(pltpu.with_memory_space_constraint(a, pltpu.HBM) for a in (
        stiffness, newton_rhs, traction, opening, state, elements.reshape(1, 128))))


def solution(mesh):
    placed = (
        P(None, "src", "rcv"),
        P(None, None, ("src", "rcv")),
        P(None, None, "rcv"),
        P(None, "rcv"),
        P(None, "rcv"),
        P("rcv"),
    )
    return jax.shard_map(
        shards,
        mesh=mesh,
        in_specs=placed,
        out_specs=(P(None, None, ("src", "rcv")), P(None, None, ("src", "rcv"))),
        check_vma=False,
    )
```

```python
import jax
import jax.numpy as jnp
from jax import lax
from jax.experimental import pallas as pl
from jax.experimental.pallas import tpu as pltpu
from jax.sharding import PartitionSpec as P

MESH = pl.DeviceIdType.MESH
F32 = jnp.float32
BF16 = jnp.bfloat16
B = 48
L = 256
NY = 8
N_RCV = 16
N_SRC = 32
TILES = 6
ORDER = (0, 1, -1, 2, -2, 3, -3, 4)


def dot_nt(a, b):
    return lax.dot_general(a, b, (((1,), (1,)), ((), ())), preferred_element_type=F32)


def kernel(k_hbm, g_hbm, tr_hbm, op_hbm, st_hbm, el_hbm, x_ref, r_ref,
           g_ref, tr_ref, op_ref, st_ref, el_ref,
           kw, k_own, low, elb, co, co_send, sb, gat, acc, j0, ar_s, ar_in, ar_out, sc_s, sc_in, sc_out,
           rs_send, rs_in, rs_fin, own, pown, sib, tf0, tf1, ts0, ts1, tb0, tb1,
           k_sem, g_sem, in_sem, sib_send, sib_recv, kp_send, kp_recv, ag_send, ag_recv, rs_ssem, rs_recv, rf_recv,
           sp_send, sp_recv, a1_send, a1_recv, a2_send, a2_recv,
           s1_send, s1_recv, s2_send, s2_recv, t_send, t_recv, tc_send, tc_recv):
    src = lax.axis_index("src")
    rcv = lax.axis_index("rcv")
    y = rcv // 2
    c = lax.rem(rcv, 2)
    other = 1 - c

    def chip(d):
        return lax.rem(y + d + NY, NY)

    def at_chip(d, core):
        return (src, chip(d) * 2 + core)

    def remote(s, d, ss, rs, dev):
        return pltpu.make_async_remote_copy(
            src_ref=s, dst_ref=d, send_sem=ss, recv_sem=rs, device_id=dev, device_id_type=MESH)

    here = (src, y * 2 + other)

    def wait_recv(ref, sem):
        remote(ref, ref, sem, sem, here).wait_recv()

    def wait_send(ref, sem):
        remote(ref, ref, sem, sem, here).wait_send()

    g_loads = [
        pltpu.make_async_copy(g_hbm.at[pl.ds(24 * i, 24)], g_ref.at[pl.ds(24 * i, 24)], g_sem.at[i]) for i in range(2)]
    for load in g_loads:
        load.start()
    loads = [
        pltpu.make_async_copy(a, b, in_sem.at[i])
        for i, (a, b) in enumerate((
            (tr_hbm, tr_ref), (op_hbm, op_ref), (st_hbm, st_ref), (el_hbm, el_ref)))
    ]
    for load in loads:
        load.start()

    barrier = pltpu.get_barrier_semaphore()

    def greet(dev):
        pl.semaphore_signal(barrier, inc=1, device_id=dev, device_id_type=MESH)

    def greet_rcv(d, carry):
        greet((src, lax.rem(rcv + d, N_RCV)))
        return carry

    def greet_src(d, carry):
        greet((lax.rem(src + d, N_SRC), rcv))
        return carry

    lax.fori_loop(1, N_RCV, greet_rcv, 0)
    lax.fori_loop(1, N_SRC, greet_src, 0)

    def k_rows(d):
        return pl.ds(pl.multiple_of(chip(d) * (2 * L), 2 * L), 2 * L)

    k_away = pltpu.make_async_copy(k_hbm.at[other], k_own, k_sem.at[0])
    k_copy = pltpu.make_async_copy(k_hbm.at[c], kw.at[c], k_sem.at[1])
    k_away.start()
    k_copy.start()

    lane = lax.broadcasted_iota(jnp.int32, (B, 128), 1)
    case = lax.broadcasted_iota(jnp.int32, (B, 128), 0)
    diag = lane == case

    def row_of(v):
        col = jnp.sum(v, axis=1, keepdims=True)
        return jnp.sum(jnp.where(diag, col, 0.0), axis=0, keepdims=True)

    def col_of(row):
        return jnp.sum(jnp.where(diag, row, 0.0), axis=1, keepdims=True)

    for load in g_loads:
        load.wait()
    g0, g1 = g_ref[:, 0, :], g_ref[:, 1, :]
    b0, b1 = g0.astype(BF16), g1.astype(BF16)
    sb[0] = b0
    sb[1] = b1
    gat[0, rcv] = jnp.where(c == 0, b0, b1)
    gg_row = row_of(g0 * g0 + g1 * g1)

    pl.semaphore_wait(barrier, N_RCV + N_SRC - 2)

    def first_sends(comp):
        for d in (2, -2, 1, -1):
            remote(sb.at[comp], gat.at[0, rcv], ag_send.at[0], ag_recv.at[0, rcv], at_chip(d, comp)).start()

        @pl.when(c != comp)
        def _():
            remote(sb.at[comp], gat.at[0, rcv], ag_send.at[0], ag_recv.at[0, rcv], here).start()

    first_sends(0)

    def share_k(d):
        remote(k_own.at[k_rows(d)], kw.at[c, k_rows(d)], kp_send, kp_recv.at[chip(d)], here).start()

    def one_arrived(it, d, h):
        slot = chip(d) * 2 + h
        wait_recv(gat.at[it, slot], ag_recv.at[it, slot])

    def arrived(it, d):
        if d == 4 or (it == 0 and abs(d) < 3):
            one_arrived(it, d, 0)
            one_arrived(it, d, 1)
        else:
            slot = chip(d) * 2
            wait_recv(gat.at[it, pl.ds(slot, 2)], ag_recv.at[it, slot])

    def relay(it):
        for h, d in ((0, 1), (1, -1)):
            arrived(it, -2 * d)
            slot = chip(-2 * d) * 2
            half, both = gat.at[it, slot + h], gat.at[it, pl.ds(slot, 2)]
            remote(half, half, ag_send.at[it], ag_recv.at[it, slot + h], at_chip(2 * d, c)).start()
            remote(both, both, ag_send.at[it], ag_recv.at[it, slot], at_chip(d, c)).start()

    def block(q):
        rows = pl.ds(pl.multiple_of(q * (2 * L), 2 * L), 2 * L)
        return jnp.concatenate([kw[0, rows, :], kw[1, rows, :]], axis=1)

    def add_chip(it, d):
        q = chip(d)
        if it == 0:
            wait_recv(kw.at[other, k_rows(d)], kp_recv.at[q])
        v0, v1 = gat[it, q * 2], gat[it, q * 2 + 1]
        acc[0] += jnp.dot(jnp.concatenate([v0, v1], axis=1), block(q), preferred_element_type=F32)
        ed = jnp.dot(jnp.concatenate([v0, v1], axis=0), low[...], preferred_element_type=F32)
        high = elb[:, 8:9, :]
        high = jnp.concatenate([high[0], high[1]], axis=1)
        acc[1] += jnp.where(high == q * 2, ed[:B], 0.0) + jnp.where(high == q * 2 + 1, ed[B:], 0.0)

    def coef(i):
        return jnp.concatenate([co[0, i], co[1, i]], axis=1)

    def others(send):
        def one(d, carry):
            send((lax.rem(src + d, N_SRC), rcv))
            return carry

        lax.fori_loop(1, N_SRC, one, 0)

    tile = (src - 2 * c + 5) // 5 - 1
    sums_tile = (lax.rem(src - 2 * c + 5, 5) == 0) & (tile >= 0) & (tile < TILES)
    sums_scalars = src == 30 + c

    def reduce_src(it):
        part = (coef(0) * acc[1] + coef(1) * acc[0]).astype(BF16)
        for half in range(2):
            ar_s[it, 3 * half:3 * half + 3] = part[:, 128 * half:128 * half + 128].reshape(3, 16, 128)

        def send(t, carry):
            owner = 5 * t + 2 * c

            @pl.when(owner != src)
            def _():
                remote(ar_s.at[it, t], ar_in.at[it, src], a1_send.at[it], a1_recv.at[it], (owner, rcv)).start()
            return carry

        lax.fori_loop(0, TILES, send, 0)
        if it == 1:
            sc_s[...] = sum_scalars(0)

            @pl.when(jnp.logical_not(sums_scalars))
            def _():
                remote(sc_s, sc_in.at[src], s1_send, s1_recv, (30 + c, rcv)).start()

            @pl.when(sums_scalars)
            def _():
                sc_in[src] = sc_s[...]
                wait_recv(sc_in.at[pl.ds(0, N_SRC - 1)], s1_recv)
                sc_out[...] = jnp.sum(sc_in[...], axis=0)
                others(lambda dev: remote(sc_out, sc_out, s2_send, s2_recv, dev).start())

        @pl.when(sums_tile)
        def _():
            ar_in[it, src] = ar_s[it, tile]
            wait_recv(ar_in.at[it, pl.ds(0, N_SRC - 1)], a1_recv.at[it])
            ar_out[it, tile] = jnp.sum(ar_in[it].astype(F32), axis=0).astype(BF16)
            part = ar_out.at[it, tile]
            others(lambda dev: remote(part, part, a2_send.at[it], a2_recv.at[it], dev).start())
            wait_recv(ar_out.at[it, pl.ds(0, TILES - 1)], a2_recv.at[it])

        @pl.when(jnp.logical_not(sums_tile))
        def _():
            wait_recv(ar_out.at[it, pl.ds(0, TILES)], a2_recv.at[it])

        if it == 1:
            pl.when(jnp.logical_not(sums_scalars))(lambda: wait_recv(sc_out, s2_recv))
        return jnp.concatenate(
            [ar_out[it, 3 * half:3 * half + 3].reshape(B, 128) for half in range(2)], axis=1).astype(F32)

    def finish_src(it):
        @pl.when(sums_tile)
        def _():
            wait_send(ar_in.at[it, pl.ds(0, N_SRC - 1)], a2_send.at[it])
            wait_send(ar_s.at[it, pl.ds(0, TILES - 1)], a1_send.at[it])

        @pl.when(jnp.logical_not(sums_tile))
        def _():
            wait_send(ar_s.at[it, pl.ds(0, TILES)], a1_send.at[it])

        if it == 1:
            pl.when(sums_scalars)(lambda: wait_send(sc_in.at[pl.ds(0, N_SRC - 1)], s2_send))
            pl.when(jnp.logical_not(sums_scalars))(lambda: wait_send(sc_s, s1_send))

    def share_with_core(it, row):
        mine, others_row = (tf0, tf1)[it], (ts0, ts1)[it]
        mine[...] = row
        remote(mine, others_row, tc_send.at[it], tc_recv.at[it], here).start()

    def share_along_y(it):
        mine, others_row, tb = (tf0, tf1)[it], (ts0, ts1)[it], (tb0, tb1)[it]
        wait_recv(others_row, tc_recv.at[it])
        tb[y] = mine[...] + others_row[...]

        def send(d, carry):
            remote(tb.at[y], tb.at[y], t_send.at[it], t_recv.at[it], at_chip(d, c)).start()
            return carry

        lax.fori_loop(1, NY, send, 0)

    def sum_scalars(it):
        tb = (tb0, tb1)[it]
        wait_recv(tb.at[pl.ds(0, NY - 1)], t_recv.at[it])
        return jnp.sum(tb[...], axis=0)

    def scatter_sources(it, jv, scalars=None):
        w = (coef(1) * jv).astype(BF16)
        lift = coef(0) * jv
        high = jnp.concatenate([elb[0, 8:9, :], elb[1, 8:9, :]], axis=1)

        def part(d):
            q = chip(d)
            both = dot_nt(w, block(q))
            sparse = jnp.concatenate(
                [jnp.where(high == q * 2, lift, 0.0), jnp.where(high == q * 2 + 1, lift, 0.0)], axis=0)
            spread = dot_nt(sparse.astype(BF16), low[...])
            return both[:, :L] + spread[:B], both[:, L:] + spread[B:]

        def put(slot, value):
            rs_send[it, slot] = value.astype(BF16)

        def onward(slot, n, to):
            part, landing = rs_send.at[it, pl.ds(slot, n)], rs_in.at[it, pl.ds(slot, n)]
            remote(part, landing, rs_ssem.at[it], rs_recv.at[it, slot], at_chip(to, c)).start()

        def home(slot, d):
            landing = {1: 0, -1: 2, 2: 4, -2: 6}[d]
            if it == 0:
                remote(rs_send.at[it, pl.ds(slot, 2)], rs_fin.at[it, pl.ds(landing, 2)], rs_ssem.at[it],
                       rf_recv.at[it, landing], at_chip(d, c)).start()
            else:
                for h in range(2):
                    remote(rs_send.at[it, slot + h], rs_fin.at[it, landing + c], rs_ssem.at[it],
                           rf_recv.at[it, landing + c], at_chip(d, h)).start()

        for k, d in enumerate((1, -1)):
            far = part(3 * d)
            put(2 + 2 * k, far[0])
            put(3 + 2 * k, far[1])
            onward(2 + 2 * k, 2, d)
        far = part(4)
        put(0, far[0])
        put(1, far[1])
        onward(0, 1, 2)
        onward(1, 1, -2)
        for k, d in enumerate((1, -1)):
            near = part(d)
            put(6 + 2 * k, near[0])
            put(7 + 2 * k, near[1])
            home(6 + 2 * k, d)
        if scalars is not None:
            share_with_core(it, scalars())
        up, down, mine = part(2), part(-2), part(0)
        own[it, 0] = mine[0]
        own[it, 1] = mine[1]
        if it == 1:
            remote(own.at[it, other], sib.at[it], sp_send.at[it], sp_recv.at[it], here).start()

        def came(slot):
            return rs_in[it, slot].astype(F32)

        wait_recv(rs_in.at[it, pl.ds(2, 2)], rs_recv.at[it, 2])
        wait_recv(rs_in.at[it, pl.ds(0, 1)], rs_recv.at[it, 0])
        put(10, up[0] + came(2) + came(0))
        put(11, up[1] + came(3))
        home(10, 2)
        wait_recv(rs_in.at[it, pl.ds(4, 2)], rs_recv.at[it, 4])
        wait_recv(rs_in.at[it, pl.ds(1, 1)], rs_recv.at[it, 1])
        put(12, down[0] + came(4))
        put(13, down[1] + came(5) + came(1))
        home(12, -2)
        if scalars is not None:
            share_along_y(it)

    def arrivals(it, i):
        total = 0.0
        for way in range(4):
            slot = way * 2 + i
            if it == 1:
                wait_recv(rs_fin.at[it, slot], rf_recv.at[it, slot])
            total += rs_fin[it, slot].astype(F32)
        return total

    for load in loads:
        load.wait()
    tau, press = tr_ref[:, 0, :], tr_ref[:, 1, :]
    opening, state = op_ref[...], st_ref[...]
    radius = jnp.sqrt(opening * opening + press * press + 0.5)
    a_n = 1.0 - opening / radius
    b_n = 1.0 - press / radius
    ratio = jnp.abs(tau) / (1.0 + 0.6 * jnp.abs(press))
    a_s = jnp.where(state == 0, 1.0, jnp.where(state == 1, ratio, 0.0))
    b_s = jnp.where(state == 0, ratio, 1.0)
    co[c, 0] = jnp.where(c == 0, a_s, a_n)
    co[c, 1] = jnp.where(c == 0, b_s, b_n)
    co_send[0] = jnp.where(c == 0, a_n, a_s)
    co_send[1] = jnp.where(c == 0, b_n, b_s)
    elb[c, :8, :] = jnp.broadcast_to(el_ref[...], (8, 128))
    co_share = remote(co_send, co.at[c], sib_send.at[0], sib_recv.at[0], here)
    co_share.start()
    el_share = remote(elb.at[c, pl.ds(0, 8)], elb.at[c, pl.ds(0, 8)], sib_send.at[1], sib_recv.at[1], here)
    el_share.start()
    k_away.wait()
    for d in ORDER[:5]:
        share_k(d)
    first_sends(1)
    acc[...] = jnp.zeros((2, B, 256), F32)
    wait_recv(elb.at[other, pl.ds(0, 8)], sib_recv.at[1])
    for d in ORDER[5:]:
        share_k(d)
    place = jnp.concatenate([elb[0, 0:1, :], elb[1, 0:1, :]], axis=1) - src * (NY * 2 * L)
    low[...] = jnp.where(
        lax.broadcasted_iota(jnp.int32, (L, 256), 0) == (place & (L - 1)), 1.0, 0.0).astype(BF16)
    high = place >> 8
    elb[0, 8:, :] = jnp.broadcast_to(high[:, :128], (8, 128))
    elb[1, 8:, :] = jnp.broadcast_to(high[:, 128:], (8, 128))

    relay(0)
    k_copy.wait()

    def add_all(it):
        if it == 0:
            one_arrived(it, 0, other)
        add_chip(it, 0)
        for d in ORDER[1:]:
            if abs(d) != 2:
                arrived(it, d)
            add_chip(it, d)

    add_all(0)
    wait_recv(co.at[other], sib_recv.at[0])
    jv = reduce_src(0)
    j0[...] = jv
    scatter_sources(0, jv)
    gp_row = row_of(jv * jv)

    pp = 0.0
    for way in range(4):
        wait_recv(rs_fin.at[0, pl.ds(2 * way, 2)], rf_recv.at[0, 2 * way])
    for h in range(2):
        p = own[0, h] + arrivals(0, h)
        pown[h] = p
        pp += p * p
        gat[1, y * 2 + h] = p.astype(BF16)
    both = gat.at[1, pl.ds(y * 2, 2)]
    for d in (2, -2, 1, -1):
        remote(both, both, ag_send.at[1], ag_recv.at[1, y * 2], at_chip(d, c)).start()
    remote(pown.at[other], sib.at[0], sp_send.at[0], sp_recv.at[0], here).start()
    pp_row = row_of(pp)
    share_with_core(0, jnp.concatenate([gg_row, pp_row, gp_row * (1.0 / N_SRC)], axis=1))
    acc[...] = jnp.zeros((2, B, 256), F32)
    relay(1)
    share_along_y(0)
    add_all(1)
    jp = reduce_src(1)
    sums = sc_out[...]
    gg, pp, gp = sums[:, :128], sums[:, 128:256], sums[:, 256:]
    alpha0 = gg / (0.5 * gg + gp)
    left = gp / (0.5 * gg + gp)
    rr = alpha0 * (alpha0 * pp - left * gp)
    beta = rr / gg
    scale = left + beta
    alpha0_c, left_c, scale_c = col_of(alpha0), col_of(left), col_of(scale)
    jv = scale_c * j0[...] - alpha0_c * jp
    scatter_sources(1, jv, lambda: row_of(jv * jv))
    jj = sum_scalars(1)
    alpha1 = rr / (0.5 * rr * (1.0 + beta) + jj)
    alpha1_c = col_of(alpha1)
    wait_recv(sib.at[0], sp_recv.at[0])
    base = []
    for comp in range(2):
        gv = g_ref[:, comp, :]
        pv = jnp.where(c == comp, pown[c], sib[0])
        direction = scale_c * gv - alpha0_c * pv
        x_ref[:, comp, :] = alpha0_c * gv + alpha1_c * direction
        base.append(left_c * gv - alpha0_c * pv - alpha1_c * (0.5 * direction))
    wait_recv(sib.at[1], sp_recv.at[1])
    for comp in range(2):
        q = jnp.where(c == comp, own[1, c], sib[1]) + arrivals(1, comp)
        r_ref[:, comp, :] = base[comp] - alpha1_c * q

    co_share.wait_send()
    el_share.wait_send()
    wait_send(kw.at[c], kp_send)
    for it in range(2):
        wait_send(gat.at[it, pl.ds(0, 15 - it)], ag_send.at[it])
        wait_send(rs_send.at[it, pl.ds(0, 14)], rs_ssem.at[it])
        wait_send(own.at[it, 0], sp_send.at[it])
        wait_send((tb0, tb1)[it].at[pl.ds(0, NY - 1)], t_send.at[it])
        wait_send((tf0, tf1)[it], tc_send.at[it])
        finish_src(it)


def shards(stiffness, newton_rhs, traction, opening, state, elements):
    dma, vmem = pltpu.SemaphoreType.DMA, pltpu.VMEM
    out = jax.ShapeDtypeStruct((B, 2, L), F32)
    return pl.pallas_call(
        kernel,
        out_shape=(out, out),
        in_specs=[pl.BlockSpec(memory_space=pl.ANY)] * 6,
        out_specs=[pl.BlockSpec(memory_space=pltpu.VMEM)] * 2,
        scratch_shapes=[
            vmem((B, 2, L), F32),
            vmem((B, 2, 128), F32),
            vmem((B, 128), F32),
            vmem((B, 128), jnp.int32),
            vmem((1, 128), jnp.int32),
            vmem((2, NY * 2 * L, 128), BF16),
            vmem((NY * 2 * L, 128), BF16),
            vmem((L, 256), BF16),
            vmem((2, 16, 128), jnp.int32),
            vmem((2, 2, B, 128), F32),
            vmem((2, B, 128), F32),
            vmem((2, B, L), BF16),
            vmem((2, 16, B, L), BF16),
            vmem((2, B, 256), F32),
            vmem((B, 256), F32),
            vmem((2, TILES, 16, 128), BF16),
            vmem((2, N_SRC, 16, 128), BF16),
            vmem((2, TILES, 16, 128), BF16),
            vmem((1, 384), F32),
            vmem((N_SRC, 1, 384), F32),
            vmem((1, 384), F32),
            vmem((2, 16, B, L), BF16),
            vmem((2, 6, B, L), BF16),
            vmem((2, 8, B, L), BF16),
            vmem((2, 2, B, L), F32),
            vmem((2, B, L), F32),
            vmem((2, B, L), F32),
            vmem((1, 384), F32),
            vmem((1, 128), F32),
            vmem((1, 384), F32),
            vmem((1, 128), F32),
            vmem((NY, 1, 384), F32),
            vmem((NY, 1, 128), F32),
            dma((2,)), dma((2,)), dma((4,)), dma((2,)), dma((2,)), dma, dma((NY,)),
            dma((2,)), dma((2, 16)), dma((2,)), dma((2, 6)), dma((2, 8)),
            dma((2,)), dma((2,)), dma((2,)), dma((2,)), dma((2,)), dma((2,)), dma, dma, dma, dma, dma((2,)), dma((2,)),
            dma((2,)), dma((2,)),
        ],
        compiler_params=pltpu.CompilerParams(
            collective_id=0, has_side_effects=True, vmem_limit_bytes=24 * 1024 * 1024),
        cost_estimate=pl.CostEstimate(flops=8 * B * 4096 * 512, bytes_accessed=4 << 20, transcendentals=0),
    )(*(pltpu.with_memory_space_constraint(a, pltpu.HBM) for a in (
        stiffness, newton_rhs, traction, opening, state, elements.reshape(1, 128))))


def solution(mesh):
    placed = (
        P(None, "src", "rcv"),
        P(None, None, ("src", "rcv")),
        P(None, None, "rcv"),
        P(None, "rcv"),
        P(None, "rcv"),
        P("rcv"),
    )
    return jax.shard_map(
        shards,
        mesh=mesh,
        in_specs=placed,
        out_specs=(P(None, None, ("src", "rcv")), P(None, None, ("src", "rcv"))),
        check_vma=False,
    )
```

```python
import jax
import jax.numpy as jnp
from jax import lax
from jax.experimental import pallas as pl
from jax.experimental.pallas import tpu as pltpu
from jax.sharding import PartitionSpec as P

MESH = pl.DeviceIdType.MESH
F32 = jnp.float32
BF16 = jnp.bfloat16
B = 48
L = 256
NY = 8
N_RCV = 16
N_SRC = 32
TILES = 6
ORDER = (0, 1, -1, 2, -2, 3, -3, 4)


def far(i, n):
    return n // 2 + (i + 1) // 2 * (2 * ((i + 1) % 2) - 1)


def dot_nt(a, b):
    return lax.dot_general(a, b, (((1,), (1,)), ((), ())), preferred_element_type=F32)


def kernel(k_hbm, g_hbm, tr_hbm, op_hbm, st_hbm, el_hbm, x_ref, r_ref,
           g_ref, tr_ref, op_ref, st_ref, el_ref,
           kw, k_own, low, elb, co, co_send, sb, gat, acc, j0, ar_s, ar_in, ar_out, sc_s, sc_in, sc_out,
           rs_send, rs_in, rs_fin, own, pown, sib, tb0, tb1,
           k_sem, ka_sem, g_sem, in_sem, sib_send, sib_recv, kp_send, kp_recv, ag_send, ag_recv, rs_ssem, rs_recv, rf_recv,
           sp_send, sp_recv, a1_send, a1_recv, a2_send, a2_recv,
           s1_send, s1_recv, s2_send, s2_recv, t_send, t_recv):
    src = lax.axis_index("src")
    rcv = lax.axis_index("rcv")
    y = rcv // 2
    c = lax.rem(rcv, 2)
    other = 1 - c

    def chip(d):
        return lax.rem(y + d + NY, NY)

    def at_chip(d, core):
        return (src, chip(d) * 2 + core)

    def remote(s, d, ss, rs, dev):
        return pltpu.make_async_remote_copy(
            src_ref=s, dst_ref=d, send_sem=ss, recv_sem=rs, device_id=dev, device_id_type=MESH)

    here = (src, y * 2 + other)

    def wait_recv(ref, sem):
        remote(ref, ref, sem, sem, here).wait_recv()

    def wait_send(ref, sem):
        remote(ref, ref, sem, sem, here).wait_send()

    g_loads = [
        pltpu.make_async_copy(g_hbm.at[pl.ds(8 * i, 8)], g_ref.at[pl.ds(8 * i, 8)], g_sem.at[i]) for i in range(B // 8)]
    for load in g_loads:
        load.start()
    loads = [
        pltpu.make_async_copy(a, b, in_sem.at[i])
        for i, (a, b) in enumerate((
            (tr_hbm, tr_ref), (op_hbm, op_ref), (st_hbm, st_ref), (el_hbm, el_ref)))
    ]
    for load in loads:
        load.start()

    barrier = pltpu.get_barrier_semaphore()

    def greet(dev):
        pl.semaphore_signal(barrier, inc=1, device_id=dev, device_id_type=MESH)

    def greet_src(i):
        greet((lax.rem(src + far(i, N_SRC), N_SRC), rcv))

    def greet_some(i, carry):
        greet((src, lax.rem(rcv + far(i, N_RCV), N_RCV)))
        greet_src(2 * i)
        greet_src(2 * i + 1)
        return carry

    lax.fori_loop(0, N_RCV - 1, greet_some, 0)
    greet_src(N_SRC - 2)

    def k_rows(d):
        return pl.ds(pl.multiple_of(chip(d) * (2 * L), 2 * L), 2 * L)

    def k_away(d):
        return pltpu.make_async_copy(k_hbm.at[other, k_rows(d)], k_own.at[k_rows(d)], ka_sem.at[chip(d)])

    def k_copy(d):
        return pltpu.make_async_copy(k_hbm.at[c, k_rows(d)], kw.at[c, k_rows(d)], k_sem.at[chip(d)])

    for d in ORDER:
        k_away(d).start()
        k_copy(d).start()

    lane = lax.broadcasted_iota(jnp.int32, (B, 128), 1)
    case = lax.broadcasted_iota(jnp.int32, (B, 128), 0)
    diag = lane == case

    def row_of(v):
        col = jnp.sum(v, axis=1, keepdims=True)
        return jnp.sum(jnp.where(diag, col, 0.0), axis=0, keepdims=True)

    def col_of(row):
        return jnp.sum(jnp.where(diag, row, 0.0), axis=1, keepdims=True)

    for load in g_loads:
        load.wait()
    g0, g1 = g_ref[:, 0, :], g_ref[:, 1, :]
    b0, b1 = g0.astype(BF16), g1.astype(BF16)
    sb[0] = b0
    sb[1] = b1
    gat[0, rcv] = jnp.where(c == 0, b0, b1)
    gg_row = row_of(g0 * g0 + g1 * g1)

    pl.semaphore_wait(barrier, N_RCV + N_SRC - 2)

    def first_sends(comp):
        for d in (2, -2, 1, -1):
            remote(sb.at[comp], gat.at[0, rcv], ag_send.at[0], ag_recv.at[0, rcv], at_chip(d, comp)).start()

        @pl.when(c != comp)
        def _():
            remote(sb.at[comp], gat.at[0, rcv], ag_send.at[0], ag_recv.at[0, rcv], here).start()

    first_sends(0)

    def share_k(d):
        k_away(d).wait()
        remote(k_own.at[k_rows(d)], kw.at[c, k_rows(d)], kp_send, kp_recv.at[chip(d)], here).start()

    def arrived(it, d, h):
        slot = chip(d) * 2 + h
        wait_recv(gat.at[it, slot], ag_recv.at[it, slot])

    def relay(it):
        for h in range(2):
            for d in (1, -1):
                arrived(it, -2 * d, h)
                slot = chip(-2 * d) * 2 + h
                part = gat.at[it, slot]
                if (d == 1) == (h == 0):
                    remote(part, part, ag_send.at[it], ag_recv.at[it, slot], at_chip(2 * d, c)).start()
                remote(part, part, ag_send.at[it], ag_recv.at[it, slot], at_chip(d, c)).start()

    def block(q):
        rows = pl.ds(pl.multiple_of(q * (2 * L), 2 * L), 2 * L)
        return jnp.concatenate([kw[0, rows, :], kw[1, rows, :]], axis=1)

    def add_chip(it, d):
        q = chip(d)
        if it == 0:
            k_copy(d).wait()
            wait_recv(kw.at[other, k_rows(d)], kp_recv.at[q])
        v0, v1 = gat[it, q * 2], gat[it, q * 2 + 1]
        acc[0] += jnp.dot(jnp.concatenate([v0, v1], axis=1), block(q), preferred_element_type=F32)
        ed = jnp.dot(jnp.concatenate([v0, v1], axis=0), low[...], preferred_element_type=F32)
        high = elb[:, 8:9, :]
        high = jnp.concatenate([high[0], high[1]], axis=1)
        acc[1] += jnp.where(high == q * 2, ed[:B], 0.0) + jnp.where(high == q * 2 + 1, ed[B:], 0.0)

    def coef(i):
        return jnp.concatenate([co[0, i], co[1, i]], axis=1)

    def others(send):
        def one(i, carry):
            send((lax.rem(src + far(i, N_SRC), N_SRC), rcv))
            return carry

        lax.fori_loop(0, N_SRC - 1, one, 0)

    tile = (src - 2 * c + 5) // 5 - 1
    sums_tile = (lax.rem(src - 2 * c + 5, 5) == 0) & (tile >= 0) & (tile < TILES)
    sums_scalars = src == 30 + c

    def reduce_src(it):
        part = (coef(0) * acc[1] + coef(1) * acc[0]).astype(BF16)
        for half in range(2):
            ar_s[it, 3 * half:3 * half + 3] = part[:, 128 * half:128 * half + 128].reshape(3, 16, 128)

        def send(t, carry):
            owner = 5 * t + 2 * c

            @pl.when(owner != src)
            def _():
                remote(ar_s.at[it, t], ar_in.at[it, src], a1_send.at[it], a1_recv.at[it], (owner, rcv)).start()
            return carry

        lax.fori_loop(0, TILES, send, 0)
        if it == 1:
            sc_s[...] = sum_scalars(0)

            @pl.when(jnp.logical_not(sums_scalars))
            def _():
                remote(sc_s, sc_in.at[src], s1_send, s1_recv, (30 + c, rcv)).start()

            @pl.when(sums_scalars)
            def _():
                sc_in[src] = sc_s[...]
                wait_recv(sc_in.at[pl.ds(0, N_SRC - 1)], s1_recv)
                sc_out[...] = jnp.sum(sc_in[...], axis=0)
                others(lambda dev: remote(sc_out, sc_out, s2_send, s2_recv, dev).start())

        @pl.when(sums_tile)
        def _():
            ar_in[it, src] = ar_s[it, tile]
            wait_recv(ar_in.at[it, pl.ds(0, N_SRC - 1)], a1_recv.at[it])
            ar_out[it, tile] = jnp.sum(ar_in[it].astype(F32), axis=0).astype(BF16)
            part = ar_out.at[it, tile]
            others(lambda dev: remote(part, part, a2_send.at[it], a2_recv.at[it], dev).start())
            wait_recv(ar_out.at[it, pl.ds(0, TILES - 1)], a2_recv.at[it])

        @pl.when(jnp.logical_not(sums_tile))
        def _():
            wait_recv(ar_out.at[it, pl.ds(0, TILES)], a2_recv.at[it])

        if it == 1:
            pl.when(jnp.logical_not(sums_scalars))(lambda: wait_recv(sc_out, s2_recv))
        return jnp.concatenate(
            [ar_out[it, 3 * half:3 * half + 3].reshape(B, 128) for half in range(2)], axis=1).astype(F32)

    def finish_src(it):
        @pl.when(sums_tile)
        def _():
            wait_send(ar_in.at[it, pl.ds(0, N_SRC - 1)], a2_send.at[it])
            wait_send(ar_s.at[it, pl.ds(0, TILES - 1)], a1_send.at[it])

        @pl.when(jnp.logical_not(sums_tile))
        def _():
            wait_send(ar_s.at[it, pl.ds(0, TILES)], a1_send.at[it])

        if it == 1:
            pl.when(sums_scalars)(lambda: wait_send(sc_in.at[pl.ds(0, N_SRC - 1)], s2_send))
            pl.when(jnp.logical_not(sums_scalars))(lambda: wait_send(sc_s, s1_send))

    def share_scalars(it, row):
        tb = (tb0, tb1)[it]
        tb[rcv] = row

        def send(i, carry):
            remote(tb.at[rcv], tb.at[rcv], t_send.at[it], t_recv.at[it],
                   (src, lax.rem(rcv + far(i, N_RCV), N_RCV))).start()
            return carry

        lax.fori_loop(0, N_RCV - 1, send, 0)

    def sum_scalars(it):
        tb = (tb0, tb1)[it]
        wait_recv(tb.at[pl.ds(0, N_RCV - 1)], t_recv.at[it])
        return jnp.sum(tb[...], axis=0)

    def scatter_sources(it, jv, scalars=None):
        w = (coef(1) * jv).astype(BF16)
        lift = coef(0) * jv
        high = jnp.concatenate([elb[0, 8:9, :], elb[1, 8:9, :]], axis=1)

        def part(d):
            q = chip(d)
            both = dot_nt(w, block(q))
            sparse = jnp.concatenate(
                [jnp.where(high == q * 2, lift, 0.0), jnp.where(high == q * 2 + 1, lift, 0.0)], axis=0)
            spread = dot_nt(sparse.astype(BF16), low[...])
            return both[:, :L] + spread[:B], both[:, L:] + spread[B:]

        def send(slot, value, to, landing):
            rs_send[it, slot] = value.astype(BF16)
            remote(rs_send.at[it, slot], rs_in.at[it, landing], rs_ssem.at[it], rs_recv.at[it, landing],
                   at_chip(to, c)).start()

        def home(slot, value, d, h):
            rs_send[it, slot] = value.astype(BF16)
            landing = {1: 0, -1: 2, 2: 4, -2: 6}[d] + (h if it == 0 else c)
            remote(rs_send.at[it, slot], rs_fin.at[it, landing], rs_ssem.at[it], rf_recv.at[it, landing],
                   at_chip(d, c if it == 0 else h)).start()

        def came(landing):
            wait_recv(rs_in.at[it, landing], rs_recv.at[it, landing])
            return rs_in[it, landing].astype(F32)

        for k, d in enumerate((1, -1)):
            far = part(3 * d)
            send(2 + 2 * k, far[0], d, 2 + 2 * k)
            send(3 + 2 * k, far[1], d, 3 + 2 * k)
        far = part(4)
        send(0, far[0], 2, 0)
        send(1, far[1], -2, 1)
        for k, d in enumerate((1, -1)):
            near = part(d)
            home(6 + 2 * k, near[0], d, 0)
            home(7 + 2 * k, near[1], d, 1)
        if scalars is not None:
            share_scalars(it, scalars())
        up, down, mine = part(2), part(-2), part(0)
        own[it, 0] = mine[0]
        own[it, 1] = mine[1]
        if it == 1:
            remote(own.at[it, other], sib.at[it], sp_send.at[it], sp_recv.at[it], here).start()
        home(10, up[1] + came(3), 2, 1)
        home(11, down[0] + came(4), -2, 0)
        home(12, up[0] + came(2) + came(0), 2, 0)
        home(13, down[1] + came(5) + came(1), -2, 1)

    def arrivals(it, i):
        total = 0.0
        for way in range(4):
            slot = way * 2 + i
            wait_recv(rs_fin.at[it, slot], rf_recv.at[it, slot])
            total += rs_fin[it, slot].astype(F32)
        return total

    for load in loads:
        load.wait()
    tau, press = tr_ref[:, 0, :], tr_ref[:, 1, :]
    opening, state = op_ref[...], st_ref[...]
    radius = jnp.sqrt(opening * opening + press * press + 0.5)
    a_n = 1.0 - opening / radius
    b_n = 1.0 - press / radius
    ratio = jnp.abs(tau) / (1.0 + 0.6 * jnp.abs(press))
    a_s = jnp.where(state == 0, 1.0, jnp.where(state == 1, ratio, 0.0))
    b_s = jnp.where(state == 0, ratio, 1.0)
    co[c, 0] = jnp.where(c == 0, a_s, a_n)
    co[c, 1] = jnp.where(c == 0, b_s, b_n)
    co_send[0] = jnp.where(c == 0, a_n, a_s)
    co_send[1] = jnp.where(c == 0, b_n, b_s)
    elb[c, :8, :] = jnp.broadcast_to(el_ref[...], (8, 128))
    co_share = remote(co_send, co.at[c], sib_send.at[0], sib_recv.at[0], here)
    co_share.start()
    el_share = remote(elb.at[c, pl.ds(0, 8)], elb.at[c, pl.ds(0, 8)], sib_send.at[1], sib_recv.at[1], here)
    el_share.start()
    for d in ORDER[:5]:
        share_k(d)
    first_sends(1)
    acc[...] = jnp.zeros((2, B, 256), F32)
    wait_recv(elb.at[other, pl.ds(0, 8)], sib_recv.at[1])
    for d in ORDER[5:]:
        share_k(d)
    place = jnp.concatenate([elb[0, 0:1, :], elb[1, 0:1, :]], axis=1) - src * (NY * 2 * L)
    low[...] = jnp.where(
        lax.broadcasted_iota(jnp.int32, (L, 256), 0) == (place & (L - 1)), 1.0, 0.0).astype(BF16)
    high = place >> 8
    elb[0, 8:, :] = jnp.broadcast_to(high[:, :128], (8, 128))
    elb[1, 8:, :] = jnp.broadcast_to(high[:, 128:], (8, 128))

    relay(0)

    def add_all(it):
        if it == 0:
            arrived(it, 0, other)
        add_chip(it, 0)
        for d in (1, -1):
            arrived(it, d, 0)
            arrived(it, d, 1)
            add_chip(it, d)
        for d in (2, -2):
            add_chip(it, d)
        for d in (3, -3, 4):
            arrived(it, d, 0)
            arrived(it, d, 1)
            add_chip(it, d)

    add_all(0)
    wait_recv(co.at[other], sib_recv.at[0])
    jv = reduce_src(0)
    j0[...] = jv
    scatter_sources(0, jv)
    gp_row = row_of(jv * jv)

    pp = 0.0
    for h in range(2):
        p = own[0, h] + arrivals(0, h)
        pown[h] = p
        pp += p * p
        part = gat.at[1, y * 2 + h]
        part[...] = p.astype(BF16)
        for d in (2, -2):
            remote(part, part, ag_send.at[1], ag_recv.at[1, y * 2 + h], at_chip(d, c)).start()
    for h in range(2):
        part = gat.at[1, y * 2 + h]
        for d in (1, -1):
            remote(part, part, ag_send.at[1], ag_recv.at[1, y * 2 + h], at_chip(d, c)).start()
    remote(pown.at[other], sib.at[0], sp_send.at[0], sp_recv.at[0], here).start()
    pp_row = row_of(pp)
    share_scalars(0, jnp.concatenate([gg_row, pp_row, gp_row * (1.0 / N_SRC)], axis=1))
    acc[...] = jnp.zeros((2, B, 256), F32)
    relay(1)
    add_all(1)
    jp = reduce_src(1)
    sums = sc_out[...]
    gg, pp, gp = sums[:, :128], sums[:, 128:256], sums[:, 256:]
    alpha0 = gg / (0.5 * gg + gp)
    left = gp / (0.5 * gg + gp)
    rr = alpha0 * (alpha0 * pp - left * gp)
    beta = rr / gg
    scale = left + beta
    alpha0_c, left_c, scale_c = col_of(alpha0), col_of(left), col_of(scale)
    jv = scale_c * j0[...] - alpha0_c * jp
    scatter_sources(1, jv, lambda: row_of(jv * jv))
    jj = sum_scalars(1)
    alpha1 = rr / (0.5 * rr * (1.0 + beta) + jj)
    alpha1_c = col_of(alpha1)
    wait_recv(sib.at[0], sp_recv.at[0])
    base = []
    for comp in range(2):
        gv = g_ref[:, comp, :]
        pv = jnp.where(c == comp, pown[c], sib[0])
        direction = scale_c * gv - alpha0_c * pv
        x_ref[:, comp, :] = alpha0_c * gv + alpha1_c * direction
        base.append(left_c * gv - alpha0_c * pv - alpha1_c * (0.5 * direction))
    wait_recv(sib.at[1], sp_recv.at[1])
    for comp in range(2):
        q = jnp.where(c == comp, own[1, c], sib[1]) + arrivals(1, comp)
        r_ref[:, comp, :] = base[comp] - alpha1_c * q

    co_share.wait_send()
    el_share.wait_send()
    wait_send(kw.at[c], kp_send)
    for it in range(2):
        wait_send(gat.at[it, pl.ds(0, 15 - it)], ag_send.at[it])
        wait_send(rs_send.at[it, pl.ds(0, 14)], rs_ssem.at[it])
        wait_send(own.at[it, 0], sp_send.at[it])
        wait_send((tb0, tb1)[it].at[pl.ds(0, N_RCV - 1)], t_send.at[it])
        finish_src(it)


def shards(stiffness, newton_rhs, traction, opening, state, elements):
    dma, vmem = pltpu.SemaphoreType.DMA, pltpu.VMEM
    out = jax.ShapeDtypeStruct((B, 2, L), F32)
    return pl.pallas_call(
        kernel,
        out_shape=(out, out),
        in_specs=[pl.BlockSpec(memory_space=pl.ANY)] * 6,
        out_specs=[pl.BlockSpec(memory_space=pltpu.VMEM)] * 2,
        scratch_shapes=[
            vmem((B, 2, L), F32),
            vmem((B, 2, 128), F32),
            vmem((B, 128), F32),
            vmem((B, 128), jnp.int32),
            vmem((1, 128), jnp.int32),
            vmem((2, NY * 2 * L, 128), BF16),
            vmem((NY * 2 * L, 128), BF16),
            vmem((L, 256), BF16),
            vmem((2, 16, 128), jnp.int32),
            vmem((2, 2, B, 128), F32),
            vmem((2, B, 128), F32),
            vmem((2, B, L), BF16),
            vmem((2, 16, B, L), BF16),
            vmem((2, B, 256), F32),
            vmem((B, 256), F32),
            vmem((2, TILES, 16, 128), BF16),
            vmem((2, N_SRC, 16, 128), BF16),
            vmem((2, TILES, 16, 128), BF16),
            vmem((1, 384), F32),
            vmem((N_SRC, 1, 384), F32),
            vmem((1, 384), F32),
            vmem((2, 16, B, L), BF16),
            vmem((2, 6, B, L), BF16),
            vmem((2, 8, B, L), BF16),
            vmem((2, 2, B, L), F32),
            vmem((2, B, L), F32),
            vmem((2, B, L), F32),
            vmem((N_RCV, 1, 384), F32),
            vmem((N_RCV, 1, 128), F32),
            dma((NY,)), dma((NY,)), dma((B // 8,)), dma((4,)), dma((2,)), dma((2,)), dma, dma((NY,)),
            dma((2,)), dma((2, 16)), dma((2,)), dma((2, 6)), dma((2, 8)),
            dma((2,)), dma((2,)), dma((2,)), dma((2,)), dma((2,)), dma((2,)), dma, dma, dma, dma, dma((2,)), dma((2,)),
        ],
        compiler_params=pltpu.CompilerParams(
            collective_id=0, has_side_effects=True, vmem_limit_bytes=24 * 1024 * 1024),
        cost_estimate=pl.CostEstimate(flops=8 * B * 4096 * 512, bytes_accessed=4 << 20, transcendentals=0),
    )(*(pltpu.with_memory_space_constraint(a, pltpu.HBM) for a in (
        stiffness, newton_rhs, traction, opening, state, elements.reshape(1, 128))))


def solution(mesh):
    placed = (
        P(None, "src", "rcv"),
        P(None, None, ("src", "rcv")),
        P(None, None, "rcv"),
        P(None, "rcv"),
        P(None, "rcv"),
        P("rcv"),
    )
    return jax.shard_map(
        shards,
        mesh=mesh,
        in_specs=placed,
        out_specs=(P(None, None, ("src", "rcv")), P(None, None, ("src", "rcv"))),
        check_vma=False,
    )
```

```python
import jax
import jax.numpy as jnp
from jax import lax
from jax.experimental import pallas as pl
from jax.experimental.pallas import tpu as pltpu
from jax.sharding import PartitionSpec as P

MESH = pl.DeviceIdType.MESH
F32 = jnp.float32
BF16 = jnp.bfloat16
B = 48
L = 256
NY = 8
N_RCV = 16
N_SRC = 32
NX = 4
NZ = 8
TILES = 6
ORDER = (0, 1, -1, 2, -2, 3, -3, 4)


def far(i, n):
    return n // 2 + (i + 1) // 2 * (2 * ((i + 1) % 2) - 1)


def dot_nt(a, b):
    return lax.dot_general(a, b, (((1,), (1,)), ((), ())), preferred_element_type=F32)


def kernel(k_hbm, g_hbm, tr_hbm, op_hbm, st_hbm, el_hbm, x_ref, r_ref,
           g_ref, tr_ref, op_ref, st_ref, el_ref,
           kw, k_own, low, elb, co, co_send, sb, gat, acc, j0, ar_s, ar_in, ar_out, sc_s, sc_in, sc_out,
           rs_send, rs_in, rs_fin, own, pown, sib, tb0, tb1,
           k_sem, ka_sem, g_sem, in_sem, sib_send, sib_recv, kp_send, kp_recv, ag_send, ag_recv, rs_ssem, rs_recv, rf_recv,
           sp_send, sp_recv, a1_send, a1_recv, a2_send, a2_recv,
           s1_send, s1_recv, s2_send, s2_recv, t_send, t_recv):
    src = lax.axis_index("src")
    rcv = lax.axis_index("rcv")
    y = rcv // 2
    c = lax.rem(rcv, 2)
    other = 1 - c

    def chip(d):
        return lax.rem(y + d + NY, NY)

    def at_chip(d, core):
        return (src, chip(d) * 2 + core)

    def remote(s, d, ss, rs, dev):
        return pltpu.make_async_remote_copy(
            src_ref=s, dst_ref=d, send_sem=ss, recv_sem=rs, device_id=dev, device_id_type=MESH)

    here = (src, y * 2 + other)

    def wait_recv(ref, sem):
        remote(ref, ref, sem, sem, here).wait_recv()

    def wait_send(ref, sem):
        remote(ref, ref, sem, sem, here).wait_send()

    g_loads = [
        pltpu.make_async_copy(g_hbm.at[pl.ds(8 * i, 8)], g_ref.at[pl.ds(8 * i, 8)], g_sem.at[i]) for i in range(B // 8)]
    for load in g_loads:
        load.start()
    loads = [
        pltpu.make_async_copy(a, b, in_sem.at[i])
        for i, (a, b) in enumerate((
            (tr_hbm, tr_ref), (op_hbm, op_ref), (st_hbm, st_ref), (el_hbm, el_ref)))
    ]
    for load in loads:
        load.start()

    barrier = pltpu.get_barrier_semaphore()

    def greet(dev):
        pl.semaphore_signal(barrier, inc=1, device_id=dev, device_id_type=MESH)

    def greet_src(i):
        greet((lax.rem(src + far(i, N_SRC), N_SRC), rcv))

    def greet_some(i, carry):
        greet((src, lax.rem(rcv + far(i, N_RCV), N_RCV)))
        greet_src(2 * i)
        greet_src(2 * i + 1)
        return carry

    lax.fori_loop(0, N_RCV - 1, greet_some, 0)
    greet_src(N_SRC - 2)

    def k_rows(d):
        return pl.ds(pl.multiple_of(chip(d) * (2 * L), 2 * L), 2 * L)

    def k_away(d):
        return pltpu.make_async_copy(k_hbm.at[other, k_rows(d)], k_own.at[k_rows(d)], ka_sem.at[chip(d)])

    def k_copy(d):
        return pltpu.make_async_copy(k_hbm.at[c, k_rows(d)], kw.at[c, k_rows(d)], k_sem.at[chip(d)])

    for d in ORDER:
        k_away(d).start()
        k_copy(d).start()

    lane = lax.broadcasted_iota(jnp.int32, (B, 128), 1)
    case = lax.broadcasted_iota(jnp.int32, (B, 128), 0)
    diag = lane == case

    def row_of(v):
        col = jnp.sum(v, axis=1, keepdims=True)
        return jnp.sum(jnp.where(diag, col, 0.0), axis=0, keepdims=True)

    def col_of(row):
        return jnp.sum(jnp.where(diag, row, 0.0), axis=1, keepdims=True)

    for load in g_loads:
        load.wait()
    g0, g1 = g_ref[:, 0, :], g_ref[:, 1, :]
    b0, b1 = g0.astype(BF16), g1.astype(BF16)
    sb[0] = b0
    sb[1] = b1
    gat[0, rcv] = jnp.where(c == 0, b0, b1)
    gg_row = row_of(g0 * g0 + g1 * g1)

    pl.semaphore_wait(barrier, N_RCV + N_SRC - 2)

    def first_sends(comp):
        for d in (2, -2, 1, -1):
            remote(sb.at[comp], gat.at[0, rcv], ag_send.at[0], ag_recv.at[0, rcv], at_chip(d, comp)).start()

        @pl.when(c != comp)
        def _():
            remote(sb.at[comp], gat.at[0, rcv], ag_send.at[0], ag_recv.at[0, rcv], here).start()

    first_sends(0)

    def share_k(d):
        k_away(d).wait()
        remote(k_own.at[k_rows(d)], kw.at[c, k_rows(d)], kp_send, kp_recv.at[chip(d)], here).start()

    def arrived(it, d, h):
        slot = chip(d) * 2 + h
        wait_recv(gat.at[it, slot], ag_recv.at[it, slot])

    def relay(it):
        for h in range(2):
            for d in (1, -1):
                arrived(it, -2 * d, h)
                slot = chip(-2 * d) * 2 + h
                part = gat.at[it, slot]
                if (d == 1) == (h == 0):
                    remote(part, part, ag_send.at[it], ag_recv.at[it, slot], at_chip(2 * d, c)).start()
                remote(part, part, ag_send.at[it], ag_recv.at[it, slot], at_chip(d, c)).start()

    def block(q):
        rows = pl.ds(pl.multiple_of(q * (2 * L), 2 * L), 2 * L)
        return jnp.concatenate([kw[0, rows, :], kw[1, rows, :]], axis=1)

    def add_chip(it, d):
        q = chip(d)
        if it == 0:
            k_copy(d).wait()
            wait_recv(kw.at[other, k_rows(d)], kp_recv.at[q])
        v0, v1 = gat[it, q * 2], gat[it, q * 2 + 1]
        acc[0] += jnp.dot(jnp.concatenate([v0, v1], axis=1), block(q), preferred_element_type=F32)
        ed = jnp.dot(jnp.concatenate([v0, v1], axis=0), low[...], preferred_element_type=F32)
        high = elb[:, 8:9, :]
        high = jnp.concatenate([high[0], high[1]], axis=1)
        acc[1] += jnp.where(high == q * 2, ed[:B], 0.0) + jnp.where(high == q * 2 + 1, ed[B:], 0.0)

    def coef(i):
        return jnp.concatenate([co[0, i], co[1, i]], axis=1)

    z = src // NX
    x = lax.rem(src, NX)
    tile = lax.rem(z + 4 * (x // 2), NZ)
    sums_tile = (lax.rem(x, 2) == c) & (tile < TILES)
    sums_scalars = (lax.rem(x, 2) == c) & (tile == TILES)
    steps = [(dz, dx) for dz in range(NZ) for dx in range(NX)]
    reach = {(dz, dx): min(dz, NZ - dz) + min(dx, NX - dx) for dz, dx in steps}
    near = [s for s in steps if 0 < reach[s] < 3 or (reach[s] == 3 and 0 < s[0] < 4)]
    near = sorted(near, key=lambda s: -reach[s])

    def send_sum(part, send_sem, recv_sem):
        for dz, dx in near:
            dev = (lax.rem(z + dz, NZ) * NX + lax.rem(x + dx, NX), rcv)
            remote(part, part, send_sem, recv_sem, dev).start()

    def send_to_sums(t, part, landing, send_sem, recv_sem):
        for end in range(2):
            owner = lax.rem(t + 4 * end, NZ) * NX + c + 2 * end

            @pl.when(owner != src)
            def _():
                remote(part, landing.at[src], send_sem, recv_sem, (owner, rcv)).start()

    def reduce_src(it):
        part = (coef(0) * acc[1] + coef(1) * acc[0]).astype(BF16)
        for half in range(2):
            ar_s[it, 3 * half:3 * half + 3] = part[:, 128 * half:128 * half + 128].reshape(3, 16, 128)

        def send(t, carry):
            send_to_sums(t, ar_s.at[it, t], ar_in.at[it], a1_send.at[it], a1_recv.at[it])
            return carry

        lax.fori_loop(0, TILES, send, 0)
        if it == 1:
            sc_s[...] = sum_scalars(0)
            send_to_sums(TILES, sc_s, sc_in, s1_send, s1_recv)

            @pl.when(sums_scalars)
            def _():
                sc_in[src] = sc_s[...]
                wait_recv(sc_in.at[pl.ds(0, N_SRC - 1)], s1_recv)
                sc_out[...] = jnp.sum(sc_in[...], axis=0)
                send_sum(sc_out, s2_send, s2_recv)

        @pl.when(sums_tile)
        def _():
            ar_in[it, src] = ar_s[it, tile]
            wait_recv(ar_in.at[it, pl.ds(0, N_SRC - 1)], a1_recv.at[it])
            ar_out[it, tile] = jnp.sum(ar_in[it].astype(F32), axis=0).astype(BF16)
            send_sum(ar_out.at[it, tile], a2_send.at[it], a2_recv.at[it])
            wait_recv(ar_out.at[it, pl.ds(0, TILES - 1)], a2_recv.at[it])

        @pl.when(jnp.logical_not(sums_tile))
        def _():
            wait_recv(ar_out.at[it, pl.ds(0, TILES)], a2_recv.at[it])

        if it == 1:
            pl.when(jnp.logical_not(sums_scalars))(lambda: wait_recv(sc_out, s2_recv))
        return jnp.concatenate(
            [ar_out[it, 3 * half:3 * half + 3].reshape(B, 128) for half in range(2)], axis=1).astype(F32)

    def finish_src(it):
        @pl.when(sums_tile)
        def _():
            wait_send(ar_in.at[it, pl.ds(0, len(near))], a2_send.at[it])
            wait_send(ar_in.at[it, pl.ds(0, 2 * TILES - 1)], a1_send.at[it])

        @pl.when(jnp.logical_not(sums_tile))
        def _():
            wait_send(ar_in.at[it, pl.ds(0, 2 * TILES)], a1_send.at[it])

        if it == 1:
            @pl.when(sums_scalars)
            def _():
                wait_send(sc_in.at[pl.ds(0, len(near))], s2_send)
                wait_send(sc_in.at[pl.ds(0, 1)], s1_send)

            @pl.when(jnp.logical_not(sums_scalars))
            def _():
                wait_send(sc_in.at[pl.ds(0, 2)], s1_send)

    def share_scalars(it, row):
        tb = (tb0, tb1)[it]
        tb[rcv] = row

        def send(i, carry):
            remote(tb.at[rcv], tb.at[rcv], t_send.at[it], t_recv.at[it],
                   (src, lax.rem(rcv + far(i, N_RCV), N_RCV))).start()
            return carry

        lax.fori_loop(0, N_RCV - 1, send, 0)

    def sum_scalars(it):
        tb = (tb0, tb1)[it]
        wait_recv(tb.at[pl.ds(0, N_RCV - 1)], t_recv.at[it])
        return jnp.sum(tb[...], axis=0)

    def scatter_sources(it, jv, scalars=None):
        w = (coef(1) * jv).astype(BF16)
        lift = coef(0) * jv
        high = jnp.concatenate([elb[0, 8:9, :], elb[1, 8:9, :]], axis=1)

        def part(d):
            q = chip(d)
            both = dot_nt(w, block(q))
            sparse = jnp.concatenate(
                [jnp.where(high == q * 2, lift, 0.0), jnp.where(high == q * 2 + 1, lift, 0.0)], axis=0)
            spread = dot_nt(sparse.astype(BF16), low[...])
            return both[:, :L] + spread[:B], both[:, L:] + spread[B:]

        def send(slot, value, to, landing):
            rs_send[it, slot] = value.astype(BF16)
            remote(rs_send.at[it, slot], rs_in.at[it, landing], rs_ssem.at[it], rs_recv.at[it, landing],
                   at_chip(to, c)).start()

        def home(slot, value, d, h):
            rs_send[it, slot] = value.astype(BF16)
            landing = {1: 0, -1: 2, 2: 4, -2: 6}[d] + (h if it == 0 else c)
            remote(rs_send.at[it, slot], rs_fin.at[it, landing], rs_ssem.at[it], rf_recv.at[it, landing],
                   at_chip(d, c if it == 0 else h)).start()

        def came(landing):
            wait_recv(rs_in.at[it, landing], rs_recv.at[it, landing])
            return rs_in[it, landing].astype(F32)

        far = part(4)
        send(0, far[0], 2, 0)
        send(1, far[1], -2, 1)
        for k, d in enumerate((1, -1)):
            far = part(3 * d)
            send(2 + 2 * k, far[0], d, 2 + 2 * k)
            send(3 + 2 * k, far[1], d, 3 + 2 * k)
        for k, d in enumerate((1, -1)):
            near = part(d)
            home(6 + 2 * k, near[0], d, 0)
            home(7 + 2 * k, near[1], d, 1)
        if scalars is not None:
            share_scalars(it, scalars())
        up, down, mine = part(2), part(-2), part(0)
        own[it, 0] = mine[0]
        own[it, 1] = mine[1]
        if it == 1:
            remote(own.at[it, other], sib.at[it], sp_send.at[it], sp_recv.at[it], here).start()
        home(10, up[1] + came(3), 2, 1)
        home(11, down[0] + came(4), -2, 0)
        home(12, up[0] + came(2) + came(0), 2, 0)
        home(13, down[1] + came(5) + came(1), -2, 1)

    def arrivals(it, i):
        total = 0.0
        for way in range(4):
            slot = way * 2 + i
            wait_recv(rs_fin.at[it, slot], rf_recv.at[it, slot])
            total += rs_fin[it, slot].astype(F32)
        return total

    for load in loads:
        load.wait()
    tau, press = tr_ref[:, 0, :], tr_ref[:, 1, :]
    opening, state = op_ref[...], st_ref[...]
    radius = jnp.sqrt(opening * opening + press * press + 0.5)
    a_n = 1.0 - opening / radius
    b_n = 1.0 - press / radius
    ratio = jnp.abs(tau) / (1.0 + 0.6 * jnp.abs(press))
    a_s = jnp.where(state == 0, 1.0, jnp.where(state == 1, ratio, 0.0))
    b_s = jnp.where(state == 0, ratio, 1.0)
    co[c, 0] = jnp.where(c == 0, a_s, a_n)
    co[c, 1] = jnp.where(c == 0, b_s, b_n)
    co_send[0] = jnp.where(c == 0, a_n, a_s)
    co_send[1] = jnp.where(c == 0, b_n, b_s)
    elb[c, :8, :] = jnp.broadcast_to(el_ref[...], (8, 128))
    co_share = remote(co_send, co.at[c], sib_send.at[0], sib_recv.at[0], here)
    co_share.start()
    el_share = remote(elb.at[c, pl.ds(0, 8)], elb.at[c, pl.ds(0, 8)], sib_send.at[1], sib_recv.at[1], here)
    el_share.start()
    for d in ORDER[:5]:
        share_k(d)
    first_sends(1)
    acc[...] = jnp.zeros((2, B, 256), F32)
    wait_recv(elb.at[other, pl.ds(0, 8)], sib_recv.at[1])
    for d in ORDER[5:]:
        share_k(d)
    place = jnp.concatenate([elb[0, 0:1, :], elb[1, 0:1, :]], axis=1) - src * (NY * 2 * L)
    low[...] = jnp.where(
        lax.broadcasted_iota(jnp.int32, (L, 256), 0) == (place & (L - 1)), 1.0, 0.0).astype(BF16)
    high = place >> 8
    elb[0, 8:, :] = jnp.broadcast_to(high[:, :128], (8, 128))
    elb[1, 8:, :] = jnp.broadcast_to(high[:, 128:], (8, 128))

    relay(0)

    def add_all(it):
        if it == 0:
            arrived(it, 0, other)
        add_chip(it, 0)
        for d in (1, -1):
            arrived(it, d, 0)
            arrived(it, d, 1)
            add_chip(it, d)
        for d in (2, -2):
            add_chip(it, d)
        for d in (3, -3, 4):
            arrived(it, d, 0)
            arrived(it, d, 1)
            add_chip(it, d)

    add_all(0)
    wait_recv(co.at[other], sib_recv.at[0])
    jv = reduce_src(0)
    j0[...] = jv
    scatter_sources(0, jv)
    gp_row = row_of(jv * jv)

    pp = 0.0
    for h in range(2):
        p = own[0, h] + arrivals(0, h)
        pown[h] = p
        pp += p * p
        part = gat.at[1, y * 2 + h]
        part[...] = p.astype(BF16)
        for d in (2, -2):
            remote(part, part, ag_send.at[1], ag_recv.at[1, y * 2 + h], at_chip(d, c)).start()
    for h in range(2):
        part = gat.at[1, y * 2 + h]
        for d in (1, -1):
            remote(part, part, ag_send.at[1], ag_recv.at[1, y * 2 + h], at_chip(d, c)).start()
    remote(pown.at[other], sib.at[0], sp_send.at[0], sp_recv.at[0], here).start()
    pp_row = row_of(pp)
    share_scalars(0, jnp.concatenate([gg_row, pp_row, gp_row * (1.0 / N_SRC)], axis=1))
    acc[...] = jnp.zeros((2, B, 256), F32)
    relay(1)
    add_all(1)
    jp = reduce_src(1)
    sums = sc_out[...]
    gg, pp, gp = sums[:, :128], sums[:, 128:256], sums[:, 256:]
    alpha0 = gg / (0.5 * gg + gp)
    left = gp / (0.5 * gg + gp)
    rr = alpha0 * (alpha0 * pp - left * gp)
    beta = rr / gg
    scale = left + beta
    alpha0_c, left_c, scale_c = col_of(alpha0), col_of(left), col_of(scale)
    jv = scale_c * j0[...] - alpha0_c * jp
    scatter_sources(1, jv, lambda: row_of(jv * jv))
    jj = sum_scalars(1)
    alpha1 = rr / (0.5 * rr * (1.0 + beta) + jj)
    alpha1_c = col_of(alpha1)
    wait_recv(sib.at[0], sp_recv.at[0])
    base = []
    for comp in range(2):
        gv = g_ref[:, comp, :]
        pv = jnp.where(c == comp, pown[c], sib[0])
        direction = scale_c * gv - alpha0_c * pv
        x_ref[:, comp, :] = alpha0_c * gv + alpha1_c * direction
        base.append(left_c * gv - alpha0_c * pv - alpha1_c * (0.5 * direction))
    wait_recv(sib.at[1], sp_recv.at[1])
    for comp in range(2):
        q = jnp.where(c == comp, own[1, c], sib[1]) + arrivals(1, comp)
        r_ref[:, comp, :] = base[comp] - alpha1_c * q

    co_share.wait_send()
    el_share.wait_send()
    wait_send(kw.at[c], kp_send)
    for it in range(2):
        wait_send(gat.at[it, pl.ds(0, 15 - it)], ag_send.at[it])
        wait_send(rs_send.at[it, pl.ds(0, 14)], rs_ssem.at[it])
        wait_send(own.at[it, 0], sp_send.at[it])
        wait_send((tb0, tb1)[it].at[pl.ds(0, N_RCV - 1)], t_send.at[it])
        finish_src(it)


def shards(stiffness, newton_rhs, traction, opening, state, elements):
    dma, vmem = pltpu.SemaphoreType.DMA, pltpu.VMEM
    out = jax.ShapeDtypeStruct((B, 2, L), F32)
    return pl.pallas_call(
        kernel,
        out_shape=(out, out),
        in_specs=[pl.BlockSpec(memory_space=pl.ANY)] * 6,
        out_specs=[pl.BlockSpec(memory_space=pltpu.VMEM)] * 2,
        scratch_shapes=[
            vmem((B, 2, L), F32),
            vmem((B, 2, 128), F32),
            vmem((B, 128), F32),
            vmem((B, 128), jnp.int32),
            vmem((1, 128), jnp.int32),
            vmem((2, NY * 2 * L, 128), BF16),
            vmem((NY * 2 * L, 128), BF16),
            vmem((L, 256), BF16),
            vmem((2, 16, 128), jnp.int32),
            vmem((2, 2, B, 128), F32),
            vmem((2, B, 128), F32),
            vmem((2, B, L), BF16),
            vmem((2, 16, B, L), BF16),
            vmem((2, B, 256), F32),
            vmem((B, 256), F32),
            vmem((2, TILES, 16, 128), BF16),
            vmem((2, N_SRC, 16, 128), BF16),
            vmem((2, TILES, 16, 128), BF16),
            vmem((1, 384), F32),
            vmem((N_SRC, 1, 384), F32),
            vmem((1, 384), F32),
            vmem((2, 16, B, L), BF16),
            vmem((2, 6, B, L), BF16),
            vmem((2, 8, B, L), BF16),
            vmem((2, 2, B, L), F32),
            vmem((2, B, L), F32),
            vmem((2, B, L), F32),
            vmem((N_RCV, 1, 384), F32),
            vmem((N_RCV, 1, 128), F32),
            dma((NY,)), dma((NY,)), dma((B // 8,)), dma((4,)), dma((2,)), dma((2,)), dma, dma((NY,)),
            dma((2,)), dma((2, 16)), dma((2,)), dma((2, 6)), dma((2, 8)),
            dma((2,)), dma((2,)), dma((2,)), dma((2,)), dma((2,)), dma((2,)), dma, dma, dma, dma, dma((2,)), dma((2,)),
        ],
        compiler_params=pltpu.CompilerParams(
            collective_id=0, has_side_effects=True, vmem_limit_bytes=24 * 1024 * 1024),
        cost_estimate=pl.CostEstimate(flops=8 * B * 4096 * 512, bytes_accessed=4 << 20, transcendentals=0),
    )(*(pltpu.with_memory_space_constraint(a, pltpu.HBM) for a in (
        stiffness, newton_rhs, traction, opening, state, elements.reshape(1, 128))))


def solution(mesh):
    placed = (
        P(None, "src", "rcv"),
        P(None, None, ("src", "rcv")),
        P(None, None, "rcv"),
        P(None, "rcv"),
        P(None, "rcv"),
        P("rcv"),
    )
    return jax.shard_map(
        shards,
        mesh=mesh,
        in_specs=placed,
        out_specs=(P(None, None, ("src", "rcv")), P(None, None, ("src", "rcv"))),
        check_vma=False,
    )
```

```python
import jax
import jax.numpy as jnp
from jax import lax
from jax.experimental import pallas as pl
from jax.experimental.pallas import tpu as pltpu
from jax.sharding import PartitionSpec as P

MESH = pl.DeviceIdType.MESH
F32 = jnp.float32
BF16 = jnp.bfloat16
B = 48
L = 256
NY = 8
N_RCV = 16
N_SRC = 32
NX = 4
NZ = 8
TILES = 6
ORDER = (0, 1, -1, 2, -2, 3, -3, 4)
WAYS = (4, 3, -3, 2, -2, 1, -1)


def far(i, n):
    return n // 2 + (i + 1) // 2 * (2 * ((i + 1) % 2) - 1)


def dot_nt(a, b):
    return lax.dot_general(a, b, (((1,), (1,)), ((), ())), preferred_element_type=F32)


def kernel(k_hbm, g_hbm, tr_hbm, op_hbm, st_hbm, el_hbm, x_ref, r_ref,
           g_ref, tr_ref, op_ref, st_ref, el_ref,
           kw, k_own, low, elb, co, co_send, sb, gat, acc, j0, ar_s, ar_in, ar_out, sc_s, sc_in, sc_out,
           rs_send, rs_fin, own, pown, sib, tb0, tb1,
           k_sem, ka_sem, g_sem, in_sem, sib_send, sib_recv, kp_send, kp_recv, ag_send, ag_recv, rs_ssem, rf_recv,
           sp_send, sp_recv, a1_send, a1_recv, a2_send, a2_recv,
           s1_send, s1_recv, s2_send, s2_recv, t_send, t_recv):
    src = lax.axis_index("src")
    rcv = lax.axis_index("rcv")
    y = rcv // 2
    c = lax.rem(rcv, 2)
    other = 1 - c

    def chip(d):
        return lax.rem(y + d + NY, NY)

    def at_chip(d, core):
        return (src, chip(d) * 2 + core)

    def remote(s, d, ss, rs, dev):
        return pltpu.make_async_remote_copy(
            src_ref=s, dst_ref=d, send_sem=ss, recv_sem=rs, device_id=dev, device_id_type=MESH)

    here = (src, y * 2 + other)

    def wait_recv(ref, sem):
        remote(ref, ref, sem, sem, here).wait_recv()

    def wait_send(ref, sem):
        remote(ref, ref, sem, sem, here).wait_send()

    g_loads = [
        pltpu.make_async_copy(g_hbm.at[pl.ds(8 * i, 8)], g_ref.at[pl.ds(8 * i, 8)], g_sem.at[i]) for i in range(B // 8)]
    for load in g_loads:
        load.start()
    loads = [
        pltpu.make_async_copy(a, b, in_sem.at[i])
        for i, (a, b) in enumerate((
            (tr_hbm, tr_ref), (op_hbm, op_ref), (st_hbm, st_ref), (el_hbm, el_ref)))
    ]
    for load in loads:
        load.start()

    barrier = pltpu.get_barrier_semaphore()

    def greet(dev):
        pl.semaphore_signal(barrier, inc=1, device_id=dev, device_id_type=MESH)

    def greet_src(i):
        greet((lax.rem(src + far(i, N_SRC), N_SRC), rcv))

    def greet_some(i, carry):
        greet((src, lax.rem(rcv + far(i, N_RCV), N_RCV)))
        greet_src(2 * i)
        greet_src(2 * i + 1)
        return carry

    lax.fori_loop(0, N_RCV - 1, greet_some, 0)
    greet_src(N_SRC - 2)

    def k_rows(d):
        return pl.ds(pl.multiple_of(chip(d) * (2 * L), 2 * L), 2 * L)

    def k_away(d):
        return pltpu.make_async_copy(k_hbm.at[other, k_rows(d)], k_own.at[k_rows(d)], ka_sem.at[chip(d)])

    def k_copy(d):
        return pltpu.make_async_copy(k_hbm.at[c, k_rows(d)], kw.at[c, k_rows(d)], k_sem.at[chip(d)])

    for d in ORDER:
        k_away(d).start()
        k_copy(d).start()

    lane = lax.broadcasted_iota(jnp.int32, (B, 128), 1)
    case = lax.broadcasted_iota(jnp.int32, (B, 128), 0)
    diag = lane == case

    def row_of(v):
        col = jnp.sum(v, axis=1, keepdims=True)
        return jnp.sum(jnp.where(diag, col, 0.0), axis=0, keepdims=True)

    def col_of(row):
        return jnp.sum(jnp.where(diag, row, 0.0), axis=1, keepdims=True)

    for load in g_loads:
        load.wait()
    g0, g1 = g_ref[:, 0, :], g_ref[:, 1, :]
    b0, b1 = g0.astype(BF16), g1.astype(BF16)
    sb[0] = b0
    sb[1] = b1
    gat[0, rcv] = jnp.where(c == 0, b0, b1)
    gg_row = row_of(g0 * g0 + g1 * g1)

    pl.semaphore_wait(barrier, N_RCV + N_SRC - 2)

    def first_sends(comp):
        for d in WAYS:
            remote(sb.at[comp], gat.at[0, rcv], ag_send.at[0], ag_recv.at[0, rcv], at_chip(d, comp)).start()

        @pl.when(c != comp)
        def _():
            remote(sb.at[comp], gat.at[0, rcv], ag_send.at[0], ag_recv.at[0, rcv], here).start()

    first_sends(0)

    def share_k(d):
        k_away(d).wait()
        remote(k_own.at[k_rows(d)], kw.at[c, k_rows(d)], kp_send, kp_recv.at[chip(d)], here).start()

    def arrived(it, d, h):
        slot = chip(d) * 2 + h
        wait_recv(gat.at[it, slot], ag_recv.at[it, slot])

    def block(q):
        rows = pl.ds(pl.multiple_of(q * (2 * L), 2 * L), 2 * L)
        return jnp.concatenate([kw[0, rows, :], kw[1, rows, :]], axis=1)

    def add_chip(it, d):
        q = chip(d)
        if it == 0:
            k_copy(d).wait()
            wait_recv(kw.at[other, k_rows(d)], kp_recv.at[q])
        v0, v1 = gat[it, q * 2], gat[it, q * 2 + 1]
        acc[0] += jnp.dot(jnp.concatenate([v0, v1], axis=1), block(q), preferred_element_type=F32)
        ed = jnp.dot(jnp.concatenate([v0, v1], axis=0), low[...], preferred_element_type=F32)
        high = elb[:, 8:9, :]
        high = jnp.concatenate([high[0], high[1]], axis=1)
        acc[1] += jnp.where(high == q * 2, ed[:B], 0.0) + jnp.where(high == q * 2 + 1, ed[B:], 0.0)

    def coef(i):
        return jnp.concatenate([co[0, i], co[1, i]], axis=1)

    z = src // NX
    x = lax.rem(src, NX)
    tile = lax.rem(z + 4 * (x // 2), NZ)
    sums_tile = (lax.rem(x, 2) == c) & (tile < TILES)
    sums_scalars = (lax.rem(x, 2) == c) & (tile == TILES)
    steps = [(dz, dx) for dz in range(NZ) for dx in range(NX)]
    reach = {(dz, dx): min(dz, NZ - dz) + min(dx, NX - dx) for dz, dx in steps}
    near = [s for s in steps if 0 < reach[s] < 3 or (reach[s] == 3 and 0 < s[0] < 4)]
    near = sorted(near, key=lambda s: -reach[s])

    def send_sum(part, send_sem, recv_sem):
        for dz, dx in near:
            dev = (lax.rem(z + dz, NZ) * NX + lax.rem(x + dx, NX), rcv)
            remote(part, part, send_sem, recv_sem, dev).start()

    def send_to_sums(t, part, landing, send_sem, recv_sem):
        for end in range(2):
            owner = lax.rem(t + 4 * end, NZ) * NX + c + 2 * end

            @pl.when(owner != src)
            def _():
                remote(part, landing.at[src], send_sem, recv_sem, (owner, rcv)).start()

    def reduce_src(it):
        part = (coef(0) * acc[1] + coef(1) * acc[0]).astype(BF16)
        for half in range(2):
            ar_s[it, 3 * half:3 * half + 3] = part[:, 128 * half:128 * half + 128].reshape(3, 16, 128)

        def send(t, carry):
            send_to_sums(t, ar_s.at[it, t], ar_in.at[it], a1_send.at[it], a1_recv.at[it])
            return carry

        lax.fori_loop(0, TILES, send, 0)
        if it == 1:
            sc_s[...] = sum_scalars(0)
            send_to_sums(TILES, sc_s, sc_in, s1_send, s1_recv)

            @pl.when(sums_scalars)
            def _():
                sc_in[src] = sc_s[...]
                wait_recv(sc_in.at[pl.ds(0, N_SRC - 1)], s1_recv)
                sc_out[...] = jnp.sum(sc_in[...], axis=0)
                send_sum(sc_out, s2_send, s2_recv)

        @pl.when(sums_tile)
        def _():
            ar_in[it, src] = ar_s[it, tile]
            wait_recv(ar_in.at[it, pl.ds(0, N_SRC - 1)], a1_recv.at[it])
            ar_out[it, tile] = jnp.sum(ar_in[it].astype(F32), axis=0).astype(BF16)
            send_sum(ar_out.at[it, tile], a2_send.at[it], a2_recv.at[it])
            wait_recv(ar_out.at[it, pl.ds(0, TILES - 1)], a2_recv.at[it])

        @pl.when(jnp.logical_not(sums_tile))
        def _():
            wait_recv(ar_out.at[it, pl.ds(0, TILES)], a2_recv.at[it])

        if it == 1:
            pl.when(jnp.logical_not(sums_scalars))(lambda: wait_recv(sc_out, s2_recv))
        return jnp.concatenate(
            [ar_out[it, 3 * half:3 * half + 3].reshape(B, 128) for half in range(2)], axis=1).astype(F32)

    def finish_src(it):
        @pl.when(sums_tile)
        def _():
            wait_send(ar_in.at[it, pl.ds(0, len(near))], a2_send.at[it])
            wait_send(ar_in.at[it, pl.ds(0, 2 * TILES - 1)], a1_send.at[it])

        @pl.when(jnp.logical_not(sums_tile))
        def _():
            wait_send(ar_in.at[it, pl.ds(0, 2 * TILES)], a1_send.at[it])

        if it == 1:
            @pl.when(sums_scalars)
            def _():
                wait_send(sc_in.at[pl.ds(0, len(near))], s2_send)
                wait_send(sc_in.at[pl.ds(0, 1)], s1_send)

            @pl.when(jnp.logical_not(sums_scalars))
            def _():
                wait_send(sc_in.at[pl.ds(0, 2)], s1_send)

    def share_scalars(it, row):
        tb = (tb0, tb1)[it]
        tb[rcv] = row

        def send(i, carry):
            remote(tb.at[rcv], tb.at[rcv], t_send.at[it], t_recv.at[it],
                   (src, lax.rem(rcv + far(i, N_RCV), N_RCV))).start()
            return carry

        lax.fori_loop(0, N_RCV - 1, send, 0)

    def sum_scalars(it):
        tb = (tb0, tb1)[it]
        wait_recv(tb.at[pl.ds(0, N_RCV - 1)], t_recv.at[it])
        return jnp.sum(tb[...], axis=0)

    def scatter_sources(it, jv, scalars=None):
        w = (coef(1) * jv).astype(BF16)
        lift = coef(0) * jv
        high = jnp.concatenate([elb[0, 8:9, :], elb[1, 8:9, :]], axis=1)

        def part(d):
            q = chip(d)
            both = dot_nt(w, block(q))
            sparse = jnp.concatenate(
                [jnp.where(high == q * 2, lift, 0.0), jnp.where(high == q * 2 + 1, lift, 0.0)], axis=0)
            spread = dot_nt(sparse.astype(BF16), low[...])
            return both[:, :L] + spread[:B], both[:, L:] + spread[B:]

        def home(d):
            value = part(d)
            for h in range(2):
                slot = 2 * WAYS.index(d) + h
                landing = 2 * WAYS.index(d) + (h if it == 0 else c)
                rs_send[it, slot] = value[h].astype(BF16)
                remote(rs_send.at[it, slot], rs_fin.at[it, landing], rs_ssem.at[it], rf_recv.at[it, landing],
                       at_chip(d, c if it == 0 else h)).start()

        for d in WAYS[:5]:
            home(d)
        if scalars is not None:
            share_scalars(it, scalars())
        for d in WAYS[5:]:
            home(d)
        mine = part(0)
        own[it, 0] = mine[0]
        own[it, 1] = mine[1]
        if it == 1:
            remote(own.at[it, other], sib.at[it], sp_send.at[it], sp_recv.at[it], here).start()

    def arrivals(it, i):
        total = 0.0
        for way in range(len(WAYS)):
            slot = way * 2 + i
            wait_recv(rs_fin.at[it, slot], rf_recv.at[it, slot])
            total += rs_fin[it, slot].astype(F32)
        return total

    for load in loads:
        load.wait()
    tau, press = tr_ref[:, 0, :], tr_ref[:, 1, :]
    opening, state = op_ref[...], st_ref[...]
    radius = jnp.sqrt(opening * opening + press * press + 0.5)
    a_n = 1.0 - opening / radius
    b_n = 1.0 - press / radius
    ratio = jnp.abs(tau) / (1.0 + 0.6 * jnp.abs(press))
    a_s = jnp.where(state == 0, 1.0, jnp.where(state == 1, ratio, 0.0))
    b_s = jnp.where(state == 0, ratio, 1.0)
    co[c, 0] = jnp.where(c == 0, a_s, a_n)
    co[c, 1] = jnp.where(c == 0, b_s, b_n)
    co_send[0] = jnp.where(c == 0, a_n, a_s)
    co_send[1] = jnp.where(c == 0, b_n, b_s)
    elb[c, :8, :] = jnp.broadcast_to(el_ref[...], (8, 128))
    co_share = remote(co_send, co.at[c], sib_send.at[0], sib_recv.at[0], here)
    co_share.start()
    el_share = remote(elb.at[c, pl.ds(0, 8)], elb.at[c, pl.ds(0, 8)], sib_send.at[1], sib_recv.at[1], here)
    el_share.start()
    for d in ORDER[:5]:
        share_k(d)
    first_sends(1)
    acc[...] = jnp.zeros((2, B, 256), F32)
    wait_recv(elb.at[other, pl.ds(0, 8)], sib_recv.at[1])
    for d in ORDER[5:]:
        share_k(d)
    place = jnp.concatenate([elb[0, 0:1, :], elb[1, 0:1, :]], axis=1) - src * (NY * 2 * L)
    low[...] = jnp.where(
        lax.broadcasted_iota(jnp.int32, (L, 256), 0) == (place & (L - 1)), 1.0, 0.0).astype(BF16)
    high = place >> 8
    elb[0, 8:, :] = jnp.broadcast_to(high[:, :128], (8, 128))
    elb[1, 8:, :] = jnp.broadcast_to(high[:, 128:], (8, 128))

    def add_all(it):
        if it == 0:
            arrived(it, 0, other)
        add_chip(it, 0)
        for d in ORDER[1:]:
            arrived(it, d, 0)
            arrived(it, d, 1)
            add_chip(it, d)

    add_all(0)
    wait_recv(co.at[other], sib_recv.at[0])
    jv = reduce_src(0)
    j0[...] = jv
    scatter_sources(0, jv)
    gp_row = row_of(jv * jv)

    pp = 0.0
    for h in range(2):
        p = own[0, h] + arrivals(0, h)
        pown[h] = p
        pp += p * p
        part = gat.at[1, y * 2 + h]
        part[...] = p.astype(BF16)
        for d in WAYS:
            remote(part, part, ag_send.at[1], ag_recv.at[1, y * 2 + h], at_chip(d, c)).start()
    remote(pown.at[other], sib.at[0], sp_send.at[0], sp_recv.at[0], here).start()
    pp_row = row_of(pp)
    share_scalars(0, jnp.concatenate([gg_row, pp_row, gp_row * (1.0 / N_SRC)], axis=1))
    acc[...] = jnp.zeros((2, B, 256), F32)
    add_all(1)
    jp = reduce_src(1)
    sums = sc_out[...]
    gg, pp, gp = sums[:, :128], sums[:, 128:256], sums[:, 256:]
    alpha0 = gg / (0.5 * gg + gp)
    left = gp / (0.5 * gg + gp)
    rr = alpha0 * (alpha0 * pp - left * gp)
    beta = rr / gg
    scale = left + beta
    alpha0_c, left_c, scale_c = col_of(alpha0), col_of(left), col_of(scale)
    jv = scale_c * j0[...] - alpha0_c * jp
    scatter_sources(1, jv, lambda: row_of(jv * jv))
    jj = sum_scalars(1)
    alpha1 = rr / (0.5 * rr * (1.0 + beta) + jj)
    alpha1_c = col_of(alpha1)
    wait_recv(sib.at[0], sp_recv.at[0])
    base = []
    for comp in range(2):
        gv = g_ref[:, comp, :]
        pv = jnp.where(c == comp, pown[c], sib[0])
        direction = scale_c * gv - alpha0_c * pv
        x_ref[:, comp, :] = alpha0_c * gv + alpha1_c * direction
        base.append(left_c * gv - alpha0_c * pv - alpha1_c * (0.5 * direction))
    wait_recv(sib.at[1], sp_recv.at[1])
    for comp in range(2):
        q = jnp.where(c == comp, own[1, c], sib[1]) + arrivals(1, comp)
        r_ref[:, comp, :] = base[comp] - alpha1_c * q

    co_share.wait_send()
    el_share.wait_send()
    wait_send(kw.at[c], kp_send)
    for it in range(2):
        wait_send(gat.at[it, pl.ds(0, 15 - it)], ag_send.at[it])
        wait_send(rs_send.at[it, pl.ds(0, 14)], rs_ssem.at[it])
        wait_send(own.at[it, 0], sp_send.at[it])
        wait_send((tb0, tb1)[it].at[pl.ds(0, N_RCV - 1)], t_send.at[it])
        finish_src(it)


def shards(stiffness, newton_rhs, traction, opening, state, elements):
    dma, vmem = pltpu.SemaphoreType.DMA, pltpu.VMEM
    out = jax.ShapeDtypeStruct((B, 2, L), F32)
    return pl.pallas_call(
        kernel,
        out_shape=(out, out),
        in_specs=[pl.BlockSpec(memory_space=pl.ANY)] * 6,
        out_specs=[pl.BlockSpec(memory_space=pltpu.VMEM)] * 2,
        scratch_shapes=[
            vmem((B, 2, L), F32),
            vmem((B, 2, 128), F32),
            vmem((B, 128), F32),
            vmem((B, 128), jnp.int32),
            vmem((1, 128), jnp.int32),
            vmem((2, NY * 2 * L, 128), BF16),
            vmem((NY * 2 * L, 128), BF16),
            vmem((L, 256), BF16),
            vmem((2, 16, 128), jnp.int32),
            vmem((2, 2, B, 128), F32),
            vmem((2, B, 128), F32),
            vmem((2, B, L), BF16),
            vmem((2, 16, B, L), BF16),
            vmem((2, B, 256), F32),
            vmem((B, 256), F32),
            vmem((2, TILES, 16, 128), BF16),
            vmem((2, N_SRC, 16, 128), BF16),
            vmem((2, TILES, 16, 128), BF16),
            vmem((1, 384), F32),
            vmem((N_SRC, 1, 384), F32),
            vmem((1, 384), F32),
            vmem((2, 16, B, L), BF16),
            vmem((2, 14, B, L), BF16),
            vmem((2, 2, B, L), F32),
            vmem((2, B, L), F32),
            vmem((2, B, L), F32),
            vmem((N_RCV, 1, 384), F32),
            vmem((N_RCV, 1, 128), F32),
            dma((NY,)), dma((NY,)), dma((B // 8,)), dma((4,)), dma((2,)), dma((2,)), dma, dma((NY,)),
            dma((2,)), dma((2, 16)), dma((2,)), dma((2, 14)),
            dma((2,)), dma((2,)), dma((2,)), dma((2,)), dma((2,)), dma((2,)), dma, dma, dma, dma, dma((2,)), dma((2,)),
        ],
        compiler_params=pltpu.CompilerParams(
            collective_id=0, has_side_effects=True, vmem_limit_bytes=24 * 1024 * 1024),
        cost_estimate=pl.CostEstimate(flops=8 * B * 4096 * 512, bytes_accessed=4 << 20, transcendentals=0),
    )(*(pltpu.with_memory_space_constraint(a, pltpu.HBM) for a in (
        stiffness, newton_rhs, traction, opening, state, elements.reshape(1, 128))))


def solution(mesh):
    placed = (
        P(None, "src", "rcv"),
        P(None, None, ("src", "rcv")),
        P(None, None, "rcv"),
        P(None, "rcv"),
        P(None, "rcv"),
        P("rcv"),
    )
    return jax.shard_map(
        shards,
        mesh=mesh,
        in_specs=placed,
        out_specs=(P(None, None, ("src", "rcv")), P(None, None, ("src", "rcv"))),
        check_vma=False,
    )
```

```python
import jax
import jax.numpy as jnp
from jax import lax
from jax.experimental import pallas as pl
from jax.experimental.pallas import tpu as pltpu
from jax.sharding import PartitionSpec as P

MESH = pl.DeviceIdType.MESH
F32 = jnp.float32
BF16 = jnp.bfloat16
B = 48
L = 256
NY = 8
N_RCV = 16
N_SRC = 32
NX = 4
NZ = 8
TILES = 6
ORDER = (0, 1, -1, 2, -2, 3, -3, 4)


def far(i, n):
    return n // 2 + (i + 1) // 2 * (2 * ((i + 1) % 2) - 1)


def dot_nt(a, b):
    return lax.dot_general(a, b, (((1,), (1,)), ((), ())), preferred_element_type=F32)


def kernel(k_hbm, g_hbm, tr_hbm, op_hbm, st_hbm, el_hbm, x_ref, r_ref,
           g_ref, tr_ref, op_ref, st_ref, el_ref,
           kw, k_own, low, elb, co, co_send, sb, gat, acc, j0, ar_s, ar_in, ar_out, sc_s, sc_in, sc_out,
           rs_send, rs_in, rs_fin, own, pown, sib, tb0, tb1,
           k_sem, ka_sem, g_sem, in_sem, sib_send, sib_recv, kp_send, kp_recv, ag_send, ag_recv, rs_ssem, rs_recv, rf_recv,
           sp_send, sp_recv, a1_send, a1_recv, a2_send, a2_recv,
           s1_send, s1_recv, s2_send, s2_recv, t_send, t_recv):
    src = lax.axis_index("src")
    rcv = lax.axis_index("rcv")
    y = rcv // 2
    c = lax.rem(rcv, 2)
    other = 1 - c

    def chip(d):
        return lax.rem(y + d + NY, NY)

    def at_chip(d, core):
        return (src, chip(d) * 2 + core)

    def remote(s, d, ss, rs, dev):
        return pltpu.make_async_remote_copy(
            src_ref=s, dst_ref=d, send_sem=ss, recv_sem=rs, device_id=dev, device_id_type=MESH)

    here = (src, y * 2 + other)

    def wait_recv(ref, sem):
        remote(ref, ref, sem, sem, here).wait_recv()

    def wait_send(ref, sem):
        remote(ref, ref, sem, sem, here).wait_send()

    g_loads = [
        pltpu.make_async_copy(g_hbm.at[pl.ds(8 * i, 8)], g_ref.at[pl.ds(8 * i, 8)], g_sem.at[i]) for i in range(B // 8)]
    for load in g_loads:
        load.start()
    loads = [
        pltpu.make_async_copy(a, b, in_sem.at[i])
        for i, (a, b) in enumerate((
            (tr_hbm, tr_ref), (op_hbm, op_ref), (st_hbm, st_ref), (el_hbm, el_ref)))
    ]
    for load in loads:
        load.start()

    barrier = pltpu.get_barrier_semaphore()

    def greet(dev):
        pl.semaphore_signal(barrier, inc=1, device_id=dev, device_id_type=MESH)

    def greet_src(i):
        greet((lax.rem(src + far(i, N_SRC), N_SRC), rcv))

    def greet_some(i, carry):
        greet((src, lax.rem(rcv + far(i, N_RCV), N_RCV)))
        greet_src(2 * i)
        greet_src(2 * i + 1)
        return carry

    lax.fori_loop(0, N_RCV - 1, greet_some, 0)
    greet_src(N_SRC - 2)

    def k_rows(d):
        return pl.ds(pl.multiple_of(chip(d) * (2 * L), 2 * L), 2 * L)

    def k_away(d):
        return pltpu.make_async_copy(k_hbm.at[other, k_rows(d)], k_own.at[k_rows(d)], ka_sem.at[chip(d)])

    def k_copy(d):
        return pltpu.make_async_copy(k_hbm.at[c, k_rows(d)], kw.at[c, k_rows(d)], k_sem.at[chip(d)])

    for d in ORDER:
        k_away(d).start()
        k_copy(d).start()

    lane = lax.broadcasted_iota(jnp.int32, (B, 128), 1)
    case = lax.broadcasted_iota(jnp.int32, (B, 128), 0)
    diag = lane == case

    def row_of(v):
        col = jnp.sum(v, axis=1, keepdims=True)
        return jnp.sum(jnp.where(diag, col, 0.0), axis=0, keepdims=True)

    def col_of(row):
        return jnp.sum(jnp.where(diag, row, 0.0), axis=1, keepdims=True)

    for load in g_loads:
        load.wait()
    g0, g1 = g_ref[:, 0, :], g_ref[:, 1, :]
    b0, b1 = g0.astype(BF16), g1.astype(BF16)
    sb[0] = b0
    sb[1] = b1
    gat[0, rcv] = jnp.where(c == 0, b0, b1)
    gg_row = row_of(g0 * g0 + g1 * g1)

    pl.semaphore_wait(barrier, N_RCV + N_SRC - 2)

    def first_sends(comp):
        for d in (2, -2, 1, -1):
            remote(sb.at[comp], gat.at[0, rcv], ag_send.at[0], ag_recv.at[0, rcv], at_chip(d, comp)).start()

        @pl.when(c != comp)
        def _():
            remote(sb.at[comp], gat.at[0, rcv], ag_send.at[0], ag_recv.at[0, rcv], here).start()

    first_sends(0)

    def share_k(d):
        k_away(d).wait()
        remote(k_own.at[k_rows(d)], kw.at[c, k_rows(d)], kp_send, kp_recv.at[chip(d)], here).start()

    def arrived(it, d, h):
        slot = chip(d) * 2 + h
        wait_recv(gat.at[it, slot], ag_recv.at[it, slot])

    def relay(it):
        for h in range(2):
            for d in (1, -1):
                arrived(it, -2 * d, h)
                slot = chip(-2 * d) * 2 + h
                part = gat.at[it, slot]
                if (d == 1) == (h == 0):
                    remote(part, part, ag_send.at[it], ag_recv.at[it, slot], at_chip(2 * d, c)).start()
                remote(part, part, ag_send.at[it], ag_recv.at[it, slot], at_chip(d, c)).start()

    def block(q):
        rows = pl.ds(pl.multiple_of(q * (2 * L), 2 * L), 2 * L)
        return jnp.concatenate([kw[0, rows, :], kw[1, rows, :]], axis=1)

    def high_bits():
        return jnp.concatenate([elb[0, 8:9, :], elb[1, 8:9, :]], axis=1)

    def add_chips(it, ds):
        if it == 0:
            for d in ds:
                k_copy(d).wait()
                wait_recv(kw.at[other, k_rows(d)], kp_recv.at[chip(d)])
        slots = [chip(d) * 2 + h for d in ds for h in range(2)]
        parts = [gat[it, slot] for slot in slots]
        stiff = jnp.concatenate([block(chip(d)) for d in ds], axis=0)
        acc[0] += jnp.dot(jnp.concatenate(parts, axis=1), stiff, preferred_element_type=F32)
        ed = jnp.dot(jnp.concatenate(parts, axis=0), low[...], preferred_element_type=F32)
        high = high_bits()
        acc[1] += sum(jnp.where(high == slot, ed[B * k:B * k + B], 0.0) for k, slot in enumerate(slots))

    def coef(i):
        return jnp.concatenate([co[0, i], co[1, i]], axis=1)

    z = src // NX
    x = lax.rem(src, NX)
    tile = lax.rem(z + 4 * (x // 2), NZ)
    sums_tile = (lax.rem(x, 2) == c) & (tile < TILES)
    sums_scalars = (lax.rem(x, 2) == c) & (tile == TILES)
    steps = [(dz, dx) for dz in range(NZ) for dx in range(NX)]
    reach = {(dz, dx): min(dz, NZ - dz) + min(dx, NX - dx) for dz, dx in steps}
    near = [s for s in steps if 0 < reach[s] < 3 or (reach[s] == 3 and 0 < s[0] < 4)]
    near = sorted(near, key=lambda s: -reach[s])

    def send_sum(part, send_sem, recv_sem):
        for dz, dx in near:
            dev = (lax.rem(z + dz, NZ) * NX + lax.rem(x + dx, NX), rcv)
            remote(part, part, send_sem, recv_sem, dev).start()

    def send_to_sums(t, part, landing, send_sem, recv_sem):
        for end in range(2):
            owner = lax.rem(t + 4 * end, NZ) * NX + c + 2 * end

            @pl.when(owner != src)
            def _():
                remote(part, landing.at[src], send_sem, recv_sem, (owner, rcv)).start()

    def reduce_src(it):
        part = (coef(0) * acc[1] + coef(1) * acc[0]).astype(BF16)
        for half in range(2):
            ar_s[it, 3 * half:3 * half + 3] = part[:, 128 * half:128 * half + 128].reshape(3, 16, 128)

        def send(t, carry):
            send_to_sums(t, ar_s.at[it, t], ar_in.at[it], a1_send.at[it], a1_recv.at[it])
            return carry

        lax.fori_loop(0, TILES, send, 0)
        if it == 1:
            sc_s[...] = sum_scalars(0)
            send_to_sums(TILES, sc_s, sc_in, s1_send, s1_recv)

            @pl.when(sums_scalars)
            def _():
                sc_in[src] = sc_s[...]
                wait_recv(sc_in.at[pl.ds(0, N_SRC - 1)], s1_recv)
                sc_out[...] = jnp.sum(sc_in[...], axis=0)
                send_sum(sc_out, s2_send, s2_recv)

        @pl.when(sums_tile)
        def _():
            ar_in[it, src] = ar_s[it, tile]
            wait_recv(ar_in.at[it, pl.ds(0, N_SRC - 1)], a1_recv.at[it])
            ar_out[it, tile] = jnp.sum(ar_in[it].astype(F32), axis=0).astype(BF16)
            send_sum(ar_out.at[it, tile], a2_send.at[it], a2_recv.at[it])
            wait_recv(ar_out.at[it, pl.ds(0, TILES - 1)], a2_recv.at[it])

        @pl.when(jnp.logical_not(sums_tile))
        def _():
            wait_recv(ar_out.at[it, pl.ds(0, TILES)], a2_recv.at[it])

        if it == 1:
            pl.when(jnp.logical_not(sums_scalars))(lambda: wait_recv(sc_out, s2_recv))
        return jnp.concatenate(
            [ar_out[it, 3 * half:3 * half + 3].reshape(B, 128) for half in range(2)], axis=1).astype(F32)

    def finish_src(it):
        @pl.when(sums_tile)
        def _():
            wait_send(ar_in.at[it, pl.ds(0, len(near))], a2_send.at[it])
            wait_send(ar_in.at[it, pl.ds(0, 2 * TILES - 1)], a1_send.at[it])

        @pl.when(jnp.logical_not(sums_tile))
        def _():
            wait_send(ar_in.at[it, pl.ds(0, 2 * TILES)], a1_send.at[it])

        if it == 1:
            @pl.when(sums_scalars)
            def _():
                wait_send(sc_in.at[pl.ds(0, len(near))], s2_send)
                wait_send(sc_in.at[pl.ds(0, 1)], s1_send)

            @pl.when(jnp.logical_not(sums_scalars))
            def _():
                wait_send(sc_in.at[pl.ds(0, 2)], s1_send)

    def share_scalars(it, row):
        tb = (tb0, tb1)[it]
        tb[rcv] = row

        def send(i, carry):
            remote(tb.at[rcv], tb.at[rcv], t_send.at[it], t_recv.at[it],
                   (src, lax.rem(rcv + far(i, N_RCV), N_RCV))).start()
            return carry

        lax.fori_loop(0, N_RCV - 1, send, 0)

    def sum_scalars(it):
        tb = (tb0, tb1)[it]
        wait_recv(tb.at[pl.ds(0, N_RCV - 1)], t_recv.at[it])
        return jnp.sum(tb[...], axis=0)

    def scatter_sources(it, jv, scalars=None):
        w = (coef(1) * jv).astype(BF16)
        lift = coef(0) * jv
        high = high_bits()

        def parts(ds):
            slots = [chip(d) * 2 + h for d in ds for h in range(2)]
            both = dot_nt(w, jnp.concatenate([block(chip(d)) for d in ds], axis=0))
            sparse = jnp.concatenate([jnp.where(high == slot, lift, 0.0) for slot in slots], axis=0)
            spread = dot_nt(sparse.astype(BF16), low[...])
            sums = [both[:, L * k:L * k + L] + spread[B * k:B * k + B] for k in range(len(slots))]
            return [sums[2 * k:2 * k + 2] for k in range(len(ds))]

        def send(slot, value, to, landing):
            rs_send[it, slot] = value.astype(BF16)
            remote(rs_send.at[it, slot], rs_in.at[it, landing], rs_ssem.at[it], rs_recv.at[it, landing],
                   at_chip(to, c)).start()

        def home(slot, value, d, h):
            rs_send[it, slot] = value.astype(BF16)
            landing = {1: 0, -1: 2, 2: 4, -2: 6}[d] + (h if it == 0 else c)
            remote(rs_send.at[it, slot], rs_fin.at[it, landing], rs_ssem.at[it], rf_recv.at[it, landing],
                   at_chip(d, c if it == 0 else h)).start()

        def came(landing):
            wait_recv(rs_in.at[it, landing], rs_recv.at[it, landing])
            return rs_in[it, landing].astype(F32)

        four, three, minus_three = parts((4, 3, -3))
        send(0, four[0], 2, 0)
        send(1, four[1], -2, 1)
        for k, (d, value) in enumerate(((1, three), (-1, minus_three))):
            send(2 + 2 * k, value[0], d, 2 + 2 * k)
            send(3 + 2 * k, value[1], d, 3 + 2 * k)
        one, minus_one, up, down, mine = parts((1, -1, 2, -2, 0))
        for k, (d, value) in enumerate(((1, one), (-1, minus_one))):
            home(6 + 2 * k, value[0], d, 0)
            home(7 + 2 * k, value[1], d, 1)
        own[it, 0] = mine[0]
        own[it, 1] = mine[1]
        if it == 1:
            remote(own.at[it, other], sib.at[it], sp_send.at[it], sp_recv.at[it], here).start()
        if scalars is not None:
            share_scalars(it, scalars())
        home(10, up[1] + came(3), 2, 1)
        home(11, down[0] + came(4), -2, 0)
        home(12, up[0] + came(2) + came(0), 2, 0)
        home(13, down[1] + came(5) + came(1), -2, 1)

    def arrivals(it, i):
        total = 0.0
        for way in range(4):
            slot = way * 2 + i
            wait_recv(rs_fin.at[it, slot], rf_recv.at[it, slot])
            total += rs_fin[it, slot].astype(F32)
        return total

    for load in loads:
        load.wait()
    tau, press = tr_ref[:, 0, :], tr_ref[:, 1, :]
    opening, state = op_ref[...], st_ref[...]
    radius = jnp.sqrt(opening * opening + press * press + 0.5)
    a_n = 1.0 - opening / radius
    b_n = 1.0 - press / radius
    ratio = jnp.abs(tau) / (1.0 + 0.6 * jnp.abs(press))
    a_s = jnp.where(state == 0, 1.0, jnp.where(state == 1, ratio, 0.0))
    b_s = jnp.where(state == 0, ratio, 1.0)
    co[c, 0] = jnp.where(c == 0, a_s, a_n)
    co[c, 1] = jnp.where(c == 0, b_s, b_n)
    co_send[0] = jnp.where(c == 0, a_n, a_s)
    co_send[1] = jnp.where(c == 0, b_n, b_s)
    elb[c, :8, :] = jnp.broadcast_to(el_ref[...], (8, 128))
    co_share = remote(co_send, co.at[c], sib_send.at[0], sib_recv.at[0], here)
    co_share.start()
    el_share = remote(elb.at[c, pl.ds(0, 8)], elb.at[c, pl.ds(0, 8)], sib_send.at[1], sib_recv.at[1], here)
    el_share.start()
    for d in ORDER[:5]:
        share_k(d)
    first_sends(1)
    acc[...] = jnp.zeros((2, B, 256), F32)
    wait_recv(elb.at[other, pl.ds(0, 8)], sib_recv.at[1])
    for d in ORDER[5:]:
        share_k(d)
    place = jnp.concatenate([elb[0, 0:1, :], elb[1, 0:1, :]], axis=1) - src * (NY * 2 * L)
    low[...] = jnp.where(
        lax.broadcasted_iota(jnp.int32, (L, 256), 0) == (place & (L - 1)), 1.0, 0.0).astype(BF16)
    high = place >> 8
    elb[0, 8:, :] = jnp.broadcast_to(high[:, :128], (8, 128))
    elb[1, 8:, :] = jnp.broadcast_to(high[:, 128:], (8, 128))

    relay(0)

    def add_all(it):
        if it == 0:
            arrived(it, 0, other)
        for d in (1, -1):
            arrived(it, d, 0)
            arrived(it, d, 1)
        add_chips(it, ORDER[:5])
        for d in ORDER[5:]:
            arrived(it, d, 0)
            arrived(it, d, 1)
        add_chips(it, ORDER[5:])

    add_all(0)
    wait_recv(co.at[other], sib_recv.at[0])
    jv = reduce_src(0)
    j0[...] = jv
    scatter_sources(0, jv)
    gp_row = row_of(jv * jv)

    pp = 0.0
    for h in range(2):
        p = own[0, h] + arrivals(0, h)
        pown[h] = p
        pp += p * p
        part = gat.at[1, y * 2 + h]
        part[...] = p.astype(BF16)
        for d in (2, -2):
            remote(part, part, ag_send.at[1], ag_recv.at[1, y * 2 + h], at_chip(d, c)).start()
    for h in range(2):
        part = gat.at[1, y * 2 + h]
        for d in (1, -1):
            remote(part, part, ag_send.at[1], ag_recv.at[1, y * 2 + h], at_chip(d, c)).start()
    remote(pown.at[other], sib.at[0], sp_send.at[0], sp_recv.at[0], here).start()
    pp_row = row_of(pp)
    share_scalars(0, jnp.concatenate([gg_row, pp_row, gp_row * (1.0 / N_SRC)], axis=1))
    acc[...] = jnp.zeros((2, B, 256), F32)
    relay(1)
    add_all(1)
    jp = reduce_src(1)
    sums = sc_out[...]
    gg, pp, gp = sums[:, :128], sums[:, 128:256], sums[:, 256:]
    alpha0 = gg / (0.5 * gg + gp)
    left = gp / (0.5 * gg + gp)
    rr = alpha0 * (alpha0 * pp - left * gp)
    beta = rr / gg
    scale = left + beta
    alpha0_c, left_c, scale_c = col_of(alpha0), col_of(left), col_of(scale)
    jv = scale_c * j0[...] - alpha0_c * jp
    scatter_sources(1, jv, lambda: row_of(jv * jv))
    jj = sum_scalars(1)
    alpha1 = rr / (0.5 * rr * (1.0 + beta) + jj)
    alpha1_c = col_of(alpha1)
    wait_recv(sib.at[0], sp_recv.at[0])
    base = []
    for comp in range(2):
        gv = g_ref[:, comp, :]
        pv = jnp.where(c == comp, pown[c], sib[0])
        direction = scale_c * gv - alpha0_c * pv
        x_ref[:, comp, :] = alpha0_c * gv + alpha1_c * direction
        base.append(left_c * gv - alpha0_c * pv - alpha1_c * (0.5 * direction))
    wait_recv(sib.at[1], sp_recv.at[1])
    for comp in range(2):
        q = jnp.where(c == comp, own[1, c], sib[1]) + arrivals(1, comp)
        r_ref[:, comp, :] = base[comp] - alpha1_c * q

    co_share.wait_send()
    el_share.wait_send()
    wait_send(kw.at[c], kp_send)
    for it in range(2):
        wait_send(gat.at[it, pl.ds(0, 15 - it)], ag_send.at[it])
        wait_send(rs_send.at[it, pl.ds(0, 14)], rs_ssem.at[it])
        wait_send(own.at[it, 0], sp_send.at[it])
        wait_send((tb0, tb1)[it].at[pl.ds(0, N_RCV - 1)], t_send.at[it])
        finish_src(it)


def shards(stiffness, newton_rhs, traction, opening, state, elements):
    dma, vmem = pltpu.SemaphoreType.DMA, pltpu.VMEM
    out = jax.ShapeDtypeStruct((B, 2, L), F32)
    return pl.pallas_call(
        kernel,
        out_shape=(out, out),
        in_specs=[pl.BlockSpec(memory_space=pl.ANY)] * 6,
        out_specs=[pl.BlockSpec(memory_space=pltpu.VMEM)] * 2,
        scratch_shapes=[
            vmem((B, 2, L), F32),
            vmem((B, 2, 128), F32),
            vmem((B, 128), F32),
            vmem((B, 128), jnp.int32),
            vmem((1, 128), jnp.int32),
            vmem((2, NY * 2 * L, 128), BF16),
            vmem((NY * 2 * L, 128), BF16),
            vmem((L, 256), BF16),
            vmem((2, 16, 128), jnp.int32),
            vmem((2, 2, B, 128), F32),
            vmem((2, B, 128), F32),
            vmem((2, B, L), BF16),
            vmem((2, 16, B, L), BF16),
            vmem((2, B, 256), F32),
            vmem((B, 256), F32),
            vmem((2, TILES, 16, 128), BF16),
            vmem((2, N_SRC, 16, 128), BF16),
            vmem((2, TILES, 16, 128), BF16),
            vmem((1, 384), F32),
            vmem((N_SRC, 1, 384), F32),
            vmem((1, 384), F32),
            vmem((2, 16, B, L), BF16),
            vmem((2, 6, B, L), BF16),
            vmem((2, 8, B, L), BF16),
            vmem((2, 2, B, L), F32),
            vmem((2, B, L), F32),
            vmem((2, B, L), F32),
            vmem((N_RCV, 1, 384), F32),
            vmem((N_RCV, 1, 128), F32),
            dma((NY,)), dma((NY,)), dma((B // 8,)), dma((4,)), dma((2,)), dma((2,)), dma, dma((NY,)),
            dma((2,)), dma((2, 16)), dma((2,)), dma((2, 6)), dma((2, 8)),
            dma((2,)), dma((2,)), dma((2,)), dma((2,)), dma((2,)), dma((2,)), dma, dma, dma, dma, dma((2,)), dma((2,)),
        ],
        compiler_params=pltpu.CompilerParams(
            collective_id=0, has_side_effects=True, vmem_limit_bytes=24 * 1024 * 1024),
        cost_estimate=pl.CostEstimate(flops=8 * B * 4096 * 512, bytes_accessed=4 << 20, transcendentals=0),
    )(*(pltpu.with_memory_space_constraint(a, pltpu.HBM) for a in (
        stiffness, newton_rhs, traction, opening, state, elements.reshape(1, 128))))


def solution(mesh):
    placed = (
        P(None, "src", "rcv"),
        P(None, None, ("src", "rcv")),
        P(None, None, "rcv"),
        P(None, "rcv"),
        P(None, "rcv"),
        P("rcv"),
    )
    return jax.shard_map(
        shards,
        mesh=mesh,
        in_specs=placed,
        out_specs=(P(None, None, ("src", "rcv")), P(None, None, ("src", "rcv"))),
        check_vma=False,
    )
```

```python
import jax
import jax.numpy as jnp
from jax import lax
from jax.experimental import pallas as pl
from jax.experimental.pallas import tpu as pltpu
from jax.sharding import PartitionSpec as P

MESH = pl.DeviceIdType.MESH
F32 = jnp.float32
BF16 = jnp.bfloat16
B = 48
L = 256
NY = 8
N_RCV = 16
N_SRC = 32
NX = 4
NZ = 8
TILES = 6
ORDER = (0, 1, -1, 2, -2, 3, -3, 4)


def far(i, n):
    return n // 2 + (i + 1) // 2 * (2 * ((i + 1) % 2) - 1)


def dot_nt(a, b):
    return lax.dot_general(a, b, (((1,), (1,)), ((), ())), preferred_element_type=F32)


def kernel(k_hbm, g_hbm, tr_hbm, op_hbm, st_hbm, el_hbm, x_ref, r_ref,
           g_ref, g_own, tr_ref, op_ref, st_ref, el_ref,
           kw, k_own, low, elb, co, co_send, sb, gat, acc, j0, ar_s, ar_in, ar_out, sc_s, sc_in, sc_out,
           rs_send, rs_in, rs_fin, own, pown, sib, tb0, tb1,
           k_sem, ka_sem, g_sem, in_sem, sib_send, sib_recv, kp_send, kp_recv, ag_send, ag_recv, rs_ssem, rs_recv, rf_recv,
           sp_send, sp_recv, a1_send, a1_recv, a2_send, a2_recv,
           s1_send, s1_recv, s2_send, s2_recv, t_send, t_recv):
    src = lax.axis_index("src")
    rcv = lax.axis_index("rcv")
    y = rcv // 2
    c = lax.rem(rcv, 2)
    other = 1 - c

    z = src // NX
    x = lax.rem(src, NX)
    tile = lax.rem(z + 4 * (x // 2), NZ)
    sums_tile = (lax.rem(x, 2) == c) & (tile < TILES)
    sums_scalars = (lax.rem(x, 2) == c) & (tile == TILES)
    sums = (lax.rem(x, 2) == c) & (tile <= TILES)

    def chip(d):
        return lax.rem(y + d + NY, NY)

    def at_chip(d, core):
        return (src, chip(d) * 2 + core)

    def remote(s, d, ss, rs, dev):
        return pltpu.make_async_remote_copy(
            src_ref=s, dst_ref=d, send_sem=ss, recv_sem=rs, device_id=dev, device_id_type=MESH)

    here = (src, y * 2 + other)

    def wait_recv(ref, sem):
        remote(ref, ref, sem, sem, here).wait_recv()

    def wait_send(ref, sem):
        remote(ref, ref, sem, sem, here).wait_send()

    g_loads = [
        pltpu.make_async_copy(g_hbm.at[pl.ds(8 * i, 8)], g_ref.at[pl.ds(8 * i, 8)], g_sem.at[i]) for i in range(B // 8)]
    for load in g_loads:
        load.start()
    loads = [
        pltpu.make_async_copy(a, b, in_sem.at[i])
        for i, (a, b) in enumerate((
            (tr_hbm, tr_ref), (op_hbm, op_ref), (st_hbm, st_ref), (el_hbm, el_ref)))
    ]
    for load in loads:
        load.start()

    barrier = pltpu.get_barrier_semaphore()

    def greet(dev):
        pl.semaphore_signal(barrier, inc=1, device_id=dev, device_id_type=MESH)

    def greet_src(i):
        to = lax.rem(src + far(i, N_SRC), N_SRC)
        to_z, to_x = to // NX, lax.rem(to, NX)
        to_sums = (lax.rem(to_x, 2) == c) & (lax.rem(to_z + 4 * (to_x // 2), NZ) <= TILES)
        pl.when(sums | to_sums)(lambda: greet((to, rcv)))

    def greet_some(i, carry):
        greet((src, lax.rem(rcv + far(i, N_RCV), N_RCV)))
        greet_src(2 * i)
        greet_src(2 * i + 1)
        return carry

    lax.fori_loop(0, N_RCV - 1, greet_some, 0)
    greet_src(N_SRC - 2)

    def k_rows(d):
        return pl.ds(pl.multiple_of(chip(d) * (2 * L), 2 * L), 2 * L)

    def k_away(d):
        return pltpu.make_async_copy(k_hbm.at[other, k_rows(d)], k_own.at[k_rows(d)], ka_sem.at[chip(d)])

    def k_copy(d):
        return pltpu.make_async_copy(k_hbm.at[c, k_rows(d)], kw.at[c, k_rows(d)], k_sem.at[chip(d)])

    for d in ORDER:
        k_away(d).start()
        k_copy(d).start()

    lane = lax.broadcasted_iota(jnp.int32, (B, 128), 1)
    case = lax.broadcasted_iota(jnp.int32, (B, 128), 0)
    diag = lane == case

    def row_of(v):
        col = jnp.sum(v, axis=1, keepdims=True)
        return jnp.sum(jnp.where(diag, col, 0.0), axis=0, keepdims=True)

    def col_of(row):
        return jnp.sum(jnp.where(diag, row, 0.0), axis=1, keepdims=True)

    for load in g_loads:
        load.wait()
    g0, g1 = g_ref[:, 0, :], g_ref[:, 1, :]
    g_own[0] = g0
    g_own[1] = g1
    b0, b1 = g0.astype(BF16), g1.astype(BF16)
    sb[0] = b0
    sb[1] = b1
    gat[0, rcv] = jnp.where(c == 0, b0, b1)
    gg_row = row_of(g0 * g0 + g1 * g1)

    pl.when(sums)(lambda: pl.semaphore_wait(barrier, N_RCV + N_SRC - 2))
    pl.when(jnp.logical_not(sums))(lambda: pl.semaphore_wait(barrier, N_RCV - 1 + 2 * (TILES + 1)))

    def first_sends(comp):
        for d in (2, -2, 1, -1):
            remote(sb.at[comp], gat.at[0, rcv], ag_send.at[0], ag_recv.at[0, rcv], at_chip(d, comp)).start()

        @pl.when(c != comp)
        def _():
            remote(sb.at[comp], gat.at[0, rcv], ag_send.at[0], ag_recv.at[0, rcv], here).start()

    first_sends(0)

    def share_k(d):
        k_away(d).wait()
        remote(k_own.at[k_rows(d)], kw.at[c, k_rows(d)], kp_send, kp_recv.at[chip(d)], here).start()

    def arrived(it, d, h):
        slot = chip(d) * 2 + h
        wait_recv(gat.at[it, slot], ag_recv.at[it, slot])

    def relay(it):
        for h in range(2):
            for d in (1, -1):
                arrived(it, -2 * d, h)
                slot = chip(-2 * d) * 2 + h
                part = gat.at[it, slot]
                if (d == 1) == (h == 0):
                    remote(part, part, ag_send.at[it], ag_recv.at[it, slot], at_chip(2 * d, c)).start()
                remote(part, part, ag_send.at[it], ag_recv.at[it, slot], at_chip(d, c)).start()

    def block(q):
        rows = pl.ds(pl.multiple_of(q * (2 * L), 2 * L), 2 * L)
        return jnp.concatenate([kw[0, rows, :], kw[1, rows, :]], axis=1)

    def high_bits():
        return jnp.concatenate([elb[0, 8:9, :], elb[1, 8:9, :]], axis=1)

    def add_chips(it, ds):
        if it == 0:
            for d in ds:
                k_copy(d).wait()
                wait_recv(kw.at[other, k_rows(d)], kp_recv.at[chip(d)])
        slots = [chip(d) * 2 + h for d in ds for h in range(2)]
        parts = [gat[it, slot] for slot in slots]
        stiff = jnp.concatenate([block(chip(d)) for d in ds], axis=0)
        acc[0] += jnp.dot(jnp.concatenate(parts, axis=1), stiff, preferred_element_type=F32)
        ed = jnp.dot(jnp.concatenate(parts, axis=0), low[...], preferred_element_type=F32)
        high = high_bits()
        acc[1] += sum(jnp.where(high == slot, ed[B * k:B * k + B], 0.0) for k, slot in enumerate(slots))

    def coef(i):
        return jnp.concatenate([co[0, i], co[1, i]], axis=1)

    steps = [(dz, dx) for dz in range(NZ) for dx in range(NX)]
    reach = {(dz, dx): min(dz, NZ - dz) + min(dx, NX - dx) for dz, dx in steps}
    near = [s for s in steps if 0 < reach[s] < 3 or (reach[s] == 3 and 0 < s[0] < 4)]
    near = sorted(near, key=lambda s: -reach[s])

    def send_sum(part, send_sem, recv_sem):
        for dz, dx in near:
            dev = (lax.rem(z + dz, NZ) * NX + lax.rem(x + dx, NX), rcv)
            remote(part, part, send_sem, recv_sem, dev).start()

    def send_to_sums(t, part, landing, send_sem, recv_sem):
        for end in range(2):
            owner = lax.rem(t + 4 * end, NZ) * NX + c + 2 * end

            @pl.when(owner != src)
            def _():
                remote(part, landing.at[src], send_sem, recv_sem, (owner, rcv)).start()

    def reduce_src(it):
        part = (coef(0) * acc[1] + coef(1) * acc[0]).astype(BF16)
        for half in range(2):
            ar_s[it, 3 * half:3 * half + 3] = part[:, 128 * half:128 * half + 128].reshape(3, 16, 128)

        def send(t, carry):
            send_to_sums(t, ar_s.at[it, t], ar_in.at[it], a1_send.at[it], a1_recv.at[it])
            return carry

        lax.fori_loop(0, TILES, send, 0)
        if it == 1:
            sc_s[...] = sum_scalars(0)
            send_to_sums(TILES, sc_s, sc_in, s1_send, s1_recv)

            @pl.when(sums_scalars)
            def _():
                sc_in[src] = sc_s[...]
                wait_recv(sc_in.at[pl.ds(0, N_SRC - 1)], s1_recv)
                sc_out[...] = jnp.sum(sc_in[...], axis=0)
                send_sum(sc_out, s2_send, s2_recv)

        @pl.when(sums_tile)
        def _():
            ar_in[it, src] = ar_s[it, tile]
            wait_recv(ar_in.at[it, pl.ds(0, N_SRC - 1)], a1_recv.at[it])
            ar_out[it, tile] = jnp.sum(ar_in[it].astype(F32), axis=0).astype(BF16)
            send_sum(ar_out.at[it, tile], a2_send.at[it], a2_recv.at[it])
            wait_recv(ar_out.at[it, pl.ds(0, TILES - 1)], a2_recv.at[it])

        @pl.when(jnp.logical_not(sums_tile))
        def _():
            wait_recv(ar_out.at[it, pl.ds(0, TILES)], a2_recv.at[it])

        if it == 1:
            pl.when(jnp.logical_not(sums_scalars))(lambda: wait_recv(sc_out, s2_recv))
        return jnp.concatenate(
            [ar_out[it, 3 * half:3 * half + 3].reshape(B, 128) for half in range(2)], axis=1).astype(F32)

    def finish_src(it):
        @pl.when(sums_tile)
        def _():
            wait_send(ar_in.at[it, pl.ds(0, len(near))], a2_send.at[it])
            wait_send(ar_in.at[it, pl.ds(0, 2 * TILES - 1)], a1_send.at[it])

        @pl.when(jnp.logical_not(sums_tile))
        def _():
            wait_send(ar_in.at[it, pl.ds(0, 2 * TILES)], a1_send.at[it])

        if it == 1:
            @pl.when(sums_scalars)
            def _():
                wait_send(sc_in.at[pl.ds(0, len(near))], s2_send)
                wait_send(sc_in.at[pl.ds(0, 1)], s1_send)

            @pl.when(jnp.logical_not(sums_scalars))
            def _():
                wait_send(sc_in.at[pl.ds(0, 2)], s1_send)

    def share_scalars(it, row):
        tb = (tb0, tb1)[it]
        tb[rcv] = row

        def send(i, carry):
            remote(tb.at[rcv], tb.at[rcv], t_send.at[it], t_recv.at[it],
                   (src, lax.rem(rcv + far(i, N_RCV), N_RCV))).start()
            return carry

        lax.fori_loop(0, N_RCV - 1, send, 0)

    def sum_scalars(it):
        tb = (tb0, tb1)[it]
        wait_recv(tb.at[pl.ds(0, N_RCV - 1)], t_recv.at[it])
        return jnp.sum(tb[...], axis=0)

    def scatter_sources(it, jv, scalars=None):
        w = (coef(1) * jv).astype(BF16)
        lift = coef(0) * jv
        high = high_bits()

        def parts(ds):
            slots = [chip(d) * 2 + h for d in ds for h in range(2)]
            both = dot_nt(w, jnp.concatenate([block(chip(d)) for d in ds], axis=0))
            sparse = jnp.concatenate([jnp.where(high == slot, lift, 0.0) for slot in slots], axis=0)
            spread = dot_nt(sparse.astype(BF16), low[...])
            totals = [both[:, L * k:L * k + L] + spread[B * k:B * k + B] for k in range(len(slots))]
            return [totals[2 * k:2 * k + 2] for k in range(len(ds))]

        def send(slot, value, to, landing):
            rs_send[it, slot] = value.astype(BF16)
            remote(rs_send.at[it, slot], rs_in.at[it, landing], rs_ssem.at[it], rs_recv.at[it, landing],
                   at_chip(to, c)).start()

        def home(slot, value, d, h):
            rs_send[it, slot] = value.astype(BF16)
            landing = {1: 0, -1: 2, 2: 4, -2: 6}[d] + (h if it == 0 else c)
            remote(rs_send.at[it, slot], rs_fin.at[it, landing], rs_ssem.at[it], rf_recv.at[it, landing],
                   at_chip(d, c if it == 0 else h)).start()

        def came(landing):
            wait_recv(rs_in.at[it, landing], rs_recv.at[it, landing])
            return rs_in[it, landing].astype(F32)

        four, three, minus_three = parts((4, 3, -3))
        send(0, four[0], 2, 0)
        send(1, four[1], -2, 1)
        for k, (d, value) in enumerate(((1, three), (-1, minus_three))):
            send(2 + 2 * k, value[0], d, 2 + 2 * k)
            send(3 + 2 * k, value[1], d, 3 + 2 * k)
        one, minus_one, up, down, mine = parts((1, -1, 2, -2, 0))
        for k, (d, value) in enumerate(((1, one), (-1, minus_one))):
            home(6 + 2 * k, value[0], d, 0)
            home(7 + 2 * k, value[1], d, 1)
        own[it, 0] = mine[0]
        own[it, 1] = mine[1]
        if it == 1:
            remote(own.at[it, other], sib.at[it], sp_send.at[it], sp_recv.at[it], here).start()
        if scalars is not None:
            share_scalars(it, scalars())
        home(10, up[1] + came(3), 2, 1)
        home(11, down[0] + came(4), -2, 0)
        home(12, up[0] + came(2) + came(0), 2, 0)
        home(13, down[1] + came(5) + came(1), -2, 1)

    def arrivals(it, i):
        total = 0.0
        for way in range(4):
            slot = way * 2 + i
            wait_recv(rs_fin.at[it, slot], rf_recv.at[it, slot])
            total += rs_fin[it, slot].astype(F32)
        return total

    for d in ORDER[:5]:
        share_k(d)

    for load in loads:
        load.wait()
    tau, press = tr_ref[:, 0, :], tr_ref[:, 1, :]
    opening, state = op_ref[...], st_ref[...]
    radius = jnp.sqrt(opening * opening + press * press + 0.5)
    a_n = 1.0 - opening / radius
    b_n = 1.0 - press / radius
    ratio = jnp.abs(tau) / (1.0 + 0.6 * jnp.abs(press))
    a_s = jnp.where(state == 0, 1.0, jnp.where(state == 1, ratio, 0.0))
    b_s = jnp.where(state == 0, ratio, 1.0)
    co[c, 0] = jnp.where(c == 0, a_s, a_n)
    co[c, 1] = jnp.where(c == 0, b_s, b_n)
    co_send[0] = jnp.where(c == 0, a_n, a_s)
    co_send[1] = jnp.where(c == 0, b_n, b_s)
    elb[c, :8, :] = jnp.broadcast_to(el_ref[...], (8, 128))
    co_share = remote(co_send, co.at[c], sib_send.at[0], sib_recv.at[0], here)
    co_share.start()
    el_share = remote(elb.at[c, pl.ds(0, 8)], elb.at[c, pl.ds(0, 8)], sib_send.at[1], sib_recv.at[1], here)
    el_share.start()
    first_sends(1)
    acc[...] = jnp.zeros((2, B, 256), F32)
    wait_recv(elb.at[other, pl.ds(0, 8)], sib_recv.at[1])
    for d in ORDER[5:]:
        share_k(d)
    place = jnp.concatenate([elb[0, 0:1, :], elb[1, 0:1, :]], axis=1) - src * (NY * 2 * L)
    low[...] = jnp.where(
        lax.broadcasted_iota(jnp.int32, (L, 256), 0) == (place & (L - 1)), 1.0, 0.0).astype(BF16)
    high = place >> 8
    elb[0, 8:, :] = jnp.broadcast_to(high[:, :128], (8, 128))
    elb[1, 8:, :] = jnp.broadcast_to(high[:, 128:], (8, 128))

    relay(0)

    def add_all(it):
        if it == 0:
            arrived(it, 0, other)
        for d in (1, -1):
            arrived(it, d, 0)
            arrived(it, d, 1)
        add_chips(it, ORDER[:5])
        for d in ORDER[5:]:
            arrived(it, d, 0)
            arrived(it, d, 1)
        add_chips(it, ORDER[5:])

    add_all(0)
    wait_recv(co.at[other], sib_recv.at[0])
    jv = reduce_src(0)
    j0[...] = jv
    scatter_sources(0, jv)
    gp_row = row_of(jv * jv)

    pp = 0.0
    for h in range(2):
        p = own[0, h] + arrivals(0, h)
        pown[h] = p
        pp += p * p
        part = gat.at[1, y * 2 + h]
        part[...] = p.astype(BF16)
        for d in (2, -2):
            remote(part, part, ag_send.at[1], ag_recv.at[1, y * 2 + h], at_chip(d, c)).start()
    for h in range(2):
        part = gat.at[1, y * 2 + h]
        for d in (1, -1):
            remote(part, part, ag_send.at[1], ag_recv.at[1, y * 2 + h], at_chip(d, c)).start()
    remote(pown.at[other], sib.at[0], sp_send.at[0], sp_recv.at[0], here).start()
    pp_row = row_of(pp)
    share_scalars(0, jnp.concatenate([gg_row, pp_row, gp_row * (1.0 / N_SRC)], axis=1))
    acc[...] = jnp.zeros((2, B, 256), F32)
    relay(1)
    add_all(1)
    jp = reduce_src(1)
    sc = sc_out[...]
    gg, pp, gp = sc[:, :128], sc[:, 128:256], sc[:, 256:]
    alpha0 = gg / (0.5 * gg + gp)
    left = gp / (0.5 * gg + gp)
    rr = alpha0 * (alpha0 * pp - left * gp)
    beta = rr / gg
    scale = left + beta
    alpha0_c, left_c, scale_c = col_of(alpha0), col_of(left), col_of(scale)
    jv = scale_c * j0[...] - alpha0_c * jp
    scatter_sources(1, jv, lambda: row_of(jv * jv))
    jj = sum_scalars(1)
    alpha1 = rr / (0.5 * rr * (1.0 + beta) + jj)
    alpha1_c = col_of(alpha1)
    wait_recv(sib.at[0], sp_recv.at[0])
    base = []
    for comp in range(2):
        gv = g_own[comp]
        pv = jnp.where(c == comp, pown[c], sib[0])
        direction = scale_c * gv - alpha0_c * pv
        x_ref[:, comp, :] = alpha0_c * gv + alpha1_c * direction
        base.append(left_c * gv - alpha0_c * pv - alpha1_c * (0.5 * direction))
    wait_recv(sib.at[1], sp_recv.at[1])
    for comp in range(2):
        q = jnp.where(c == comp, own[1, c], sib[1]) + arrivals(1, comp)
        r_ref[:, comp, :] = base[comp] - alpha1_c * q

    co_share.wait_send()
    el_share.wait_send()
    wait_send(kw.at[c], kp_send)
    for it in range(2):
        wait_send(gat.at[it, pl.ds(0, 15 - it)], ag_send.at[it])
        wait_send(rs_send.at[it, pl.ds(0, 14)], rs_ssem.at[it])
        wait_send(own.at[it, 0], sp_send.at[it])
        wait_send((tb0, tb1)[it].at[pl.ds(0, N_RCV - 1)], t_send.at[it])
        finish_src(it)


def shards(stiffness, newton_rhs, traction, opening, state, elements):
    dma, vmem = pltpu.SemaphoreType.DMA, pltpu.VMEM
    out = jax.ShapeDtypeStruct((B, 2, L), F32)
    return pl.pallas_call(
        kernel,
        out_shape=(out, out),
        in_specs=[pl.BlockSpec(memory_space=pl.ANY)] * 6,
        out_specs=[pl.BlockSpec(memory_space=pltpu.VMEM)] * 2,
        scratch_shapes=[
            vmem((B, 2, L), F32),
            vmem((2, B, L), F32),
            vmem((B, 2, 128), F32),
            vmem((B, 128), F32),
            vmem((B, 128), jnp.int32),
            vmem((1, 128), jnp.int32),
            vmem((2, NY * 2 * L, 128), BF16),
            vmem((NY * 2 * L, 128), BF16),
            vmem((L, 256), BF16),
            vmem((2, 16, 128), jnp.int32),
            vmem((2, 2, B, 128), F32),
            vmem((2, B, 128), F32),
            vmem((2, B, L), BF16),
            vmem((2, 16, B, L), BF16),
            vmem((2, B, 256), F32),
            vmem((B, 256), F32),
            vmem((2, TILES, 16, 128), BF16),
            vmem((2, N_SRC, 16, 128), BF16),
            vmem((2, TILES, 16, 128), BF16),
            vmem((1, 384), F32),
            vmem((N_SRC, 1, 384), F32),
            vmem((1, 384), F32),
            vmem((2, 16, B, L), BF16),
            vmem((2, 6, B, L), BF16),
            vmem((2, 8, B, L), BF16),
            vmem((2, 2, B, L), F32),
            vmem((2, B, L), F32),
            vmem((2, B, L), F32),
            vmem((N_RCV, 1, 384), F32),
            vmem((N_RCV, 1, 128), F32),
            dma((NY,)), dma((NY,)), dma((B // 8,)), dma((4,)), dma((2,)), dma((2,)), dma, dma((NY,)),
            dma((2,)), dma((2, 16)), dma((2,)), dma((2, 6)), dma((2, 8)),
            dma((2,)), dma((2,)), dma((2,)), dma((2,)), dma((2,)), dma((2,)), dma, dma, dma, dma, dma((2,)), dma((2,)),
        ],
        compiler_params=pltpu.CompilerParams(
            collective_id=0, has_side_effects=True, vmem_limit_bytes=24 * 1024 * 1024),
        cost_estimate=pl.CostEstimate(flops=8 * B * 4096 * 512, bytes_accessed=4 << 20, transcendentals=0),
    )(*(pltpu.with_memory_space_constraint(a, pltpu.HBM) for a in (
        stiffness, newton_rhs, traction, opening, state, elements.reshape(1, 128))))


def solution(mesh):
    placed = (
        P(None, "src", "rcv"),
        P(None, None, ("src", "rcv")),
        P(None, None, "rcv"),
        P(None, "rcv"),
        P(None, "rcv"),
        P("rcv"),
    )
    return jax.shard_map(
        shards,
        mesh=mesh,
        in_specs=placed,
        out_specs=(P(None, None, ("src", "rcv")), P(None, None, ("src", "rcv"))),
        check_vma=False,
    )
```

```python
import jax
import jax.numpy as jnp
from jax import lax
from jax.experimental import pallas as pl
from jax.experimental.pallas import tpu as pltpu
from jax.sharding import PartitionSpec as P

MESH = pl.DeviceIdType.MESH
F32 = jnp.float32
BF16 = jnp.bfloat16
B = 48
L = 256
NY = 8
N_RCV = 16
N_SRC = 32
NX = 4
NZ = 8
TILES = 6
ORDER = (0, 1, -1, 2, -2, 3, -3, 4)


def far(i, n):
    return n // 2 + (i + 1) // 2 * (2 * ((i + 1) % 2) - 1)


def dot_nt(a, b):
    return lax.dot_general(a, b, (((1,), (1,)), ((), ())), preferred_element_type=F32)


def kernel(k_hbm, g_hbm, tr_hbm, op_hbm, st_hbm, el_hbm, x_ref, r_ref,
           g_ref, g_own, tr_ref, op_ref, st_ref, el_ref,
           kw, k_own, low, elb, co, co_send, sb, gat, acc, j0, ar_s, ar_in, ar_out, sc_s, sc_in, sc_out,
           rs_send, rs_in, rs_fin, own, pown, sib, tb0, tb1,
           k_sem, ka_sem, g_sem, in_sem, sib_send, sib_recv, kp_send, kp_recv, ag_send, ag_recv, rs_ssem, rs_recv, rf_recv,
           sp_send, sp_recv, a1_send, a1_recv, a2_send, a2_recv,
           s1_send, s1_recv, s2_send, s2_recv, t_send, t_recv):
    src = lax.axis_index("src")
    rcv = lax.axis_index("rcv")
    y = rcv // 2
    c = lax.rem(rcv, 2)
    other = 1 - c

    z = src // NX
    x = lax.rem(src, NX)
    tile = lax.rem(z + 4 * (x // 2), NZ)
    sums_tile = (lax.rem(x, 2) == c) & (tile < TILES)
    sums_scalars = (lax.rem(x, 2) == c) & (tile == TILES)
    sums = (lax.rem(x, 2) == c) & (tile <= TILES)

    def chip(d):
        return lax.rem(y + d + NY, NY)

    def at_chip(d, core):
        return (src, chip(d) * 2 + core)

    def remote(s, d, ss, rs, dev):
        return pltpu.make_async_remote_copy(
            src_ref=s, dst_ref=d, send_sem=ss, recv_sem=rs, device_id=dev, device_id_type=MESH)

    def start_rows(s, d, ss, rs, dev):
        for first in range(0, B, 16):
            remote(s.at[pl.ds(first, 16)], d.at[pl.ds(first, 16)], ss, rs, dev).start()

    here = (src, y * 2 + other)

    def wait_recv(ref, sem):
        remote(ref, ref, sem, sem, here).wait_recv()

    def wait_send(ref, sem):
        remote(ref, ref, sem, sem, here).wait_send()

    g_loads = [
        pltpu.make_async_copy(g_hbm.at[pl.ds(8 * i, 8)], g_ref.at[pl.ds(8 * i, 8)], g_sem.at[i]) for i in range(B // 8)]
    for load in g_loads:
        load.start()
    loads = [
        pltpu.make_async_copy(a, b, in_sem.at[i])
        for i, (a, b) in enumerate((
            (tr_hbm, tr_ref), (op_hbm, op_ref), (st_hbm, st_ref), (el_hbm, el_ref)))
    ]
    for load in loads:
        load.start()

    barrier = pltpu.get_barrier_semaphore()

    def greet(dev):
        pl.semaphore_signal(barrier, inc=1, device_id=dev, device_id_type=MESH)

    def greet_src(i):
        to = lax.rem(src + far(i, N_SRC), N_SRC)
        to_z, to_x = to // NX, lax.rem(to, NX)
        to_sums = (lax.rem(to_x, 2) == c) & (lax.rem(to_z + 4 * (to_x // 2), NZ) <= TILES)
        pl.when(sums | to_sums)(lambda: greet((to, rcv)))

    def greet_some(i, carry):
        greet((src, lax.rem(rcv + far(i, N_RCV), N_RCV)))
        greet_src(2 * i)
        greet_src(2 * i + 1)
        return carry

    lax.fori_loop(0, N_RCV - 1, greet_some, 0)
    greet_src(N_SRC - 2)

    def k_rows(d):
        return pl.ds(pl.multiple_of(chip(d) * (2 * L), 2 * L), 2 * L)

    def k_away(d):
        return pltpu.make_async_copy(k_hbm.at[other, k_rows(d)], k_own.at[k_rows(d)], ka_sem.at[chip(d)])

    def k_copy(d):
        return pltpu.make_async_copy(k_hbm.at[c, k_rows(d)], kw.at[c, k_rows(d)], k_sem.at[chip(d)])

    for d in ORDER:
        k_away(d).start()
        k_copy(d).start()

    lane = lax.broadcasted_iota(jnp.int32, (B, 128), 1)
    case = lax.broadcasted_iota(jnp.int32, (B, 128), 0)
    diag = lane == case

    def row_of(v):
        col = jnp.sum(v, axis=1, keepdims=True)
        return jnp.sum(jnp.where(diag, col, 0.0), axis=0, keepdims=True)

    def col_of(row):
        return jnp.sum(jnp.where(diag, row, 0.0), axis=1, keepdims=True)

    for load in g_loads:
        load.wait()
    g0, g1 = g_ref[:, 0, :], g_ref[:, 1, :]
    g_own[0] = g0
    g_own[1] = g1
    b0, b1 = g0.astype(BF16), g1.astype(BF16)
    sb[0] = b0
    sb[1] = b1
    gat[0, rcv] = jnp.where(c == 0, b0, b1)
    gg_row = row_of(g0 * g0 + g1 * g1)

    pl.when(sums)(lambda: pl.semaphore_wait(barrier, N_RCV + N_SRC - 2))
    pl.when(jnp.logical_not(sums))(lambda: pl.semaphore_wait(barrier, N_RCV - 1 + 2 * (TILES + 1)))

    def first_sends(comp):
        for d in (2, -2):
            start_rows(sb.at[comp], gat.at[0, rcv], ag_send.at[0], ag_recv.at[0, rcv], at_chip(d, comp))
        for d in (1, -1):
            remote(sb.at[comp], gat.at[0, rcv], ag_send.at[0], ag_recv.at[0, rcv], at_chip(d, comp)).start()

        @pl.when(c != comp)
        def _():
            remote(sb.at[comp], gat.at[0, rcv], ag_send.at[0], ag_recv.at[0, rcv], here).start()

    first_sends(0)

    def share_k(d):
        k_away(d).wait()
        remote(k_own.at[k_rows(d)], kw.at[c, k_rows(d)], kp_send, kp_recv.at[chip(d)], here).start()

    def arrived(it, d, h):
        slot = chip(d) * 2 + h
        wait_recv(gat.at[it, slot], ag_recv.at[it, slot])

    def relay(it):
        for h in range(2):
            for d in (1, -1):
                arrived(it, -2 * d, h)
                slot = chip(-2 * d) * 2 + h
                part = gat.at[it, slot]
                if (d == 1) == (h == 0):
                    start_rows(part, part, ag_send.at[it], ag_recv.at[it, slot], at_chip(2 * d, c))
                start_rows(part, part, ag_send.at[it], ag_recv.at[it, slot], at_chip(d, c))

    def block(q):
        rows = pl.ds(pl.multiple_of(q * (2 * L), 2 * L), 2 * L)
        return jnp.concatenate([kw[0, rows, :], kw[1, rows, :]], axis=1)

    def high_bits():
        return jnp.concatenate([elb[0, 8:9, :], elb[1, 8:9, :]], axis=1)

    def add_chips(it, ds):
        if it == 0:
            for d in ds:
                k_copy(d).wait()
                wait_recv(kw.at[other, k_rows(d)], kp_recv.at[chip(d)])
        slots = [chip(d) * 2 + h for d in ds for h in range(2)]
        parts = [gat[it, slot] for slot in slots]
        stiff = jnp.concatenate([block(chip(d)) for d in ds], axis=0)
        acc[0] += jnp.dot(jnp.concatenate(parts, axis=1), stiff, preferred_element_type=F32)
        ed = jnp.dot(jnp.concatenate(parts, axis=0), low[...], preferred_element_type=F32)
        high = high_bits()
        acc[1] += sum(jnp.where(high == slot, ed[B * k:B * k + B], 0.0) for k, slot in enumerate(slots))

    def coef(i):
        return jnp.concatenate([co[0, i], co[1, i]], axis=1)

    steps = [(dz, dx) for dz in range(NZ) for dx in range(NX)]
    reach = {(dz, dx): min(dz, NZ - dz) + min(dx, NX - dx) for dz, dx in steps}
    near = [s for s in steps if 0 < reach[s] < 3 or (reach[s] == 3 and 0 < s[0] < 4)]
    near = sorted(near, key=lambda s: -reach[s])

    def send_sum(part, send_sem, recv_sem):
        for dz, dx in near:
            dev = (lax.rem(z + dz, NZ) * NX + lax.rem(x + dx, NX), rcv)
            remote(part, part, send_sem, recv_sem, dev).start()

    def send_to_sums(t, part, landing, send_sem, recv_sem):
        for end in range(2):
            owner = lax.rem(t + 4 * end, NZ) * NX + c + 2 * end

            @pl.when(owner != src)
            def _():
                remote(part, landing.at[src], send_sem, recv_sem, (owner, rcv)).start()

    def reduce_src(it):
        part = (coef(0) * acc[1] + coef(1) * acc[0]).astype(BF16)
        for half in range(2):
            ar_s[it, 3 * half:3 * half + 3] = part[:, 128 * half:128 * half + 128].reshape(3, 16, 128)

        def send(t, carry):
            send_to_sums(t, ar_s.at[it, t], ar_in.at[it], a1_send.at[it], a1_recv.at[it])
            return carry

        lax.fori_loop(0, TILES, send, 0)
        if it == 1:
            sc_s[...] = sum_scalars(0)
            send_to_sums(TILES, sc_s, sc_in, s1_send, s1_recv)

            @pl.when(sums_scalars)
            def _():
                sc_in[src] = sc_s[...]
                wait_recv(sc_in.at[pl.ds(0, N_SRC - 1)], s1_recv)
                sc_out[...] = jnp.sum(sc_in[...], axis=0)
                send_sum(sc_out, s2_send, s2_recv)

        @pl.when(sums_tile)
        def _():
            ar_in[it, src] = ar_s[it, tile]
            wait_recv(ar_in.at[it, pl.ds(0, N_SRC - 1)], a1_recv.at[it])
            ar_out[it, tile] = jnp.sum(ar_in[it].astype(F32), axis=0).astype(BF16)
            send_sum(ar_out.at[it, tile], a2_send.at[it], a2_recv.at[it])
            wait_recv(ar_out.at[it, pl.ds(0, TILES - 1)], a2_recv.at[it])

        @pl.when(jnp.logical_not(sums_tile))
        def _():
            wait_recv(ar_out.at[it, pl.ds(0, TILES)], a2_recv.at[it])

        if it == 1:
            pl.when(jnp.logical_not(sums_scalars))(lambda: wait_recv(sc_out, s2_recv))
        return jnp.concatenate(
            [ar_out[it, 3 * half:3 * half + 3].reshape(B, 128) for half in range(2)], axis=1).astype(F32)

    def finish_src(it):
        @pl.when(sums_tile)
        def _():
            wait_send(ar_in.at[it, pl.ds(0, len(near))], a2_send.at[it])
            wait_send(ar_in.at[it, pl.ds(0, 2 * TILES - 1)], a1_send.at[it])

        @pl.when(jnp.logical_not(sums_tile))
        def _():
            wait_send(ar_in.at[it, pl.ds(0, 2 * TILES)], a1_send.at[it])

        if it == 1:
            @pl.when(sums_scalars)
            def _():
                wait_send(sc_in.at[pl.ds(0, len(near))], s2_send)
                wait_send(sc_in.at[pl.ds(0, 1)], s1_send)

            @pl.when(jnp.logical_not(sums_scalars))
            def _():
                wait_send(sc_in.at[pl.ds(0, 2)], s1_send)

    def share_scalars(it, row):
        tb = (tb0, tb1)[it]
        tb[rcv] = row

        def send(i, carry):
            remote(tb.at[rcv], tb.at[rcv], t_send.at[it], t_recv.at[it],
                   (src, lax.rem(rcv + far(i, N_RCV), N_RCV))).start()
            return carry

        lax.fori_loop(0, N_RCV - 1, send, 0)

    def sum_scalars(it):
        tb = (tb0, tb1)[it]
        wait_recv(tb.at[pl.ds(0, N_RCV - 1)], t_recv.at[it])
        return jnp.sum(tb[...], axis=0)

    def scatter_sources(it, jv, scalars=None):
        w = (coef(1) * jv).astype(BF16)
        lift = coef(0) * jv
        high = high_bits()

        def parts(ds):
            slots = [chip(d) * 2 + h for d in ds for h in range(2)]
            both = dot_nt(w, jnp.concatenate([block(chip(d)) for d in ds], axis=0))
            sparse = jnp.concatenate([jnp.where(high == slot, lift, 0.0) for slot in slots], axis=0)
            spread = dot_nt(sparse.astype(BF16), low[...])
            totals = [both[:, L * k:L * k + L] + spread[B * k:B * k + B] for k in range(len(slots))]
            return [totals[2 * k:2 * k + 2] for k in range(len(ds))]

        def send(slot, value, to, landing):
            rs_send[it, slot] = value.astype(BF16)
            start_rows(rs_send.at[it, slot], rs_in.at[it, landing], rs_ssem.at[it], rs_recv.at[it, landing],
                       at_chip(to, c))

        def home(slot, value, d, h):
            rs_send[it, slot] = value.astype(BF16)
            landing = {1: 0, -1: 2, 2: 4, -2: 6}[d] + (h if it == 0 else c)
            copy = (rs_send.at[it, slot], rs_fin.at[it, landing], rs_ssem.at[it], rf_recv.at[it, landing],
                    at_chip(d, c if it == 0 else h))
            if abs(d) == 2:
                start_rows(*copy)
            else:
                remote(*copy).start()

        def came(landing):
            wait_recv(rs_in.at[it, landing], rs_recv.at[it, landing])
            return rs_in[it, landing].astype(F32)

        four, three, minus_three = parts((4, 3, -3))
        send(0, four[0], 2, 0)
        send(1, four[1], -2, 1)
        for k, (d, value) in enumerate(((1, three), (-1, minus_three))):
            send(2 + 2 * k, value[0], d, 2 + 2 * k)
            send(3 + 2 * k, value[1], d, 3 + 2 * k)
        one, minus_one, up, down, mine = parts((1, -1, 2, -2, 0))
        for k, (d, value) in enumerate(((1, one), (-1, minus_one))):
            home(6 + 2 * k, value[0], d, 0)
            home(7 + 2 * k, value[1], d, 1)
        own[it, 0] = mine[0]
        own[it, 1] = mine[1]
        if it == 1:
            remote(own.at[it, other], sib.at[it], sp_send.at[it], sp_recv.at[it], here).start()
        if scalars is not None:
            share_scalars(it, scalars())
        home(10, up[1] + came(3), 2, 1)
        home(11, down[0] + came(4), -2, 0)
        home(12, up[0] + came(2) + came(0), 2, 0)
        home(13, down[1] + came(5) + came(1), -2, 1)

    def arrivals(it, i):
        total = 0.0
        for way in range(4):
            slot = way * 2 + i
            wait_recv(rs_fin.at[it, slot], rf_recv.at[it, slot])
            total += rs_fin[it, slot].astype(F32)
        return total

    for d in ORDER[:5]:
        share_k(d)

    for load in loads:
        load.wait()
    tau, press = tr_ref[:, 0, :], tr_ref[:, 1, :]
    opening, state = op_ref[...], st_ref[...]
    radius = jnp.sqrt(opening * opening + press * press + 0.5)
    a_n = 1.0 - opening / radius
    b_n = 1.0 - press / radius
    ratio = jnp.abs(tau) / (1.0 + 0.6 * jnp.abs(press))
    a_s = jnp.where(state == 0, 1.0, jnp.where(state == 1, ratio, 0.0))
    b_s = jnp.where(state == 0, ratio, 1.0)
    co[c, 0] = jnp.where(c == 0, a_s, a_n)
    co[c, 1] = jnp.where(c == 0, b_s, b_n)
    co_send[0] = jnp.where(c == 0, a_n, a_s)
    co_send[1] = jnp.where(c == 0, b_n, b_s)
    elb[c, :8, :] = jnp.broadcast_to(el_ref[...], (8, 128))
    co_share = remote(co_send, co.at[c], sib_send.at[0], sib_recv.at[0], here)
    co_share.start()
    el_share = remote(elb.at[c, pl.ds(0, 8)], elb.at[c, pl.ds(0, 8)], sib_send.at[1], sib_recv.at[1], here)
    el_share.start()
    first_sends(1)
    acc[...] = jnp.zeros((2, B, 256), F32)
    wait_recv(elb.at[other, pl.ds(0, 8)], sib_recv.at[1])
    for d in ORDER[5:]:
        share_k(d)
    place = jnp.concatenate([elb[0, 0:1, :], elb[1, 0:1, :]], axis=1) - src * (NY * 2 * L)
    low[...] = jnp.where(
        lax.broadcasted_iota(jnp.int32, (L, 256), 0) == (place & (L - 1)), 1.0, 0.0).astype(BF16)
    high = place >> 8
    elb[0, 8:, :] = jnp.broadcast_to(high[:, :128], (8, 128))
    elb[1, 8:, :] = jnp.broadcast_to(high[:, 128:], (8, 128))

    relay(0)

    def add_all(it):
        if it == 0:
            arrived(it, 0, other)
        for d in (1, -1):
            arrived(it, d, 0)
            arrived(it, d, 1)
        add_chips(it, ORDER[:5])
        for d in ORDER[5:]:
            arrived(it, d, 0)
            arrived(it, d, 1)
        add_chips(it, ORDER[5:])

    add_all(0)
    wait_recv(co.at[other], sib_recv.at[0])
    jv = reduce_src(0)
    j0[...] = jv
    scatter_sources(0, jv)
    gp_row = row_of(jv * jv)

    pp = 0.0
    for h in range(2):
        p = own[0, h] + arrivals(0, h)
        pown[h] = p
        pp += p * p
        part = gat.at[1, y * 2 + h]
        part[...] = p.astype(BF16)
        for d in (2, -2):
            start_rows(part, part, ag_send.at[1], ag_recv.at[1, y * 2 + h], at_chip(d, c))
    for h in range(2):
        part = gat.at[1, y * 2 + h]
        for d in (1, -1):
            remote(part, part, ag_send.at[1], ag_recv.at[1, y * 2 + h], at_chip(d, c)).start()
    remote(pown.at[other], sib.at[0], sp_send.at[0], sp_recv.at[0], here).start()
    pp_row = row_of(pp)
    share_scalars(0, jnp.concatenate([gg_row, pp_row, gp_row * (1.0 / N_SRC)], axis=1))
    acc[...] = jnp.zeros((2, B, 256), F32)
    relay(1)
    add_all(1)
    jp = reduce_src(1)
    sc = sc_out[...]
    gg, pp, gp = sc[:, :128], sc[:, 128:256], sc[:, 256:]
    alpha0 = gg / (0.5 * gg + gp)
    left = gp / (0.5 * gg + gp)
    rr = alpha0 * (alpha0 * pp - left * gp)
    beta = rr / gg
    scale = left + beta
    alpha0_c, left_c, scale_c = col_of(alpha0), col_of(left), col_of(scale)
    jv = scale_c * j0[...] - alpha0_c * jp
    scatter_sources(1, jv, lambda: row_of(jv * jv))
    jj = sum_scalars(1)
    alpha1 = rr / (0.5 * rr * (1.0 + beta) + jj)
    alpha1_c = col_of(alpha1)
    wait_recv(sib.at[0], sp_recv.at[0])
    base = []
    for comp in range(2):
        gv = g_own[comp]
        pv = jnp.where(c == comp, pown[c], sib[0])
        direction = scale_c * gv - alpha0_c * pv
        x_ref[:, comp, :] = alpha0_c * gv + alpha1_c * direction
        base.append(left_c * gv - alpha0_c * pv - alpha1_c * (0.5 * direction))
    wait_recv(sib.at[1], sp_recv.at[1])
    for comp in range(2):
        q = jnp.where(c == comp, own[1, c], sib[1]) + arrivals(1, comp)
        r_ref[:, comp, :] = base[comp] - alpha1_c * q

    co_share.wait_send()
    el_share.wait_send()
    wait_send(kw.at[c], kp_send)
    for it in range(2):
        wait_send(gat.at[it, pl.ds(0, 15 - it)], ag_send.at[it])
        wait_send(rs_send.at[it, pl.ds(0, 14)], rs_ssem.at[it])
        wait_send(own.at[it, 0], sp_send.at[it])
        wait_send((tb0, tb1)[it].at[pl.ds(0, N_RCV - 1)], t_send.at[it])
        finish_src(it)


def shards(stiffness, newton_rhs, traction, opening, state, elements):
    dma, vmem = pltpu.SemaphoreType.DMA, pltpu.VMEM
    out = jax.ShapeDtypeStruct((B, 2, L), F32)
    return pl.pallas_call(
        kernel,
        out_shape=(out, out),
        in_specs=[pl.BlockSpec(memory_space=pl.ANY)] * 6,
        out_specs=[pl.BlockSpec(memory_space=pltpu.VMEM)] * 2,
        scratch_shapes=[
            vmem((B, 2, L), F32),
            vmem((2, B, L), F32),
            vmem((B, 2, 128), F32),
            vmem((B, 128), F32),
            vmem((B, 128), jnp.int32),
            vmem((1, 128), jnp.int32),
            vmem((2, NY * 2 * L, 128), BF16),
            vmem((NY * 2 * L, 128), BF16),
            vmem((L, 256), BF16),
            vmem((2, 16, 128), jnp.int32),
            vmem((2, 2, B, 128), F32),
            vmem((2, B, 128), F32),
            vmem((2, B, L), BF16),
            vmem((2, 16, B, L), BF16),
            vmem((2, B, 256), F32),
            vmem((B, 256), F32),
            vmem((2, TILES, 16, 128), BF16),
            vmem((2, N_SRC, 16, 128), BF16),
            vmem((2, TILES, 16, 128), BF16),
            vmem((1, 384), F32),
            vmem((N_SRC, 1, 384), F32),
            vmem((1, 384), F32),
            vmem((2, 16, B, L), BF16),
            vmem((2, 6, B, L), BF16),
            vmem((2, 8, B, L), BF16),
            vmem((2, 2, B, L), F32),
            vmem((2, B, L), F32),
            vmem((2, B, L), F32),
            vmem((N_RCV, 1, 384), F32),
            vmem((N_RCV, 1, 128), F32),
            dma((NY,)), dma((NY,)), dma((B // 8,)), dma((4,)), dma((2,)), dma((2,)), dma, dma((NY,)),
            dma((2,)), dma((2, 16)), dma((2,)), dma((2, 6)), dma((2, 8)),
            dma((2,)), dma((2,)), dma((2,)), dma((2,)), dma((2,)), dma((2,)), dma, dma, dma, dma, dma((2,)), dma((2,)),
        ],
        compiler_params=pltpu.CompilerParams(
            collective_id=0, has_side_effects=True, vmem_limit_bytes=24 * 1024 * 1024),
        cost_estimate=pl.CostEstimate(flops=8 * B * 4096 * 512, bytes_accessed=4 << 20, transcendentals=0),
    )(*(pltpu.with_memory_space_constraint(a, pltpu.HBM) for a in (
        stiffness, newton_rhs, traction, opening, state, elements.reshape(1, 128))))


def solution(mesh):
    placed = (
        P(None, "src", "rcv"),
        P(None, None, ("src", "rcv")),
        P(None, None, "rcv"),
        P(None, "rcv"),
        P(None, "rcv"),
        P("rcv"),
    )
    return jax.shard_map(
        shards,
        mesh=mesh,
        in_specs=placed,
        out_specs=(P(None, None, ("src", "rcv")), P(None, None, ("src", "rcv"))),
        check_vma=False,
    )
```
